32 devices in a mesh: gx: 2 (over x), gy: 4 (over z), gz: 4 (over y, core).
Axes of the slice: x: 2, y: 2, z: 4, core: 2. Of those that a mesh axis runs over, the one named last changes fastest.
Arguments:
- pressure: float32 [2, 32, 32, 512], P(None, 'gx', 'gy', 'gz'), may hold values from -6 to 6
- saturation: float32 [3, 2, 32, 32, 512], P(None, None, 'gx', 'gy', 'gz'), may hold values from 0.15 to 0.45
- permeability: float32 [32, 32, 512], P('gx', 'gy', 'gz'), may hold values from 0.5 to 2
- porosity: float32 [32, 32, 512], P('gx', 'gy', 'gz'), may hold values from 0.1 to 0.35
- upwind_flags: int32 [32, 32, 512], P('gx', 'gy', 'gz'), may hold values from 0 to 63
- diag_inverse: float32 [2, 3, 3, 32, 32, 512], P(None, None, None, 'gx', 'gy', 'gz'), may hold values from -0.12 to 0.8, as said below
- seismic_obs: float32 [32, 32, 512], P('gx', 'gy', 'gz'), may hold values from -6 to 6
- well_x: int32 [2, 4, 64], P('gx', 'gy'), may hold values from 0 to 15
- well_y: int32 [2, 4, 64], P('gx', 'gy'), may hold values from 0 to 7
- well_top: int32 [2, 4, 64], P('gx', 'gy'), may hold values from 0 to 255
- well_len: int32 [2, 4, 64], P('gx', 'gy'), may hold values from 128 to 256
- well_bhp: float32 [2, 2, 4, 64], P(None, 'gx', 'gy'), may hold values from -3 to 3
- well_obs: float32 [2, 2, 4, 64], P(None, 'gx', 'gy'), may hold values from -48 to 48
- fault_cell: int32 [32, 16, 128], P(('gx', 'gy', 'gz')), may hold values from 0 to 16383
- fault_count: int32 [32, 16], P(('gx', 'gy', 'gz')), may hold values from 0 to 128, as said below
- fault_trans: float32 [32, 16, 128], P(('gx', 'gy', 'gz')), may hold values from 0.5 to 2, as said below
- fault_up: int32 [32, 16, 128], P(('gx', 'gy', 'gz')), may hold values from 0 to 3, as said below
- region_map: int32 [8, 8, 128], P('gx', 'gy', 'gz'), may hold values from 0 to 1023
Outputs:
- adjoint: float32 [2, 3, 32, 32, 512], P(None, None, 'gx', 'gy', 'gz')
- region_grad: float32 [2, 1024], P(None, ('gx', 'gy', 'gz'))
The draws below stay inside these ranges and needn't reach their ends.
Inputs may be any that keep to these rules, and one draw needn't show every extreme that they name: fault_count[dev][p] equals fault_count[i * 16 + p][a] of the connection's other end; a device has no connections with itself; in every draw one device of each group of 16 has exactly 128 connections with every other device of its group. `fault_cell`: slot s of dev toward peer p and slot s of that peer toward dev are the two ends of one connection. `fault_trans`: both ends of a connection hold the same transmissibility. `fault_up`: the two ends of a connection hold opposite bits. `diag_inverse`: entries [t][0][0] lie in 0.25 to 0.5, entries [t][u][u] for u = 1, 2 in 0.4 to 0.8, all others in -0.12 to 0.12.
All inputs are finite; a program needn't handle non-finite values.
Results may differ from the reference program's by a relative error of at most 0.0001.
Values sent between devices are 32-bit elements; how exact they have to be, the bound alone decides.
A program may use at most 128 MiB of HBM per device.

```python
import math
import jax
import jax.numpy as jnp
from jax import lax

CX = 16
CY = 8
CZ = 128
ITERS = 6
WELL_COL = 64
CAP = 128
BOX = 4
GROUPS = 2
PEERS = 16
NX = 32
NY = 32
NZ = 512
NREG = 1024
N_GX = 2
N_GY = 4
N_GZ = 4
DEVICES = 32


def symmetric_pick(base_draw):
    members = jnp.arange(PEERS)
    lower_index = jnp.minimum(members[:, None], members[None, :])
    upper_index = jnp.maximum(members[:, None], members[None, :])
    return base_draw[:, lower_index, upper_index]


def draw_fault_count(key, part):
    base_draw = jax.random.randint(jax.random.fold_in(key, 101), (GROUPS, PEERS, PEERS), 0, CAP // 2 + 1)
    paired = symmetric_pick(base_draw)
    busiest = jax.random.randint(jax.random.fold_in(key, 102), (GROUPS,), 0, PEERS)
    members = jnp.arange(PEERS)
    touches = (members[None, :, None] == busiest[:, None, None]) | (members[None, None, :] == busiest[:, None, None])
    paired = jnp.where(touches, CAP, paired)
    paired = jnp.where((members[:, None] == members[None, :])[None], 0, paired)
    return paired.reshape(GROUPS * PEERS, PEERS).astype(jnp.int32)


def draw_fault_trans(key, part):
    uniform_draw = jax.random.uniform(jax.random.fold_in(key, 103), (GROUPS, PEERS, PEERS, CAP), jnp.float32)
    values = 0.5 + 1.5 * uniform_draw
    return symmetric_pick(values).reshape(GROUPS * PEERS, PEERS, CAP).astype(jnp.float32)


def draw_fault_up(key, part):
    base_draw = jax.random.randint(jax.random.fold_in(key, 104), (GROUPS, PEERS, PEERS, CAP), 0, 4)
    paired = symmetric_pick(base_draw)
    members = jnp.arange(PEERS)
    flipped = (members[:, None] > members[None, :])[None, :, :, None]
    return jnp.where(flipped, 3 - paired, paired).reshape(GROUPS * PEERS, PEERS, CAP).astype(jnp.int32)


def draw_diag_inverse(key, part):
    uniform_draw = jax.random.uniform(jax.random.fold_in(key, 105), (2, 3, 3, NX, NY, NZ), jnp.float32)
    lower_table = jnp.array([[0.25, -0.12, -0.12], [-0.12, 0.4, -0.12], [-0.12, -0.12, 0.4]], jnp.float32)
    width_table = jnp.array([[0.25, 0.24, 0.24], [0.24, 0.4, 0.24], [0.24, 0.24, 0.4]], jnp.float32)
    result = lower_table[None, :, :, None, None, None] + width_table[None, :, :, None, None, None] * uniform_draw
    return result.astype(jnp.float32)


def place_ends(values, key, low, high):
    longest = values.shape.index(max(values.shape))
    spots = []
    for shift in (0, 1):
        where = [jax.random.randint(jax.random.fold_in(key, axis), (), 0, length) for axis, length in enumerate(values.shape)]
        where[longest] = (where[longest] + shift) % values.shape[longest]
        spots.append(tuple(where))
    return values.at[spots[0]].set(low).at[spots[1]].set(high)


def levels(key, dims, cuts, low, top_value):
    def one(position, parts):
        draws = jax.random.uniform(jax.random.fold_in(jax.random.fold_in(key, 6), position), (parts,), jnp.float32, low / len(cuts), top_value / len(cuts))
        return jnp.repeat(jnp.exp(draws), dims[position] // parts).reshape((-1,) + (1,) * (len(dims) - position - 1))

    factor_of = one(*cuts[0])
    for cut in cuts[1:]:
        factor_of = factor_of * one(*cut)
    return factor_of


def scatter_about(rng, dims, deviation, most, cuts=(), held_as=jnp.bfloat16):
    values = deviation * jax.random.normal(rng, dims, jnp.float32)
    if cuts:
        values = values * levels(rng, dims, cuts, -0.22, 0.18)
    return jnp.clip(values, -most, most).astype(held_as)


def setup_inputs(seed: int = 0) -> dict:
    splits = jax.random.split(jax.random.key(seed), 19)
    return {
        "pressure": scatter_about(splits[0], (2, NX, NY, NZ), 1.0, 6.0, ((1, 2), (2, 4), (3, 4)), jnp.float32),
        "saturation": jnp.clip(0.15 + 0.29999998 * jax.random.uniform(splits[1], (3, 2, NX, NY, NZ), jnp.float32) ** levels(splits[1], (3, 2, NX, NY, NZ), ((2, 2), (3, 4), (4, 4)), -0.2, 0.2), 0.15, 0.45),
        "permeability": jnp.clip(jnp.exp(math.log(2.0) - 1.3862944 * jax.random.uniform(splits[2], (NX, NY, NZ), jnp.float32) ** levels(splits[2], (NX, NY, NZ), ((0, 2), (1, 4), (2, 4)), -0.2, 0.2)), 0.5, 2.0),
        "porosity": jnp.clip(0.1 + 0.25 * jax.random.uniform(splits[3], (NX, NY, NZ), jnp.float32) ** levels(splits[3], (NX, NY, NZ), ((0, 2), (1, 4), (2, 4)), -0.2, 0.2), 0.1, 0.35),
        "upwind_flags": place_ends(jax.random.randint(splits[4], (NX, NY, NZ), 0, 64), jax.random.fold_in(splits[4], 1), 0, 63).astype(jnp.int32),
        "diag_inverse": draw_diag_inverse(jax.random.fold_in(splits[18], 71), 0),
        "seismic_obs": scatter_about(splits[6], (NX, NY, NZ), 1.0, 6.0, ((0, 2), (1, 4), (2, 4)), jnp.float32),
        "well_x": place_ends(jax.random.randint(splits[7], (N_GX, N_GY, WELL_COL), 0, CX), jax.random.fold_in(splits[7], 1), 0, CX - 1).astype(jnp.int32),
        "well_y": place_ends(jax.random.randint(splits[8], (N_GX, N_GY, WELL_COL), 0, CY), jax.random.fold_in(splits[8], 1), 0, CY - 1).astype(jnp.int32),
        "well_top": place_ends(jax.random.randint(splits[9], (N_GX, N_GY, WELL_COL), 0, NZ // 2), jax.random.fold_in(splits[9], 1), 0, (NZ // 2) - 1).astype(jnp.int32),
        "well_len": place_ends(jax.random.randint(splits[10], (N_GX, N_GY, WELL_COL), NZ // 4, NZ // 2 + 1), jax.random.fold_in(splits[10], 1), NZ // 4, (NZ // 2 + 1) - 1).astype(jnp.int32),
        "well_bhp": scatter_about(splits[11], (2, N_GX, N_GY, WELL_COL), 0.5, 3.0, ((1, 2), (2, 4)), jnp.float32),
        "well_obs": scatter_about(splits[12], (2, N_GX, N_GY, WELL_COL), 8.0, 48.0, ((1, 2), (2, 4)), jnp.float32),
        "fault_cell": place_ends(jax.random.randint(splits[13], (DEVICES, PEERS, CAP), 0, CX * CY * CZ), jax.random.fold_in(splits[13], 1), 0, (CX * CY * CZ) - 1).astype(jnp.int32),
        "fault_count": draw_fault_count(jax.random.fold_in(splits[18], 71), 0),
        "fault_trans": draw_fault_trans(jax.random.fold_in(splits[18], 71), 0),
        "fault_up": draw_fault_up(jax.random.fold_in(splits[18], 71), 0),
        "region_map": place_ends(jax.random.randint(splits[17], (NX // BOX, NY // BOX, NZ // BOX), 0, NREG), jax.random.fold_in(splits[17], 1), 0, NREG - 1).astype(jnp.int32),
    }


fluid_viscosity = (0.4, 0.5, 1.0)
sigma_sq = 64.0

def phase_mobility(water_sat, oil_sat):
    gas_sat = 1.0 - water_sat - oil_sat
    return jnp.stack([water_sat * water_sat / fluid_viscosity[0], oil_sat * oil_sat / fluid_viscosity[1], gas_sat * gas_sat / fluid_viscosity[2]])

def mobility_slopes(water_sat, oil_sat):
    gas_sat = 1.0 - water_sat - oil_sat
    return (2.0 * water_sat / fluid_viscosity[0] - 2.0 * gas_sat / fluid_viscosity[2], 2.0 * oil_sat / fluid_viscosity[1] - 2.0 * gas_sat / fluid_viscosity[2])

def shift_ahead(quantity, along_axis):
    extent = quantity.shape[along_axis]
    border = jnp.zeros_like(lax.slice_in_dim(quantity, 0, 1, axis=along_axis))
    return lax.slice_in_dim(jnp.concatenate([quantity, border], axis=along_axis), 1, extent + 1, axis=along_axis)

def shift_behind(quantity, along_axis):
    extent = quantity.shape[along_axis]
    border = jnp.zeros_like(lax.slice_in_dim(quantity, 0, 1, axis=along_axis))
    return lax.slice_in_dim(jnp.concatenate([border, quantity], axis=along_axis), 0, extent, axis=along_axis)

def face_coefficients(permeability, mobility, upwind_flags, step_index):
    ahead_list = []
    behind_list = []
    for direction in range(3):
        face_trans = jnp.sqrt(permeability * shift_ahead(permeability, direction))
        upwind_bit = jnp.bitwise_and(jnp.right_shift(upwind_flags, 3 * step_index + direction), 1)
        chosen = jnp.where(upwind_bit[None] == 1, mobility, shift_ahead(mobility, direction + 1))
        coefficient = face_trans[None] * chosen
        ahead_list.append(coefficient)
        behind_list.append(shift_behind(coefficient, direction + 1))
    return (ahead_list, behind_list)

def global_cells(device_ids, cell_index):
    block_x = device_ids // PEERS
    block_y = device_ids // N_GZ % N_GY
    block_z = device_ids % N_GZ
    local_x = cell_index // (CY * CZ)
    local_y = cell_index // CZ % CY
    local_z = cell_index % CZ
    return ((block_x * CX + local_x) * NY + block_y * CY + local_y) * NZ + block_z * CZ + local_z

def apply_inverse(inverse, residual):
    return lax.optimization_barrier(jnp.sum(inverse * residual[:, None], axis=0))

def neighbour_sum(lagrange, ahead_list, behind_list, fault_coef, own_cells, other_cells):
    upper_terms = [lax.optimization_barrier(jnp.sum(ahead_list[direction] * shift_ahead(lagrange, direction + 1), axis=0)) for direction in range(3)]
    lower_terms = [lax.optimization_barrier(jnp.sum(behind_list[direction] * shift_behind(lagrange, direction + 1), axis=0)) for direction in range(3)]
    face_total = upper_terms[0] + lower_terms[0] + upper_terms[1] + lower_terms[1] + upper_terms[2] + lower_terms[2]
    flattened = lagrange.reshape(3, -1)
    contribution = lax.optimization_barrier(jnp.sum(fault_coef * flattened[:, other_cells], axis=0))
    faults = jnp.zeros((flattened.shape[1],), jnp.float32).at[own_cells.reshape(-1)].add(contribution.reshape(-1))
    return face_total + faults.reshape(lagrange.shape[1:])

def box_sums(quantity):
    shaped = quantity.reshape(quantity.shape[0] // BOX, BOX, quantity.shape[1] // BOX, BOX, quantity.shape[2] // BOX, BOX)
    return lax.optimization_barrier(jnp.sum(shaped, axis=(1, 3, 5))).reshape(-1)

def reference(pressure, saturation, permeability, porosity, upwind_flags, diag_inverse, seismic_obs, well_x, well_y, well_top, well_len, well_bhp, well_obs, fault_cell, fault_count, fault_trans, fault_up, region_map):
    mobility = [phase_mobility(saturation[step_index + 1, 0], saturation[step_index + 1, 1]) for step_index in range(2)]
    coefficients = [face_coefficients(permeability, mobility[step_index], upwind_flags, step_index) for step_index in range(2)]
    devices = GROUPS * PEERS
    device_ids = jnp.arange(devices, dtype=jnp.int32)[:, None, None]
    peer_index = jnp.arange(PEERS, dtype=jnp.int32)[None, :, None]
    peer_devices = device_ids // PEERS * PEERS + peer_index
    peer_cells = jnp.transpose(fault_cell.reshape(GROUPS, PEERS, PEERS, CAP), (0, 2, 1, 3)).reshape(devices, PEERS, CAP)
    own_cells = global_cells(device_ids, fault_cell)
    other_cells = global_cells(peer_devices, peer_cells)
    live_slots = (jnp.arange(CAP, dtype=jnp.int32)[None, None, :] < fault_count[:, :, None]).astype(jnp.float32)
    fault_coef = []
    for step_index in range(2):
        flattened = mobility[step_index].reshape(3, -1)
        upwind_bit = jnp.bitwise_and(jnp.right_shift(fault_up, step_index), 1)
        chosen = jnp.where(upwind_bit[None] == 1, flattened[:, own_cells], flattened[:, other_cells])
        fault_coef.append(fault_trans[None] * chosen * live_slots[None])
    column_x = (jnp.arange(N_GX, dtype=jnp.int32)[:, None, None] * CX + well_x).reshape(-1)
    column_y = (jnp.arange(N_GY, dtype=jnp.int32)[None, :, None] * CY + well_y).reshape(-1)
    top_cells = well_top.reshape(-1)[:, None]
    depth_index = jnp.arange(NZ, dtype=jnp.int32)[None, :]
    perforated = ((depth_index >= top_cells) & (depth_index < top_cells + well_len.reshape(-1)[:, None])).astype(jnp.float32)
    column_perm = permeability[column_x, column_y]
    sources = []
    explicit = jnp.zeros(permeability.shape, jnp.float32)
    for step_index in range(2):
        column_pressure = pressure[step_index][column_x, column_y]
        column_total = lax.optimization_barrier(jnp.sum(mobility[step_index][:, column_x, column_y], axis=0))
        drawdown = column_pressure - well_bhp[step_index].reshape(-1)[:, None]
        well_rate = lax.optimization_barrier(jnp.sum(perforated * column_perm * column_total * drawdown, axis=1))
        misfit = (well_rate - well_obs[step_index].reshape(-1)) / sigma_sq
        water_slope, oil_slope = mobility_slopes(saturation[step_index + 1, 0][column_x, column_y], saturation[step_index + 1, 1][column_x, column_y])
        weight = misfit[:, None] * column_perm * perforated
        added = jnp.stack([weight * column_total, weight * drawdown * water_slope, weight * drawdown * oil_slope])
        sources.append(jnp.zeros((3,) + permeability.shape, jnp.float32).at[:, column_x, column_y].add(added))
        explicit = explicit.at[column_x, column_y].add(weight * column_total * drawdown)
    sources[1] = sources[1].at[1].add(saturation[2, 0] - seismic_obs)

    def solve(step_index, source):
        ahead_list, behind_list = coefficients[step_index]
        lagrange = jnp.zeros_like(source)
        for sweep_index in range(ITERS):
            coupling = neighbour_sum(lagrange, ahead_list, behind_list, fault_coef[step_index], own_cells, other_cells)
            residual = jnp.concatenate([(source[0] + coupling)[None], source[1:]], axis=0)
            lagrange = apply_inverse(diag_inverse[step_index], residual)
        return lagrange
    late = solve(1, sources[1])
    early_source = sources[0] + jnp.stack([jnp.zeros_like(porosity), porosity * (late[0] - late[2]), porosity * (late[1] - late[2])])
    early = solve(0, early_source)
    solved = [early, late]
    flux_list = []
    porosity_terms = []
    for step_index in (1, 0):
        lagrange = solved[step_index]
        ahead_list, behind_list = coefficients[step_index]
        pressure_here = pressure[step_index]
        flux_grad = jnp.zeros_like(pressure_here)
        for direction in range(3):
            local_ahead = lax.optimization_barrier(jnp.sum(ahead_list[direction] * lagrange, axis=0))
            local_behind = lax.optimization_barrier(jnp.sum(behind_list[direction] * lagrange, axis=0))
            upper_term = lax.optimization_barrier(jnp.sum(ahead_list[direction] * shift_ahead(lagrange, direction + 1), axis=0))
            lower_term = lax.optimization_barrier(jnp.sum(behind_list[direction] * shift_behind(lagrange, direction + 1), axis=0))
            flux_grad = flux_grad + 0.5 * (pressure_here - shift_ahead(pressure_here, direction)) * (local_ahead - upper_term) + 0.5 * (shift_behind(pressure_here, direction) - pressure_here) * (lower_term - local_behind)
        flux_list.append(flux_grad)
        water_change = saturation[step_index + 1, 0] - saturation[step_index, 0]
        oil_change = saturation[step_index + 1, 1] - saturation[step_index, 1]
        porosity_terms.append(lagrange[0] * water_change + lagrange[1] * oil_change - lagrange[2] * (water_change + oil_change))
    log_perm_grad = explicit - (flux_list[0] + flux_list[1])
    porosity_gradient = -(porosity_terms[0] + porosity_terms[1])
    box_totals = jnp.stack([box_sums(log_perm_grad), box_sums(porosity_gradient)], axis=1)
    region_grad = jax.ops.segment_sum(box_totals, region_map.reshape(-1), num_segments=NREG).T
    return (jnp.stack([early, late]), region_grad)
```

```python
import functools

import jax
import jax.numpy as jnp
from jax import lax
from jax.experimental import pallas as pl
from jax.experimental.pallas import tpu as pltpu
from jax.sharding import PartitionSpec as P

ITERS = 6
BOX = 4
PARAM_REGIONS = 32
LANES = 128
NEAR = 8
MESH = pl.DeviceIdType.MESH

fluid_viscosity = (0.4, 0.5, 1.0)
sigma_sq = 64.0
SIDES = tuple((dim, side) for dim in range(3) for side in range(2))


def phase_mobility(water_sat, oil_sat):
    gas_sat = 1.0 - water_sat - oil_sat
    return [
        water_sat * water_sat / fluid_viscosity[0],
        oil_sat * oil_sat / fluid_viscosity[1],
        gas_sat * gas_sat / fluid_viscosity[2],
    ]


def mobility_slopes(water_sat, oil_sat):
    gas_sat = 1.0 - water_sat - oil_sat
    return (
        2.0 * water_sat / fluid_viscosity[0] - 2.0 * gas_sat / fluid_viscosity[2],
        2.0 * oil_sat / fluid_viscosity[1] - 2.0 * gas_sat / fluid_viscosity[2],
    )


def split(value, parts):
    pieces = []
    for _ in range(parts):
        piece = value.astype(jnp.bfloat16)
        pieces.append(piece)
        value = value - piece.astype(jnp.float32)
    return pieces


def kernel(
    counts,
    pressure_hbm,
    saturation_hbm,
    perm_hbm,
    porosity_hbm,
    flags_hbm,
    inverse_hbm,
    seismic_hbm,
    well_x_ref,
    well_y_ref,
    well_top_ref,
    well_len_ref,
    bhp_ref,
    obs_ref,
    fault_cell_ref,
    fault_count_ref,
    fault_trans_ref,
    fault_up_ref,
    map_ref,
    lam_hbm,
    region_ref,
    pressure_ref,
    sat_ref,
    perm_ref,
    porosity_ref,
    flags_ref,
    inverse_ref,
    seismic_ref,
    in_sem,
    out_sem,
    mob,
    wp,
    wm,
    src,
    explicit,
    lam,
    const,
    lead,
    turn_c,
    turn_d,
    push,
    push_turn_c,
    push_turn_d,
    flux_base,
    flux_lead,
    por,
    total_r,
    delta,
    row_hot,
    z_hot,
    found_hot,
    f_cell,
    f_scale,
    f_up,
    f_tmp,
    f_own,
    f_coef,
    f_send,
    bx_s,
    by_s,
    bz_s,
    bx_r,
    by_r,
    bz_r,
    b_ss,
    b_rs,
    map_r,
    map_ss,
    map_rs,
    m_s,
    m_r,
    m_ss,
    m_rs,
    w_s,
    w_r,
    w_ss,
    w_rs,
    x_s,
    y_s,
    z_s,
    x_r,
    y_r,
    z_r,
    h_ss,
    h_rs,
    v_s,
    v_r,
    v_ss,
    v_rs,
    c_s,
    c_r,
    c_ss,
    c_rs,
    r_s,
    r_r,
    r_ss,
    r_rs,
):
    n_gx, n_gy, n_gz = counts
    here = (lax.axis_index("gx"), lax.axis_index("gy"), lax.axis_index("gz"))
    peers = n_gy * n_gz
    devices = n_gx * peers
    me = here[1] * n_gz + here[2]
    index = here[0] * peers + me
    shape = perm_ref.shape
    nx, ny, nz = shape
    rows = nx * ny
    slots = c_r.shape[2]
    f32 = jnp.float32

    def flip(number, bits):
        bit = 1
        while bit <= bits:
            if bits & bit:
                number = number + bit - 2 * bit * lax.rem(number // bit, 2)
            bit *= 2
        return number

    def peer(order):
        return (here[0], flip(here[1], order // n_gz), flip(here[2], order % n_gz))

    def peer_place(order):
        other = peer(order)
        return other[1] * n_gz + other[2]

    def toward(dim, step):
        moved = list(here)
        moved[dim] = lax.rem(here[dim] + step + counts[dim], counts[dim])
        return tuple(moved)

    def device(number):
        return (number // peers, lax.rem(number, peers) // n_gz, lax.rem(number, n_gz))

    def remote(source, target, send, recv, to):
        return pltpu.make_async_remote_copy(
            src_ref=source,
            dst_ref=target,
            send_sem=send,
            recv_sem=recv,
            device_id=to,
            device_id_type=MESH,
        )

    has_next = [here[dim] < counts[dim] - 1 for dim in range(3)]
    has_last = [here[dim] > 0 for dim in range(3)]

    def sends(dim, side):
        return has_next[dim] if side == 0 else has_last[dim]

    def receives(dim, side):
        return has_last[dim] if side == 0 else has_next[dim]

    loads = [
        pltpu.make_async_copy(source, target, in_sem.at[n])
        for n, (source, target) in enumerate(
            (
                (saturation_hbm, sat_ref),
                (perm_hbm, perm_ref),
                (pressure_hbm, pressure_ref),
                (flags_hbm, flags_ref),
                (seismic_hbm, seismic_ref),
                (inverse_hbm, inverse_ref),
                (porosity_hbm, porosity_ref),
            )
        )
    ]
    for load in loads:
        load.start()
    for ref in (bx_r, by_r, bz_r, x_r, y_r, z_r, m_r, v_r, c_r, map_r):
        ref[...] = jnp.zeros_like(ref)

    barrier = pltpu.get_barrier_semaphore()
    for offset in range(1, devices):
        pl.semaphore_signal(
            barrier,
            inc=1,
            device_id=device(lax.rem(index + offset, devices)),
            device_id_type=MESH,
        )

    yi = lax.broadcasted_iota(jnp.int32, shape, 1)
    zi = lax.broadcasted_iota(jnp.int32, shape, 2)
    iotas = (None, yi, zi)
    diagonal = lax.broadcasted_iota(jnp.int32, shape, 0) == zi

    def pack(field, lane):
        return jnp.sum(jnp.where(diagonal, field[:, :, lane : lane + 1], 0.0), axis=0)

    def unpack(tile):
        return jnp.concatenate(
            [jnp.broadcast_to(tile[:, x : x + 1], (ny, nz))[None] for x in range(nx)], axis=0
        )

    def at_next(field, dim, edge):
        if dim == 0:
            return jnp.concatenate([field[1:], edge], axis=0)
        last = shape[dim] - 1
        return jnp.where(iotas[dim] == last, edge, pltpu.roll(field, last, dim))

    def at_last(field, dim, edge):
        if dim == 0:
            return jnp.concatenate([edge, field[:-1]], axis=0)
        return jnp.where(iotas[dim] == 0, edge, pltpu.roll(field, 1, dim))

    def edge_of(dim, halo):
        if dim == 0:
            return halo[None]
        return halo if dim == 1 else unpack(halo)

    def no_edge(dim):
        return jnp.zeros((1, ny, nz), f32) if dim == 0 else 0.0

    def faults_in_order(array, target):
        for order in range(peers):
            target[order : order + 1, :] = array[pl.ds(peer_place(order), 1), :]

    faults_in_order(fault_cell_ref.at[0], f_cell)
    faults_in_order(fault_up_ref.at[0], f_up)
    slot_index = lax.broadcasted_iota(jnp.int32, (1, slots), 1)
    for p in range(peers):
        f_tmp[p : p + 1, :] = jnp.where(
            slot_index < fault_count_ref[:, p : p + 1], fault_trans_ref[0, p : p + 1, :], 0.0
        )
    faults_in_order(f_tmp, f_scale)
    f_row = f_cell[...] // nz
    f_z = f_cell[...] - f_row * nz

    def gather(refs, unroll):
        def body(x, chosen):
            for y in range(ny):
                here_row = f_row == x * ny + y
                chosen = [
                    jnp.where(
                        here_row,
                        jnp.take_along_axis(
                            jnp.broadcast_to(ref[x, y : y + 1, :], (peers, nz)),
                            f_z,
                            axis=1,
                            mode="promise_in_bounds",
                        ),
                        value,
                    )
                    for ref, value in zip(refs, chosen)
                ]
            return chosen

        start = [jnp.zeros((peers, slots), f32) for _ in refs]
        return lax.fori_loop(0, nx, body, start, unroll=unroll)

    loads[0].wait()
    mobility = [phase_mobility(sat_ref[t + 1, 0], sat_ref[t + 1, 1]) for t in range(2)]
    for t in range(2):
        for k in range(3):
            mob[t, k] = mobility[t][k]
    for load in loads[1:4]:
        load.wait()
    perm = perm_ref[...]

    def bundle(part, fields):
        for q, field in enumerate(fields):
            bx_s[part, 0, q] = field[nx - 1]
            bx_s[part, 1, q] = field[0]
            by_s[part, 0, q] = field[:, ny - 1 :, :]
            by_s[part, 1, q] = field[:, :1, :]
            bz_s[part, 0, q] = pack(field, nz - 1)
            bz_s[part, 1, q] = pack(field, 0)

    def bundle_copy(part, dim, side):
        sent, got = ((bx_s, bx_r), (by_s, by_r), (bz_s, bz_r))[dim]
        return remote(
            sent.at[part, side],
            got.at[part, side],
            b_ss.at[part, dim, side],
            b_rs.at[part, dim, side],
            toward(dim, 1 - 2 * side),
        )

    def map_copy(dim, side):
        return remote(
            map_ref,
            map_r.at[2 * dim + side],
            map_ss.at[dim, side],
            map_rs.at[dim, side],
            toward(dim, 1 - 2 * side),
        )

    def start_faces(copies):
        for dim, side in SIDES:

            @pl.when(sends(dim, side))
            def _():
                for copy in copies:
                    copy(dim, side).start()

    def wait_faces(copies):
        for dim, side in SIDES:

            @pl.when(sends(dim, side))
            def _():
                for copy in copies:
                    copy(dim, side).wait_send()

            @pl.when(receives(dim, side))
            def _():
                for copy in copies:
                    copy(dim, side).wait_recv()

    bundle(0, [perm] + mobility[1] + [flags_ref[...].astype(f32)])

    n_wells = well_top_ref.shape[2]
    eye = lax.broadcasted_iota(jnp.int32, (n_wells, n_wells), 0) == lax.broadcasted_iota(
        jnp.int32, (n_wells, n_wells), 1
    )

    def as_column(row):
        return jnp.sum(jnp.where(eye, row.astype(f32), 0.0), axis=1, keepdims=True)

    def as_row(column):
        return jnp.sum(jnp.where(eye, column, 0.0), axis=0, keepdims=True)

    well_row = well_x_ref[0] * ny + well_y_ref[0]
    well_hot = (
        (
            lax.broadcasted_iota(jnp.int32, (n_wells, rows), 1).astype(f32) == as_column(well_row)
        )
        .astype(f32)
        .astype(jnp.bfloat16)
    )
    well_hot_t = (lax.broadcasted_iota(jnp.int32, (rows, n_wells), 0) == well_row).astype(f32)
    depth = (here[2] * nz + lax.broadcasted_iota(jnp.int32, (n_wells, nz), 1)).astype(f32)
    top = as_column(well_top_ref[0])
    bottom = as_column(well_top_ref[0] + well_len_ref[0])
    perforated = jnp.where((depth >= top) & (depth < bottom), 1.0, 0.0)

    def total(t):
        return perm_ref[...] * (mob[t, 0] + mob[t, 1] + mob[t, 2])

    fields = []
    for t in range(2):
        whole = total(t)
        fields += [
            (whole * pressure_ref[t]).reshape(rows, nz),
            whole.reshape(rows, nz),
        ]
    pieces = jnp.concatenate(split(jnp.concatenate(fields, axis=1), 3), axis=0)
    of_wells = jnp.dot(
        jnp.concatenate([well_hot] * 3, axis=1), pieces, preferred_element_type=f32
    )
    w_s[...] = jnp.zeros_like(w_s)
    for t in range(2):
        bhp = as_column(bhp_ref[t, 0])
        rate = jnp.sum(
            perforated
            * (
                of_wells[:, 2 * t * nz : (2 * t + 1) * nz]
                - bhp * of_wells[:, (2 * t + 1) * nz : (2 * t + 2) * nz]
            ),
            axis=1,
            keepdims=True,
        )
        w_s[t : t + 1, :n_wells] = as_row(rate)

    pl.semaphore_wait(barrier, devices - 1)
    w_copies = []
    for offset in range(1, n_gz):
        copy = remote(
            w_s,
            w_r.at[offset],
            w_ss.at[offset],
            w_rs.at[offset],
            (here[0], here[1], lax.rem(here[2] + offset, n_gz)),
        )
        copy.start()
        w_copies.append(copy)
    start_faces([functools.partial(bundle_copy, 0)])

    def order_far_first():
        return range(peers - 1, 0, -1)

    def group(order):
        return 0 if order < NEAR else 1

    own = gather([mob.at[t, k] for t in (1, 0) for k in range(3)], False)
    for q in range(6):
        f_own[q] = own[q]
        m_s[q] = own[q]
    for order in order_far_first():
        remote(
            m_s.at[:, pl.ds(order, 1)],
            m_r.at[:, pl.ds(order, 1)],
            m_ss,
            m_rs,
            peer(order),
        ).start()

    for order in range(peers):
        lanes = slice(order * slots, (order + 1) * slots)
        row_hot[:, lanes] = (
            (lax.broadcasted_iota(jnp.int32, (rows, slots), 0) == f_row[order : order + 1])
            .astype(f32)
            .astype(jnp.bfloat16)
        )
        z_hot[:, lanes] = (
            (lax.broadcasted_iota(jnp.int32, (nz, slots), 0) == f_z[order : order + 1])
            .astype(f32)
            .astype(jnp.bfloat16)
        )

    def scatter(values, first):
        high, low = split(values, 2)
        marked = []
        for n in range(values.shape[0]):
            order = first + n
            if order == 0:
                continue
            hot = z_hot[:, order * slots : (order + 1) * slots]
            marked.append(
                jnp.concatenate(
                    [hot * jnp.broadcast_to(part[n : n + 1], hot.shape) for part in (high, low)],
                    axis=0,
                )
            )
        start = max(first, 1)
        added = lax.dot_general(
            row_hot[:, start * slots : (first + values.shape[0]) * slots],
            jnp.concatenate(marked, axis=1),
            (((1,), (1,)), ((), ())),
            preferred_element_type=f32,
        )
        return (added[:, :nz] + added[:, nz:]).reshape(shape)

    for load in loads[4:]:
        load.wait()
    for copy in w_copies:
        copy.wait()
    rates = w_s[...]
    for offset in range(1, n_gz):
        rates = rates + w_r[offset]

    def sources(t):
        misfit = (rates[t : t + 1, :n_wells] - obs_ref[t, 0]) / sigma_sq
        weighted = well_hot_t * misfit
        both = jnp.concatenate([weighted, weighted * bhp_ref[t, 0]], axis=0)
        spread = jnp.dot(
            jnp.concatenate(split(both, 3), axis=0),
            perforated.astype(jnp.bfloat16),
            preferred_element_type=f32,
        )
        spread = spread[: 2 * rows] + spread[2 * rows : 4 * rows] + spread[4 * rows :]
        drawn = pressure_ref[t] * spread[:rows].reshape(shape) - spread[rows:].reshape(shape)
        water_slope, oil_slope = mobility_slopes(sat_ref[t + 1, 0], sat_ref[t + 1, 1])
        whole = total(t)
        src[t, 0] = whole * spread[:rows].reshape(shape)
        water_source = perm_ref[...] * drawn * water_slope
        if t == 1:
            water_source = water_source + (sat_ref[2, 0] - seismic_ref[...])
        src[t, 1] = water_source
        src[t, 2] = perm_ref[...] * drawn * oil_slope
        return whole * drawn

    def face_coefficients(t, flags, bits_at, perm_from, mob_from):
        own_flags = flags.astype(jnp.int32)
        for dim in range(3):
            got = (bx_r, by_r, bz_r)[dim]

            def halo(part, side, q):
                return edge_of(dim, got[part, side, q])

            up_face = jnp.sqrt(
                perm_ref[...] * at_next(perm_ref[...], dim, halo(0, 1, 0))
            )
            low_face = jnp.sqrt(
                perm_ref[...] * at_last(perm_ref[...], dim, halo(0, 0, 0))
            )
            up_ok = has_next[dim].astype(f32)
            low_ok = has_last[dim].astype(f32)
            if dim == 0:
                up_face = jnp.concatenate([up_face[:-1], up_face[-1:] * up_ok], axis=0)
                low_face = jnp.concatenate([low_face[:1] * low_ok, low_face[1:]], axis=0)
            else:
                up_face = up_face * jnp.where(iotas[dim] == shape[dim] - 1, up_ok, 1.0)
                low_face = low_face * jnp.where(iotas[dim] == 0, low_ok, 1.0)
            bit = 3 * t + dim
            low_flags = at_last(flags, dim, halo(0, 0, 4)).astype(jnp.int32)
            own_up = jnp.bitwise_and(jnp.right_shift(own_flags, bit), 1) == 1
            low_up = jnp.bitwise_and(jnp.right_shift(low_flags, bit), 1) == 1
            for k in range(3):
                part, q = mob_from(k)
                m = mob[t, k]
                wp[t, dim, k] = up_face * jnp.where(
                    own_up, m, at_next(m, dim, halo(part, 1, q))
                )
                wm[t, dim, k] = low_face * jnp.where(
                    low_up, at_last(m, dim, halo(part, 0, q)), m
                )

    def face_copy(parity, dim, side):
        sent, got = ((x_s, x_r), (y_s, y_r), (z_s, z_r))[dim]
        return remote(
            sent.at[side],
            got.at[parity, side],
            h_ss.at[dim, side],
            h_rs.at[parity, dim, side],
            toward(dim, 1 - 2 * side),
        )

    def send_faces(parity, up, down):
        x_s[0] = up[0][nx - 1]
        x_s[1] = down[0][0]
        y_s[0] = up[1][:, ny - 1 :, :]
        y_s[1] = down[1][:, :1, :]
        z_s[0] = pack(up[2], nz - 1)
        z_s[1] = pack(down[2], 0)
        start_faces([functools.partial(face_copy, parity)])
        inner = at_last(up[0], 0, no_edge(0)) + at_next(down[0], 0, no_edge(0))
        for dim in (1, 2):
            inner = inner + at_last(up[dim], dim, 0.0) + at_next(down[dim], dim, 0.0)
        return inner

    def add_faces(parity, inner):
        wait_faces([functools.partial(face_copy, parity)])
        inner = jnp.concatenate(
            [
                inner[:1] + x_r[parity, 0][None],
                inner[1 : nx - 1],
                inner[nx - 1 :] + x_r[parity, 1][None],
            ],
            axis=0,
        )
        inner = inner + jnp.where(
            yi == 0, y_r[parity, 0], jnp.where(yi == ny - 1, y_r[parity, 1], 0.0)
        )
        return inner + jnp.where(
            zi == 0,
            unpack(z_r[parity, 0]),
            jnp.where(zi == nz - 1, unpack(z_r[parity, 1]), 0.0),
        )

    def fault_copy(parity, low, high, order, to):
        return remote(
            c_s.at[parity, low:high],
            c_r.at[parity, low:high],
            c_ss.at[parity],
            c_rs.at[parity, group(low)],
            to,
        )

    def send_faults(parity, values):
        c_s[parity] = values
        for order in order_far_first():
            fault_copy(parity, order, order + 1, order, peer(order)).start()

    def add_faults(parity, inner):
        fault_copy(parity, 1, NEAR, 1, peer(1)).wait_recv()
        inner = inner + scatter(c_r[parity, :NEAR], 0)
        fault_copy(parity, NEAR, peers, NEAR, peer(NEAR)).wait_recv()
        inner = inner + scatter(c_r[parity, NEAR:], NEAR)
        fault_copy(parity, 1, peers, 1, peer(1)).wait_send()
        return inner

    def scalar_round(parity, t, aside):
        send_faults(parity, f_send[t] * gather([delta], True)[0])
        now = delta[...]
        inner = send_faces(
            parity,
            [push[t, 0, dim] * now for dim in range(3)],
            [push[t, 1, dim] * now for dim in range(3)],
        )
        if aside is not None:
            aside()
        inner = add_faces(parity, inner)
        inner = add_faults(parity, inner)
        delta[...] = inner
        total_r[...] += inner

    def dot3(coefficients, values):
        return sum(coefficients(k) * values(k) for k in range(3))

    def scalar_push(t):
        for dim in range(3):
            push[t, 0, dim] = dot3(lambda k: wp[t, dim, k], lambda k: inverse_ref[t, 0, k])
            push[t, 1, dim] = dot3(lambda k: wm[t, dim, k], lambda k: inverse_ref[t, 0, k])

    def scalar_faults(t):
        values = gather([inverse_ref.at[t, 0, k] for k in range(3)], False)
        f_send[t] = dot3(lambda k: f_coef[t, k], lambda k: values[k])

    explicit[...] = sources(1)
    total_r[...] = src[1, 0]
    for k in range(3):
        const[k] = inverse_ref[1, 1, k] * src[1, 1] + inverse_ref[1, 2, k] * src[1, 2]
        lam[1, k] = const[k] + inverse_ref[1, 0, k] * src[1, 0]
    values = gather([lam.at[1, k] for k in range(3)], True)
    for k in range(3):
        v_s[k] = values[k]

    def vector_copy(low, high, to):
        return remote(
            v_s.at[:, low:high],
            v_r.at[:, low:high],
            v_ss,
            v_rs.at[group(low)],
            to,
        )

    for order in order_far_first():
        vector_copy(order, order + 1, peer(order)).start()
    wait_faces([functools.partial(bundle_copy, 0)])
    flags = flags_ref[...].astype(f32)
    face_coefficients(1, flags, None, None, lambda k: (0, 1 + k))
    inner = send_faces(
        0,
        [dot3(lambda k: wp[1, dim, k], lambda k: lam[1, k]) for dim in range(3)],
        [dot3(lambda k: wm[1, dim, k], lambda k: lam[1, k]) for dim in range(3)],
    )
    bundle(1, [mob[0, k] for k in range(3)] + [pressure_ref[t] for t in range(2)])
    start_faces([functools.partial(bundle_copy, 1), map_copy])
    scalar_push(1)
    m_all = remote(m_s.at[:, 1:], m_r.at[:, 1:], m_ss, m_rs, peer(1))
    m_all.wait()
    for t in range(2):
        own_up = jnp.bitwise_and(jnp.right_shift(f_up[...], t), 1) == 1
        for k in range(3):
            q = 3 * (1 - t) + k
            f_coef[t, k] = f_scale[...] * jnp.where(own_up, f_own[q], m_r[q])
    scalar_faults(1)
    inner = add_faces(0, inner)

    def arrived(low, high):
        return dot3(lambda k: f_coef[1, k, low:high], lambda k: v_r[k, low:high])

    vector_copy(1, NEAR, peer(1)).wait_recv()
    inner = inner + scatter(arrived(0, NEAR), 0)
    vector_copy(NEAR, peers, peer(NEAR)).wait_recv()
    inner = inner + scatter(arrived(NEAR, peers), NEAR)
    vector_copy(1, peers, peer(1)).wait_send()
    delta[...] = inner
    total_r[...] += inner

    def prepare_turn():
        explicit[...] += sources(0)
        wait_faces([functools.partial(bundle_copy, 1), map_copy])
        face_coefficients(0, flags_ref[...].astype(f32), None, None, lambda k: (1, k))
        porosity = porosity_ref[...]
        first = src[0, 1] + porosity * (const[0] - const[2])
        second = src[0, 2] + porosity * (const[1] - const[2])
        d_first = porosity * (inverse_ref[1, 0, 0] - inverse_ref[1, 0, 2])
        d_second = porosity * (inverse_ref[1, 0, 1] - inverse_ref[1, 0, 2])
        for k in range(3):
            turn_c[k] = (
                inverse_ref[0, 0, k] * src[0, 0]
                + inverse_ref[0, 1, k] * first
                + inverse_ref[0, 2, k] * second
            )
            turn_d[k] = inverse_ref[0, 1, k] * d_first + inverse_ref[0, 2, k] * d_second
        for side, w in enumerate((wp, wm)):
            for dim in range(3):
                push_turn_c[side, dim] = dot3(lambda k: w[0, dim, k], lambda k: turn_c[k])
                push_turn_d[side, dim] = dot3(lambda k: w[0, dim, k], lambda k: turn_d[k])
        values = gather([ref.at[k] for ref in (turn_c, turn_d) for k in range(3)], False)
        f_send[2] = dot3(lambda k: f_coef[0, k], lambda k: values[k])
        f_send[3] = dot3(lambda k: f_coef[0, k], lambda k: values[3 + k])

    n_rounds = ITERS - 1
    scalar_round(1, 1, prepare_turn)

    def more(t):
        def body(step, carry):
            scalar_round(lax.rem(step, 2), t, None)
            return carry

        return body

    lax.fori_loop(2, n_rounds, more(1), 0)

    out_late = pltpu.make_async_copy(lam.at[1], lam_hbm.at[1], out_sem.at[1])
    out_early = pltpu.make_async_copy(lam.at[0], lam_hbm.at[0], out_sem.at[0])
    parity = n_rounds % 2
    send_faults(parity, f_send[2] + f_send[3] * gather([total_r], True)[0])
    now = total_r[...]
    inner = send_faces(
        parity,
        [push_turn_c[0, dim] + push_turn_d[0, dim] * now for dim in range(3)],
        [push_turn_c[1, dim] + push_turn_d[1, dim] * now for dim in range(3)],
    )
    for k in range(3):
        lam[1, k] = const[k] + inverse_ref[1, 0, k] * total_r[...]
    out_late.start()
    porosity = porosity_ref[...]
    first = src[0, 1] + porosity * (lam[1, 0] - lam[1, 2])
    second = src[0, 2] + porosity * (lam[1, 1] - lam[1, 2])
    for k in range(3):
        const[k] = inverse_ref[0, 1, k] * first + inverse_ref[0, 2, k] * second
    scalar_push(0)
    scalar_faults(0)
    inner = add_faces(parity, inner)
    inner = add_faults(parity, inner)
    delta[...] = inner
    total_r[...] = src[0, 0] + inner

    n_bx, n_by, n_bz = nx // BOX, ny // BOX, nz // BOX
    n_boxes = n_bx * n_by
    wide = n_boxes * n_bz

    def prepare_gradient():
        for dim in range(3):
            got = (bx_r, by_r, bz_r)[dim]
            flux_base[0, dim] = jnp.zeros(shape, f32)
            flux_base[1, dim] = jnp.zeros(shape, f32)
            for t in range(2):
                p_here = pressure_ref[t]
                up_p = 0.5 * (
                    p_here - at_next(p_here, dim, edge_of(dim, got[1, 1, 3 + t]))
                )
                down_p = -0.5 * (
                    at_last(p_here, dim, edge_of(dim, got[1, 0, 3 + t])) - p_here
                )
                source = (lambda k: const[k]) if t == 0 else (lambda k: lam[1, k])
                flux_base[0, dim] += up_p * dot3(lambda k: wp[t, dim, k], source)
                flux_base[1, dim] += down_p * dot3(lambda k: wm[t, dim, k], source)
                if t == 0:
                    flux_lead[0, dim] = up_p * push[0, 0, dim]
                    flux_lead[1, dim] = down_p * push[0, 1, dim]
        steps = []
        for t in range(2):
            water = sat_ref[t + 1, 0] - sat_ref[t, 0]
            oil = sat_ref[t + 1, 1] - sat_ref[t, 1]
            steps.append((water, oil, water + oil))
        por[0] = -(
            lam[1, 0] * steps[1][0]
            + lam[1, 1] * steps[1][1]
            - lam[1, 2] * steps[1][2]
            + const[0] * steps[0][0]
            + const[1] * steps[0][1]
            - const[2] * steps[0][2]
        )
        por[1] = -(
            inverse_ref[0, 0, 0] * steps[0][0]
            + inverse_ref[0, 0, 1] * steps[0][1]
            - inverse_ref[0, 0, 2] * steps[0][2]
        )
        z_lane = lax.broadcasted_iota(jnp.int32, (1, n_bz), 1)

        def own_map(bx, by):
            return map_ref[bx, by : by + 1, :]

        def other_map(dim, side, bx, by):
            return map_r[2 * dim + side, bx, by : by + 1, :]

        labels = [[], [], []]
        for bx in range(n_bx):
            for by in range(n_by):
                labels[0].append(own_map(bx, by))
                labels[1].append(
                    other_map(1, 0, bx, n_by - 1) if by == 0 else other_map(1, 1, bx, 0)
                )
                if bx == 0:
                    label = other_map(0, 0, n_bx - 1, by)
                elif bx == n_bx - 1:
                    label = other_map(0, 1, 0, by)
                else:
                    even, odd = 2 * (bx - 1), 2 * (bx - 1) + 1
                    label = jnp.zeros((1, n_bz), jnp.int32)
                    for lane, side, box in (
                        (0, 0, even),
                        (1, 0, odd),
                        (n_bz - 2, 1, odd),
                        (n_bz - 1, 1, even),
                    ):
                        edge = n_bz - 1 if side == 0 else 0
                        label = jnp.where(
                            z_lane == lane,
                            other_map(2, side, box, by)[:, edge : edge + 1],
                            label,
                        )
                labels[2].append(label)
        n_regions = devices * PARAM_REGIONS
        for part in range(3):
            label = jnp.concatenate(labels[part], axis=1)
            found_hot[:, part * wide : (part + 1) * wide] = (
                (lax.broadcasted_iota(jnp.int32, (n_regions, wide), 0) == label)
                .astype(f32)
                .astype(jnp.bfloat16)
            )

    parity = (n_rounds + 1) % 2
    scalar_round(parity, 0, prepare_gradient)
    lax.fori_loop(n_rounds + 2, 2 * n_rounds, more(0), 0)

    now = total_r[...]
    flux = [
        [flux_base[side, dim] + flux_lead[side, dim] * now for dim in range(3)]
        for side in range(2)
    ]
    gradient = explicit[...]
    for dim in range(3):
        gradient = gradient - (
            flux[0][dim]
            + flux[1][dim]
            + at_last(flux[0][dim], dim, no_edge(dim))
            + at_next(flux[1][dim], dim, no_edge(dim))
        )

    def x_sums(field):
        return jnp.sum(field.reshape(n_bx, BOX, ny, nz), axis=1)

    y_pushed = x_sums(jnp.where(yi == 0, flux[1][1], 0.0) + jnp.where(yi == ny - 1, flux[0][1], 0.0))
    z_pushed = x_sums(jnp.where(zi == 0, flux[1][2], 0.0) + jnp.where(zi == nz - 1, flux[0][2], 0.0))
    lane = lax.broadcasted_iota(jnp.int32, (ny, nz), 1)

    def moved(tile):
        return jnp.where(
            lane == BOX,
            pltpu.roll(tile, BOX, 1),
            jnp.where(lane == nz - 1 - BOX, pltpu.roll(tile, nz - BOX, 1), 0.0),
        )

    mixed = jnp.concatenate(
        [flux[1][0][0][None]]
        + [(z_pushed[2 * n] + moved(z_pushed[2 * n + 1]))[None] for n in range(n_bx // 2)]
        + [flux[0][0][nx - 1][None]],
        axis=0,
    )
    stacked = jnp.concatenate(
        [x_sums(gradient), x_sums(por[0] + por[1] * now), -y_pushed, -mixed], axis=0
    ).reshape(4 * n_bx * ny, nz)
    z_boxes = (
        (
            lax.broadcasted_iota(jnp.int32, (nz, wide), 0) // BOX
            == lax.rem(lax.broadcasted_iota(jnp.int32, (nz, wide), 1), n_bz)
        )
        .astype(f32)
        .astype(jnp.bfloat16)
    )
    boxed = jnp.dot(
        jnp.concatenate(split(stacked, 2), axis=1),
        jnp.concatenate([z_boxes] * 2, axis=0),
        preferred_element_type=f32,
    )
    in_box = (
        lax.broadcasted_iota(jnp.int32, (n_bx * ny, wide), 1) // n_bz
        == lax.broadcasted_iota(jnp.int32, (n_bx * ny, wide), 0) // BOX
    )
    sums = [
        jnp.sum(
            jnp.where(in_box, boxed[n * n_bx * ny : (n + 1) * n_bx * ny], 0.0),
            axis=0,
            keepdims=True,
        )
        for n in range(4)
    ]
    none = jnp.zeros((1, wide), f32)
    perm_row = jnp.concatenate([sums[0], sums[2], sums[3]], axis=1)
    por_row = jnp.concatenate([sums[1], none, none], axis=1)
    parts = [
        part.astype(f32) for row in (perm_row, por_row) for part in split(row, 2)
    ]
    which = lax.broadcasted_iota(jnp.int32, (8, 3 * wide), 0)
    lines = jnp.zeros((8, 3 * wide), f32)
    for n, part in enumerate(parts):
        lines = jnp.where(which == n, part, lines)
    found = lax.dot_general(
        lines.astype(jnp.bfloat16),
        found_hot[...],
        (((1,), (1,)), ((), ())),
        preferred_element_type=f32,
    )
    together = LANES // PARAM_REGIONS
    for n in range(devices // together):
        lanes = slice(n * LANES, (n + 1) * LANES)
        r_s[n, 0:1] = found[0:1, lanes] + found[1:2, lanes]
        r_s[n, 1:2] = found[2:3, lanes] + found[3:4, lanes]
    r_copies = []
    for offset in range(1, devices):
        other = lax.rem(index + offset, devices)
        copy = remote(
            r_s.at[other // together],
            r_r.at[offset],
            r_ss.at[offset],
            r_rs.at[offset],
            device(other),
        )
        copy.start()
        r_copies.append(copy)
    for k in range(3):
        lam[0, k] = const[k] + inverse_ref[0, 0, k] * total_r[...]
    out_early.start()
    part = r_s[index // together]
    for offset, copy in enumerate(r_copies):
        copy.wait_recv()
        part = part + r_r[offset + 1]
    mine = jnp.full((2, PARAM_REGIONS), lax.rem(index, together), jnp.int32)
    result = jnp.zeros((2, PARAM_REGIONS), f32)
    for n in range(together):
        result = jnp.where(
            mine == n, part[:, n * PARAM_REGIONS : (n + 1) * PARAM_REGIONS], result
        )
    region_ref[...] = result
    for copy in r_copies:
        copy.wait_send()
    out_late.wait()
    out_early.wait()


def local(*arrays):
    (
        pressure,
        saturation,
        permeability,
        porosity,
        upwind_flags,
        diag_inverse,
        seismic_obs,
        well_x,
        well_y,
        well_top,
        well_len,
        well_bhp,
        well_obs,
        fault_cell,
        fault_count,
        fault_trans,
        fault_up,
        region_map,
    ) = arrays
    counts = tuple(lax.axis_size(axis) for axis in ("gx", "gy", "gz"))
    nx, ny, nz = permeability.shape
    peers, slots = fault_cell.shape[1:]
    devices = counts[0] * peers
    hbm = pl.BlockSpec(memory_space=pltpu.HBM)
    vmem = pl.BlockSpec(memory_space=pltpu.VMEM)
    f32 = jnp.float32
    bf16 = jnp.bfloat16
    dma = pltpu.SemaphoreType.DMA

    def field(*lead, dtype=f32):
        return pltpu.VMEM(lead + (nx, ny, nz), dtype)

    def per_fault(*lead, dtype=f32):
        return pltpu.VMEM(lead + (peers, slots), dtype)

    bundles = [(2, 2, 5, ny, nz), (2, 2, 5, nx, 1, nz), (2, 2, 5, ny, nz)]
    faces = [(2, ny, nz), (2, nx, 1, nz), (2, ny, nz)]
    large = arrays[:7]
    scratch = [
        *[pltpu.VMEM(array.shape, array.dtype) for array in large],
        dma((len(large),)),
        dma((2,)),
        field(2, 3),
        field(2, 3, 3),
        field(2, 3, 3),
        field(2, 3),
        field(),
        field(2, 3),
        field(3),
        field(1),
        field(3),
        field(3),
        field(2, 2, 3),
        field(2, 3),
        field(2, 3),
        field(2, 3),
        field(2, 3),
        field(2),
        field(),
        field(),
        pltpu.VMEM((nx * ny, peers * slots), bf16),
        pltpu.VMEM((nz, peers * slots), bf16),
        pltpu.VMEM((devices * PARAM_REGIONS, 3 * region_map.size), bf16),
        per_fault(dtype=jnp.int32),
        per_fault(),
        per_fault(dtype=jnp.int32),
        per_fault(),
        per_fault(6),
        per_fault(2, 3),
        per_fault(4),
        *[pltpu.VMEM(s, f32) for s in bundles],
        *[pltpu.VMEM(s, f32) for s in bundles],
        dma((2, 3, 2)),
        dma((2, 3, 2)),
        pltpu.VMEM((6,) + region_map.shape, jnp.int32),
        dma((3, 2)),
        dma((3, 2)),
        per_fault(6),
        per_fault(6),
        dma,
        dma,
        pltpu.VMEM((8, LANES), f32),
        pltpu.VMEM((counts[2], 8, LANES), f32),
        dma((counts[2],)),
        dma((counts[2],)),
        *[pltpu.VMEM(s, f32) for s in faces],
        *[pltpu.VMEM((2,) + s, f32) for s in faces],
        dma((3, 2)),
        dma((2, 3, 2)),
        per_fault(3),
        per_fault(3),
        dma,
        dma((2,)),
        per_fault(2),
        per_fault(2),
        dma((2,)),
        dma((2, 2)),
        pltpu.VMEM((devices * PARAM_REGIONS // LANES, 2, LANES), f32),
        pltpu.VMEM((devices, 2, LANES), f32),
        dma((devices,)),
        dma((devices,)),
    ]
    return pl.pallas_call(
        functools.partial(kernel, counts),
        out_shape=(
            jax.ShapeDtypeStruct((2, 3, nx, ny, nz), f32),
            jax.ShapeDtypeStruct((2, PARAM_REGIONS), f32),
        ),
        in_specs=[hbm] * 7 + [vmem] * 11,
        out_specs=(hbm, vmem),
        scratch_shapes=scratch,
        compiler_params=pltpu.CompilerParams(
            collective_id=0, has_side_effects=True, vmem_limit_bytes=60 * 2**20
        ),
    )(*arrays)


def solution(mesh):
    cells = P("gx", "gy", "gz")
    column = P("gx", "gy", None)
    every = ("gx", "gy", "gz")
    placed = (
        P(None, "gx", "gy", "gz"),
        P(None, None, "gx", "gy", "gz"),
        cells,
        cells,
        cells,
        P(None, None, None, "gx", "gy", "gz"),
        cells,
        column,
        column,
        column,
        column,
        P(None, "gx", "gy", None),
        P(None, "gx", "gy", None),
        P(every, None, None),
        P(every, None),
        P(every, None, None),
        P(every, None, None),
        cells,
    )
    return jax.shard_map(
        local,
        mesh=mesh,
        in_specs=placed,
        out_specs=(P(None, None, "gx", "gy", "gz"), P(None, every)),
        check_vma=False,
    )
```

```python
import functools

import jax
import jax.numpy as jnp
from jax import lax
from jax.experimental import pallas as pl
from jax.experimental.pallas import tpu as pltpu
from jax.sharding import PartitionSpec as P

ITERS = 6
BOX = 4
PARAM_REGIONS = 32
LANES = 128
CUTS = (1, 8, 12, 16)
MESH = pl.DeviceIdType.MESH

fluid_viscosity = (0.4, 0.5, 1.0)
sigma_sq = 64.0
SIDES = tuple((dim, side) for dim in range(3) for side in range(2))


def phase_mobility(water_sat, oil_sat):
    gas_sat = 1.0 - water_sat - oil_sat
    return [
        water_sat * water_sat / fluid_viscosity[0],
        oil_sat * oil_sat / fluid_viscosity[1],
        gas_sat * gas_sat / fluid_viscosity[2],
    ]


def mobility_slopes(water_sat, oil_sat):
    gas_sat = 1.0 - water_sat - oil_sat
    return (
        2.0 * water_sat / fluid_viscosity[0] - 2.0 * gas_sat / fluid_viscosity[2],
        2.0 * oil_sat / fluid_viscosity[1] - 2.0 * gas_sat / fluid_viscosity[2],
    )


def split(value, parts):
    pieces = []
    for _ in range(parts):
        piece = value.astype(jnp.bfloat16)
        pieces.append(piece)
        value = value - piece.astype(jnp.float32)
    return pieces


def kernel(
    counts,
    pressure_hbm,
    saturation_hbm,
    perm_hbm,
    porosity_hbm,
    flags_hbm,
    inverse_hbm,
    seismic_hbm,
    well_x_ref,
    well_y_ref,
    well_top_ref,
    well_len_ref,
    bhp_ref,
    obs_ref,
    fault_cell_ref,
    fault_count_ref,
    fault_trans_ref,
    fault_up_ref,
    map_ref,
    lam_hbm,
    region_ref,
    pressure_ref,
    sat_ref,
    perm_ref,
    porosity_ref,
    flags_ref,
    inverse_ref,
    seismic_ref,
    in_sem,
    out_sem,
    mob,
    wp,
    wm,
    src,
    explicit,
    lam,
    const,
    lead,
    turn_c,
    turn_d,
    push,
    push_turn_c,
    push_turn_d,
    flux_base,
    flux_lead,
    por,
    total_r,
    delta,
    row_hot,
    z_hot,
    found_hot,
    f_cell,
    f_scale,
    f_up,
    f_tmp,
    f_own,
    f_coef,
    f_send,
    bx_s,
    by_s,
    bz_s,
    bx_r,
    by_r,
    bz_r,
    b_ss,
    b_rs,
    map_r,
    map_ss,
    map_rs,
    m_s,
    m_r,
    m_ss,
    m_rs,
    w_s,
    w_r,
    w_ss,
    w_rs,
    x_s,
    y_s,
    z_s,
    x_r,
    y_r,
    z_r,
    h_ss,
    h_rs,
    v_s,
    v_r,
    v_ss,
    v_rs,
    c_s,
    c_r,
    c_ss,
    c_rs,
    r_s,
    r_r,
    r_ss,
    r_rs,
):
    n_gx, n_gy, n_gz = counts
    here = (lax.axis_index("gx"), lax.axis_index("gy"), lax.axis_index("gz"))
    peers = n_gy * n_gz
    devices = n_gx * peers
    me = here[1] * n_gz + here[2]
    index = here[0] * peers + me
    shape = perm_ref.shape
    nx, ny, nz = shape
    rows = nx * ny
    slots = c_r.shape[2]
    f32 = jnp.float32

    def flip(number, bits):
        bit = 1
        while bit <= bits:
            if bits & bit:
                number = number + bit - 2 * bit * lax.rem(number // bit, 2)
            bit *= 2
        return number

    def peer(order):
        return (here[0], flip(here[1], order // n_gz), flip(here[2], order % n_gz))

    def peer_place(order):
        other = peer(order)
        return other[1] * n_gz + other[2]

    def toward(dim, step):
        moved = list(here)
        moved[dim] = lax.rem(here[dim] + step + counts[dim], counts[dim])
        return tuple(moved)

    def device(number):
        return (number // peers, lax.rem(number, peers) // n_gz, lax.rem(number, n_gz))

    def remote(source, target, send, recv, to):
        return pltpu.make_async_remote_copy(
            src_ref=source,
            dst_ref=target,
            send_sem=send,
            recv_sem=recv,
            device_id=to,
            device_id_type=MESH,
        )

    has_next = [here[dim] < counts[dim] - 1 for dim in range(3)]
    has_last = [here[dim] > 0 for dim in range(3)]

    def sends(dim, side):
        return has_next[dim] if side == 0 else has_last[dim]

    def receives(dim, side):
        return has_last[dim] if side == 0 else has_next[dim]

    loads = [
        pltpu.make_async_copy(source, target, in_sem.at[n])
        for n, (source, target) in enumerate(
            (
                (saturation_hbm, sat_ref),
                (perm_hbm, perm_ref),
                (pressure_hbm, pressure_ref),
                (flags_hbm, flags_ref),
                (seismic_hbm, seismic_ref),
                (inverse_hbm, inverse_ref),
                (porosity_hbm, porosity_ref),
            )
        )
    ]
    for load in loads:
        load.start()
    for ref in (bx_r, by_r, bz_r, x_r, y_r, z_r, m_r, v_r, c_r, map_r):
        ref[...] = jnp.zeros_like(ref)

    barrier = pltpu.get_barrier_semaphore()
    for offset in range(1, devices):
        pl.semaphore_signal(
            barrier,
            inc=1,
            device_id=device(lax.rem(index + offset, devices)),
            device_id_type=MESH,
        )

    yi = lax.broadcasted_iota(jnp.int32, shape, 1)
    zi = lax.broadcasted_iota(jnp.int32, shape, 2)
    iotas = (None, yi, zi)
    diagonal = lax.broadcasted_iota(jnp.int32, shape, 0) == zi

    def pack(field, lane):
        return jnp.sum(jnp.where(diagonal, field[:, :, lane : lane + 1], 0.0), axis=0)

    def unpack(tile):
        return jnp.concatenate(
            [jnp.broadcast_to(tile[:, x : x + 1], (ny, nz))[None] for x in range(nx)], axis=0
        )

    def at_next(field, dim, edge):
        if dim == 0:
            return jnp.concatenate([field[1:], edge], axis=0)
        last = shape[dim] - 1
        return jnp.where(iotas[dim] == last, edge, pltpu.roll(field, last, dim))

    def at_last(field, dim, edge):
        if dim == 0:
            return jnp.concatenate([edge, field[:-1]], axis=0)
        return jnp.where(iotas[dim] == 0, edge, pltpu.roll(field, 1, dim))

    def edge_of(dim, halo):
        if dim == 0:
            return halo[None]
        return halo if dim == 1 else unpack(halo)

    def no_edge(dim):
        return jnp.zeros((1, ny, nz), f32) if dim == 0 else 0.0

    def faults_in_order(array, target):
        for order in range(peers):
            target[order : order + 1, :] = array[pl.ds(peer_place(order), 1), :]

    faults_in_order(fault_cell_ref.at[0], f_cell)
    faults_in_order(fault_up_ref.at[0], f_up)
    slot_index = lax.broadcasted_iota(jnp.int32, (1, slots), 1)
    for p in range(peers):
        f_tmp[p : p + 1, :] = jnp.where(
            slot_index < fault_count_ref[:, p : p + 1], fault_trans_ref[0, p : p + 1, :], 0.0
        )
    faults_in_order(f_tmp, f_scale)
    f_row = f_cell[...] // nz
    f_z = f_cell[...] - f_row * nz

    def gather_half(ref, low, high):
        row, at = f_row[low:high], f_z[low:high]

        def body(x, chosen):
            for y in range(ny):
                taken = jnp.take_along_axis(
                    jnp.broadcast_to(ref[x, y : y + 1, :], (high - low, nz)),
                    at,
                    axis=1,
                    mode="promise_in_bounds",
                )
                chosen = jnp.where(row == x * ny + y, taken, chosen)
            return chosen

        return lax.fori_loop(0, nx, body, jnp.zeros((high - low, slots), f32), unroll=True)

    def gather(refs, unroll):
        def body(x, chosen):
            for y in range(ny):
                here_row = f_row == x * ny + y
                chosen = [
                    jnp.where(
                        here_row,
                        jnp.take_along_axis(
                            jnp.broadcast_to(ref[x, y : y + 1, :], (peers, nz)),
                            f_z,
                            axis=1,
                            mode="promise_in_bounds",
                        ),
                        value,
                    )
                    for ref, value in zip(refs, chosen)
                ]
            return chosen

        start = [jnp.zeros((peers, slots), f32) for _ in refs]
        return lax.fori_loop(0, nx, body, start, unroll=unroll)

    loads[0].wait()
    mobility = [phase_mobility(sat_ref[t + 1, 0], sat_ref[t + 1, 1]) for t in range(2)]
    for t in range(2):
        for k in range(3):
            mob[t, k] = mobility[t][k]
    for load in loads[1:4]:
        load.wait()
    perm = perm_ref[...]

    def bundle(part, fields):
        for q, field in enumerate(fields):
            bx_s[part, 0, q] = field[nx - 1]
            bx_s[part, 1, q] = field[0]
            by_s[part, 0, q] = field[:, ny - 1 :, :]
            by_s[part, 1, q] = field[:, :1, :]
            bz_s[part, 0, q] = pack(field, nz - 1)
            bz_s[part, 1, q] = pack(field, 0)

    def bundle_copy(part, dim, side):
        sent, got = ((bx_s, bx_r), (by_s, by_r), (bz_s, bz_r))[dim]
        return remote(
            sent.at[part, side],
            got.at[part, side],
            b_ss.at[part, dim, side],
            b_rs.at[part, dim, side],
            toward(dim, 1 - 2 * side),
        )

    def map_copy(dim, side):
        return remote(
            map_ref,
            map_r.at[2 * dim + side],
            map_ss.at[dim, side],
            map_rs.at[dim, side],
            toward(dim, 1 - 2 * side),
        )

    def start_faces(copies):
        for dim, side in SIDES:

            @pl.when(sends(dim, side))
            def _():
                for copy in copies:
                    copy(dim, side).start()

    def wait_faces(copies):
        for dim, side in SIDES:

            @pl.when(sends(dim, side))
            def _():
                for copy in copies:
                    copy(dim, side).wait_send()

            @pl.when(receives(dim, side))
            def _():
                for copy in copies:
                    copy(dim, side).wait_recv()

    bundle(0, [perm] + mobility[1] + [flags_ref[...].astype(f32)])

    n_wells = well_top_ref.shape[2]
    eye = lax.broadcasted_iota(jnp.int32, (n_wells, n_wells), 0) == lax.broadcasted_iota(
        jnp.int32, (n_wells, n_wells), 1
    )

    def as_column(row):
        return jnp.sum(jnp.where(eye, row.astype(f32), 0.0), axis=1, keepdims=True)

    def as_row(column):
        return jnp.sum(jnp.where(eye, column, 0.0), axis=0, keepdims=True)

    well_row = well_x_ref[0] * ny + well_y_ref[0]
    well_hot = (
        (
            lax.broadcasted_iota(jnp.int32, (n_wells, rows), 1).astype(f32) == as_column(well_row)
        )
        .astype(f32)
        .astype(jnp.bfloat16)
    )
    well_hot_t = (lax.broadcasted_iota(jnp.int32, (rows, n_wells), 0) == well_row).astype(f32)
    depth = (here[2] * nz + lax.broadcasted_iota(jnp.int32, (n_wells, nz), 1)).astype(f32)
    top = as_column(well_top_ref[0])
    bottom = as_column(well_top_ref[0] + well_len_ref[0])
    perforated = jnp.where((depth >= top) & (depth < bottom), 1.0, 0.0)

    def total(t):
        return perm_ref[...] * (mob[t, 0] + mob[t, 1] + mob[t, 2])

    fields = []
    for t in range(2):
        whole = total(t)
        fields += [
            (whole * pressure_ref[t]).reshape(rows, nz),
            whole.reshape(rows, nz),
        ]
    pieces = jnp.concatenate(split(jnp.concatenate(fields, axis=1), 3), axis=0)
    of_wells = jnp.dot(
        jnp.concatenate([well_hot] * 3, axis=1), pieces, preferred_element_type=f32
    )
    w_s[...] = jnp.zeros_like(w_s)
    for t in range(2):
        bhp = as_column(bhp_ref[t, 0])
        rate = jnp.sum(
            perforated
            * (
                of_wells[:, 2 * t * nz : (2 * t + 1) * nz]
                - bhp * of_wells[:, (2 * t + 1) * nz : (2 * t + 2) * nz]
            ),
            axis=1,
            keepdims=True,
        )
        w_s[t : t + 1, :n_wells] = as_row(rate)

    pl.semaphore_wait(barrier, devices - 1)
    w_copies = []
    for offset in range(1, n_gz):
        copy = remote(
            w_s,
            w_r.at[offset],
            w_ss.at[offset],
            w_rs.at[offset],
            (here[0], here[1], lax.rem(here[2] + offset, n_gz)),
        )
        copy.start()
        w_copies.append(copy)
    start_faces([functools.partial(bundle_copy, 0)])

    def order_far_first():
        return range(peers - 1, 0, -1)

    groups = list(zip(CUTS[:-1], CUTS[1:]))

    def group(order):
        return [low <= order < high for low, high in groups].index(True)

    own = gather([mob.at[t, k] for t in (1, 0) for k in range(3)], False)
    for q in range(6):
        f_own[q] = own[q]
        m_s[q] = own[q]
    for order in order_far_first():
        remote(
            m_s.at[:, pl.ds(order, 1)],
            m_r.at[:, pl.ds(order, 1)],
            m_ss,
            m_rs,
            peer(order),
        ).start()

    for order in range(peers):
        lanes = slice(order * slots, (order + 1) * slots)
        row_hot[:, lanes] = (
            (lax.broadcasted_iota(jnp.int32, (rows, slots), 0) == f_row[order : order + 1])
            .astype(f32)
            .astype(jnp.bfloat16)
        )
        z_hot[lanes, :] = (
            (lax.broadcasted_iota(jnp.int32, (nz, slots), 0) == f_z[order : order + 1])
            .astype(f32)
            .T.astype(jnp.bfloat16)
        )

    def scatter(read, start, stop):
        base = start // 4 * 4
        parts = split(read(base, stop), 2)
        marked = [[], []]
        for order in range(start, stop):
            hot = row_hot[:, order * slots : (order + 1) * slots]
            at = order - base
            for pieces, part in zip(marked, parts):
                pieces.append(hot * jnp.broadcast_to(part[at : at + 1], hot.shape))
        added = lax.dot_general(
            jnp.concatenate([jnp.concatenate(pieces, axis=1) for pieces in marked], axis=0),
            z_hot[start * slots : stop * slots, :],
            (((1,), (0,)), ((), ())),
            preferred_element_type=f32,
        )
        return (added[:rows] + added[rows:]).reshape(shape)

    for load in loads[4:]:
        load.wait()
    for copy in w_copies:
        copy.wait()
    rates = w_s[...]
    for offset in range(1, n_gz):
        rates = rates + w_r[offset]

    def sources(t):
        misfit = (rates[t : t + 1, :n_wells] - obs_ref[t, 0]) / sigma_sq
        weighted = well_hot_t * misfit
        both = jnp.concatenate([weighted, weighted * bhp_ref[t, 0]], axis=0)
        spread = jnp.dot(
            jnp.concatenate(split(both, 3), axis=0),
            perforated.astype(jnp.bfloat16),
            preferred_element_type=f32,
        )
        spread = spread[: 2 * rows] + spread[2 * rows : 4 * rows] + spread[4 * rows :]
        drawn = pressure_ref[t] * spread[:rows].reshape(shape) - spread[rows:].reshape(shape)
        water_slope, oil_slope = mobility_slopes(sat_ref[t + 1, 0], sat_ref[t + 1, 1])
        whole = total(t)
        src[t, 0] = whole * spread[:rows].reshape(shape)
        water_source = perm_ref[...] * drawn * water_slope
        if t == 1:
            water_source = water_source + (sat_ref[2, 0] - seismic_ref[...])
        src[t, 1] = water_source
        src[t, 2] = perm_ref[...] * drawn * oil_slope
        return whole * drawn

    def face_coefficients(t, flags, bits_at, perm_from, mob_from):
        own_flags = flags.astype(jnp.int32)
        for dim in range(3):
            got = (bx_r, by_r, bz_r)[dim]

            def halo(part, side, q):
                return edge_of(dim, got[part, side, q])

            up_face = jnp.sqrt(
                perm_ref[...] * at_next(perm_ref[...], dim, halo(0, 1, 0))
            )
            low_face = jnp.sqrt(
                perm_ref[...] * at_last(perm_ref[...], dim, halo(0, 0, 0))
            )
            up_ok = has_next[dim].astype(f32)
            low_ok = has_last[dim].astype(f32)
            if dim == 0:
                up_face = jnp.concatenate([up_face[:-1], up_face[-1:] * up_ok], axis=0)
                low_face = jnp.concatenate([low_face[:1] * low_ok, low_face[1:]], axis=0)
            else:
                up_face = up_face * jnp.where(iotas[dim] == shape[dim] - 1, up_ok, 1.0)
                low_face = low_face * jnp.where(iotas[dim] == 0, low_ok, 1.0)
            bit = 3 * t + dim
            low_flags = at_last(flags, dim, halo(0, 0, 4)).astype(jnp.int32)
            own_up = jnp.bitwise_and(jnp.right_shift(own_flags, bit), 1) == 1
            low_up = jnp.bitwise_and(jnp.right_shift(low_flags, bit), 1) == 1
            for k in range(3):
                part, q = mob_from(k)
                m = mob[t, k]
                wp[t, dim, k] = up_face * jnp.where(
                    own_up, m, at_next(m, dim, halo(part, 1, q))
                )
                wm[t, dim, k] = low_face * jnp.where(
                    low_up, at_last(m, dim, halo(part, 0, q)), m
                )

    def face_copy(parity, dim, side):
        sent, got = ((x_s, x_r), (y_s, y_r), (z_s, z_r))[dim]
        return remote(
            sent.at[side],
            got.at[parity, side],
            h_ss.at[dim, side],
            h_rs.at[parity, dim, side],
            toward(dim, 1 - 2 * side),
        )

    def send_faces(parity, up, down):
        x_s[0] = up[0][nx - 1]
        x_s[1] = down[0][0]
        y_s[0] = up[1][:, ny - 1 :, :]
        y_s[1] = down[1][:, :1, :]
        z_s[0] = pack(up[2], nz - 1)
        z_s[1] = pack(down[2], 0)
        start_faces([functools.partial(face_copy, parity)])
        inner = at_last(up[0], 0, no_edge(0)) + at_next(down[0], 0, no_edge(0))
        for dim in (1, 2):
            inner = inner + at_last(up[dim], dim, 0.0) + at_next(down[dim], dim, 0.0)
        return inner

    def add_faces(parity, inner):
        wait_faces([functools.partial(face_copy, parity)])
        inner = jnp.concatenate(
            [
                inner[:1] + x_r[parity, 0][None],
                inner[1 : nx - 1],
                inner[nx - 1 :] + x_r[parity, 1][None],
            ],
            axis=0,
        )
        inner = inner + jnp.where(
            yi == 0, y_r[parity, 0], jnp.where(yi == ny - 1, y_r[parity, 1], 0.0)
        )
        return inner + jnp.where(
            zi == 0,
            unpack(z_r[parity, 0]),
            jnp.where(zi == nz - 1, unpack(z_r[parity, 1]), 0.0),
        )

    def fault_copy(parity, low, high, order, to):
        return remote(
            c_s.at[parity, low:high],
            c_r.at[parity, low:high],
            c_ss.at[parity],
            c_rs.at[parity, group(low)],
            to,
        )

    def send_faults(parity, ref, lead, fixed):
        for low in range(peers - 8, -8, -8):
            part = slice(low, low + 8)
            values = f_send[lead, part] * gather_half(ref, low, low + 8)
            if fixed is not None:
                values = values + f_send[fixed, part]
            c_s[parity, part] = values
            for order in range(low + 7, max(low, 1) - 1, -1):
                fault_copy(parity, order, order + 1, order, peer(order)).start()

    def add_faults(parity, inner):
        def read(low, high):
            return c_r[parity, low:high]

        for low, high in groups:
            fault_copy(parity, low, high, low, peer(low)).wait_recv()
            inner = inner + scatter(read, low, high)
        fault_copy(parity, 1, peers, 1, peer(1)).wait_send()
        return inner

    def scalar_round(parity, t, aside):
        send_faults(parity, delta, t, None)
        now = delta[...]
        inner = send_faces(
            parity,
            [push[t, 0, dim] * now for dim in range(3)],
            [push[t, 1, dim] * now for dim in range(3)],
        )
        if aside is not None:
            aside()
        inner = add_faces(parity, inner)
        inner = add_faults(parity, inner)
        delta[...] = inner
        total_r[...] += inner

    def dot3(coefficients, values):
        return sum(coefficients(k) * values(k) for k in range(3))

    def scalar_push(t):
        for dim in range(3):
            push[t, 0, dim] = dot3(lambda k: wp[t, dim, k], lambda k: inverse_ref[t, 0, k])
            push[t, 1, dim] = dot3(lambda k: wm[t, dim, k], lambda k: inverse_ref[t, 0, k])

    def scalar_faults(t):
        values = gather([inverse_ref.at[t, 0, k] for k in range(3)], False)
        f_send[t] = dot3(lambda k: f_coef[t, k], lambda k: values[k])

    explicit[...] = sources(1)
    total_r[...] = src[1, 0]
    for k in range(3):
        const[k] = inverse_ref[1, 1, k] * src[1, 1] + inverse_ref[1, 2, k] * src[1, 2]
        lam[1, k] = const[k] + inverse_ref[1, 0, k] * src[1, 0]
    values = gather([lam.at[1, k] for k in range(3)], True)
    for k in range(3):
        v_s[k] = values[k]

    def vector_copy(low, high, to):
        return remote(
            v_s.at[:, low:high],
            v_r.at[:, low:high],
            v_ss,
            v_rs.at[group(low)],
            to,
        )

    for order in order_far_first():
        vector_copy(order, order + 1, peer(order)).start()
    wait_faces([functools.partial(bundle_copy, 0)])
    flags = flags_ref[...].astype(f32)
    face_coefficients(1, flags, None, None, lambda k: (0, 1 + k))
    inner = send_faces(
        0,
        [dot3(lambda k: wp[1, dim, k], lambda k: lam[1, k]) for dim in range(3)],
        [dot3(lambda k: wm[1, dim, k], lambda k: lam[1, k]) for dim in range(3)],
    )
    bundle(1, [mob[0, k] for k in range(3)] + [pressure_ref[t] for t in range(2)])
    start_faces([functools.partial(bundle_copy, 1), map_copy])
    scalar_push(1)
    m_all = remote(m_s.at[:, 1:], m_r.at[:, 1:], m_ss, m_rs, peer(1))
    m_all.wait()
    for t in range(2):
        own_up = jnp.bitwise_and(jnp.right_shift(f_up[...], t), 1) == 1
        for k in range(3):
            q = 3 * (1 - t) + k
            f_coef[t, k] = f_scale[...] * jnp.where(own_up, f_own[q], m_r[q])
    scalar_faults(1)
    inner = add_faces(0, inner)

    def arrived(low, high):
        return dot3(lambda k: f_coef[1, k, low:high], lambda k: v_r[k, low:high])

    for low, high in groups:
        vector_copy(low, high, peer(low)).wait_recv()
        inner = inner + scatter(arrived, low, high)
    vector_copy(1, peers, peer(1)).wait_send()
    delta[...] = inner
    total_r[...] += inner

    def prepare_turn():
        explicit[...] += sources(0)
        wait_faces([functools.partial(bundle_copy, 1), map_copy])
        face_coefficients(0, flags_ref[...].astype(f32), None, None, lambda k: (1, k))
        porosity = porosity_ref[...]
        first = src[0, 1] + porosity * (const[0] - const[2])
        second = src[0, 2] + porosity * (const[1] - const[2])
        d_first = porosity * (inverse_ref[1, 0, 0] - inverse_ref[1, 0, 2])
        d_second = porosity * (inverse_ref[1, 0, 1] - inverse_ref[1, 0, 2])
        for k in range(3):
            turn_c[k] = (
                inverse_ref[0, 0, k] * src[0, 0]
                + inverse_ref[0, 1, k] * first
                + inverse_ref[0, 2, k] * second
            )
            turn_d[k] = inverse_ref[0, 1, k] * d_first + inverse_ref[0, 2, k] * d_second
        for side, w in enumerate((wp, wm)):
            for dim in range(3):
                push_turn_c[side, dim] = dot3(lambda k: w[0, dim, k], lambda k: turn_c[k])
                push_turn_d[side, dim] = dot3(lambda k: w[0, dim, k], lambda k: turn_d[k])
        values = gather([ref.at[k] for ref in (turn_c, turn_d) for k in range(3)], False)
        f_send[2] = dot3(lambda k: f_coef[0, k], lambda k: values[k])
        f_send[3] = dot3(lambda k: f_coef[0, k], lambda k: values[3 + k])

    n_rounds = ITERS - 1
    scalar_round(1, 1, prepare_turn)

    def more(t):
        def body(step, carry):
            scalar_round(lax.rem(step, 2), t, None)
            return carry

        return body

    lax.fori_loop(2, n_rounds, more(1), 0)

    out_late = pltpu.make_async_copy(lam.at[1], lam_hbm.at[1], out_sem.at[1])
    out_early = pltpu.make_async_copy(lam.at[0], lam_hbm.at[0], out_sem.at[0])
    parity = n_rounds % 2
    send_faults(parity, total_r, 3, 2)
    now = total_r[...]
    inner = send_faces(
        parity,
        [push_turn_c[0, dim] + push_turn_d[0, dim] * now for dim in range(3)],
        [push_turn_c[1, dim] + push_turn_d[1, dim] * now for dim in range(3)],
    )
    for k in range(3):
        lam[1, k] = const[k] + inverse_ref[1, 0, k] * total_r[...]
    out_late.start()
    porosity = porosity_ref[...]
    first = src[0, 1] + porosity * (lam[1, 0] - lam[1, 2])
    second = src[0, 2] + porosity * (lam[1, 1] - lam[1, 2])
    for k in range(3):
        const[k] = inverse_ref[0, 1, k] * first + inverse_ref[0, 2, k] * second
    scalar_push(0)
    scalar_faults(0)
    inner = add_faces(parity, inner)
    inner = add_faults(parity, inner)
    delta[...] = inner
    total_r[...] = src[0, 0] + inner

    n_bx, n_by, n_bz = nx // BOX, ny // BOX, nz // BOX
    n_boxes = n_bx * n_by
    wide = n_boxes * n_bz

    def prepare_gradient():
        for dim in range(3):
            got = (bx_r, by_r, bz_r)[dim]
            flux_base[0, dim] = jnp.zeros(shape, f32)
            flux_base[1, dim] = jnp.zeros(shape, f32)
            for t in range(2):
                p_here = pressure_ref[t]
                up_p = 0.5 * (
                    p_here - at_next(p_here, dim, edge_of(dim, got[1, 1, 3 + t]))
                )
                down_p = -0.5 * (
                    at_last(p_here, dim, edge_of(dim, got[1, 0, 3 + t])) - p_here
                )
                source = (lambda k: const[k]) if t == 0 else (lambda k: lam[1, k])
                flux_base[0, dim] += up_p * dot3(lambda k: wp[t, dim, k], source)
                flux_base[1, dim] += down_p * dot3(lambda k: wm[t, dim, k], source)
                if t == 0:
                    flux_lead[0, dim] = up_p * push[0, 0, dim]
                    flux_lead[1, dim] = down_p * push[0, 1, dim]
        steps = []
        for t in range(2):
            water = sat_ref[t + 1, 0] - sat_ref[t, 0]
            oil = sat_ref[t + 1, 1] - sat_ref[t, 1]
            steps.append((water, oil, water + oil))
        por[0] = -(
            lam[1, 0] * steps[1][0]
            + lam[1, 1] * steps[1][1]
            - lam[1, 2] * steps[1][2]
            + const[0] * steps[0][0]
            + const[1] * steps[0][1]
            - const[2] * steps[0][2]
        )
        por[1] = -(
            inverse_ref[0, 0, 0] * steps[0][0]
            + inverse_ref[0, 0, 1] * steps[0][1]
            - inverse_ref[0, 0, 2] * steps[0][2]
        )
        z_lane = lax.broadcasted_iota(jnp.int32, (1, n_bz), 1)

        def own_map(bx, by):
            return map_ref[bx, by : by + 1, :]

        def other_map(dim, side, bx, by):
            return map_r[2 * dim + side, bx, by : by + 1, :]

        labels = [[], [], []]
        for bx in range(n_bx):
            for by in range(n_by):
                labels[0].append(own_map(bx, by))
                labels[1].append(
                    other_map(1, 0, bx, n_by - 1) if by == 0 else other_map(1, 1, bx, 0)
                )
                if bx == 0:
                    label = other_map(0, 0, n_bx - 1, by)
                elif bx == n_bx - 1:
                    label = other_map(0, 1, 0, by)
                else:
                    even, odd = 2 * (bx - 1), 2 * (bx - 1) + 1
                    label = jnp.zeros((1, n_bz), jnp.int32)
                    for lane, side, box in (
                        (0, 0, even),
                        (1, 0, odd),
                        (n_bz - 2, 1, odd),
                        (n_bz - 1, 1, even),
                    ):
                        edge = n_bz - 1 if side == 0 else 0
                        label = jnp.where(
                            z_lane == lane,
                            other_map(2, side, box, by)[:, edge : edge + 1],
                            label,
                        )
                labels[2].append(label)
        n_regions = devices * PARAM_REGIONS
        for part in range(3):
            label = jnp.concatenate(labels[part], axis=1)
            found_hot[:, part * wide : (part + 1) * wide] = (
                (lax.broadcasted_iota(jnp.int32, (n_regions, wide), 0) == label)
                .astype(f32)
                .astype(jnp.bfloat16)
            )

    parity = (n_rounds + 1) % 2
    scalar_round(parity, 0, prepare_gradient)
    lax.fori_loop(n_rounds + 2, 2 * n_rounds, more(0), 0)

    now = total_r[...]
    flux = [
        [flux_base[side, dim] + flux_lead[side, dim] * now for dim in range(3)]
        for side in range(2)
    ]
    gradient = explicit[...]
    for dim in range(3):
        gradient = gradient - (
            flux[0][dim]
            + flux[1][dim]
            + at_last(flux[0][dim], dim, no_edge(dim))
            + at_next(flux[1][dim], dim, no_edge(dim))
        )

    def x_sums(field):
        return jnp.sum(field.reshape(n_bx, BOX, ny, nz), axis=1)

    y_pushed = x_sums(jnp.where(yi == 0, flux[1][1], 0.0) + jnp.where(yi == ny - 1, flux[0][1], 0.0))
    z_pushed = x_sums(jnp.where(zi == 0, flux[1][2], 0.0) + jnp.where(zi == nz - 1, flux[0][2], 0.0))
    lane = lax.broadcasted_iota(jnp.int32, (ny, nz), 1)

    def moved(tile):
        return jnp.where(
            lane == BOX,
            pltpu.roll(tile, BOX, 1),
            jnp.where(lane == nz - 1 - BOX, pltpu.roll(tile, nz - BOX, 1), 0.0),
        )

    mixed = jnp.concatenate(
        [flux[1][0][0][None]]
        + [(z_pushed[2 * n] + moved(z_pushed[2 * n + 1]))[None] for n in range(n_bx // 2)]
        + [flux[0][0][nx - 1][None]],
        axis=0,
    )
    stacked = jnp.concatenate(
        [x_sums(gradient), x_sums(por[0] + por[1] * now), -y_pushed, -mixed], axis=0
    ).reshape(4 * n_bx * ny, nz)
    z_boxes = (
        (
            lax.broadcasted_iota(jnp.int32, (nz, wide), 0) // BOX
            == lax.rem(lax.broadcasted_iota(jnp.int32, (nz, wide), 1), n_bz)
        )
        .astype(f32)
        .astype(jnp.bfloat16)
    )
    boxed = jnp.dot(
        jnp.concatenate(split(stacked, 2), axis=1),
        jnp.concatenate([z_boxes] * 2, axis=0),
        preferred_element_type=f32,
    )
    in_box = (
        lax.broadcasted_iota(jnp.int32, (n_bx * ny, wide), 1) // n_bz
        == lax.broadcasted_iota(jnp.int32, (n_bx * ny, wide), 0) // BOX
    )
    sums = [
        jnp.sum(
            jnp.where(in_box, boxed[n * n_bx * ny : (n + 1) * n_bx * ny], 0.0),
            axis=0,
            keepdims=True,
        )
        for n in range(4)
    ]
    none = jnp.zeros((1, wide), f32)
    perm_row = jnp.concatenate([sums[0], sums[2], sums[3]], axis=1)
    por_row = jnp.concatenate([sums[1], none, none], axis=1)
    parts = [
        part.astype(f32) for row in (perm_row, por_row) for part in split(row, 2)
    ]
    which = lax.broadcasted_iota(jnp.int32, (8, 3 * wide), 0)
    lines = jnp.zeros((8, 3 * wide), f32)
    for n, part in enumerate(parts):
        lines = jnp.where(which == n, part, lines)
    found = lax.dot_general(
        lines.astype(jnp.bfloat16),
        found_hot[...],
        (((1,), (1,)), ((), ())),
        preferred_element_type=f32,
    )
    together = LANES // PARAM_REGIONS
    for n in range(devices // together):
        lanes = slice(n * LANES, (n + 1) * LANES)
        r_s[n, 0:1] = found[0:1, lanes] + found[1:2, lanes]
        r_s[n, 1:2] = found[2:3, lanes] + found[3:4, lanes]
    for order in sorted(range(1, devices), key=lambda n: (-(n % peers // n_gz), -n)):
        to = (flip(here[0], order // peers),) + peer(order % peers)[1:]
        other = to[0] * peers + to[1] * n_gz + to[2]
        remote(
            r_s.at[other // together],
            r_r.at[order],
            r_ss,
            r_rs,
            to,
        ).start()
    for k in range(3):
        lam[0, k] = const[k] + inverse_ref[0, 0, k] * total_r[...]
    out_early.start()
    part = r_s[index // together]
    r_all = remote(r_r.at[1:], r_r.at[1:], r_ss, r_rs, peer(1))
    r_all.wait_recv()
    for order in range(1, devices):
        part = part + r_r[order]
    mine = jnp.full((2, PARAM_REGIONS), lax.rem(index, together), jnp.int32)
    result = jnp.zeros((2, PARAM_REGIONS), f32)
    for n in range(together):
        result = jnp.where(
            mine == n, part[:, n * PARAM_REGIONS : (n + 1) * PARAM_REGIONS], result
        )
    region_ref[...] = result
    r_all.wait_send()
    out_late.wait()
    out_early.wait()


def local(*arrays):
    (
        pressure,
        saturation,
        permeability,
        porosity,
        upwind_flags,
        diag_inverse,
        seismic_obs,
        well_x,
        well_y,
        well_top,
        well_len,
        well_bhp,
        well_obs,
        fault_cell,
        fault_count,
        fault_trans,
        fault_up,
        region_map,
    ) = arrays
    counts = tuple(lax.axis_size(axis) for axis in ("gx", "gy", "gz"))
    nx, ny, nz = permeability.shape
    peers, slots = fault_cell.shape[1:]
    devices = counts[0] * peers
    hbm = pl.BlockSpec(memory_space=pltpu.HBM)
    vmem = pl.BlockSpec(memory_space=pltpu.VMEM)
    f32 = jnp.float32
    bf16 = jnp.bfloat16
    dma = pltpu.SemaphoreType.DMA

    def field(*lead, dtype=f32):
        return pltpu.VMEM(lead + (nx, ny, nz), dtype)

    def per_fault(*lead, dtype=f32):
        return pltpu.VMEM(lead + (peers, slots), dtype)

    bundles = [(2, 2, 5, ny, nz), (2, 2, 5, nx, 1, nz), (2, 2, 5, ny, nz)]
    faces = [(2, ny, nz), (2, nx, 1, nz), (2, ny, nz)]
    large = arrays[:7]
    scratch = [
        *[pltpu.VMEM(array.shape, array.dtype) for array in large],
        dma((len(large),)),
        dma((2,)),
        field(2, 3),
        field(2, 3, 3),
        field(2, 3, 3),
        field(2, 3),
        field(),
        field(2, 3),
        field(3),
        field(1),
        field(3),
        field(3),
        field(2, 2, 3),
        field(2, 3),
        field(2, 3),
        field(2, 3),
        field(2, 3),
        field(2),
        field(),
        field(),
        pltpu.VMEM((nx * ny, peers * slots), bf16),
        pltpu.VMEM((peers * slots, nz), bf16),
        pltpu.VMEM((devices * PARAM_REGIONS, 3 * region_map.size), bf16),
        per_fault(dtype=jnp.int32),
        per_fault(),
        per_fault(dtype=jnp.int32),
        per_fault(),
        per_fault(6),
        per_fault(2, 3),
        per_fault(4),
        *[pltpu.VMEM(s, f32) for s in bundles],
        *[pltpu.VMEM(s, f32) for s in bundles],
        dma((2, 3, 2)),
        dma((2, 3, 2)),
        pltpu.VMEM((6,) + region_map.shape, jnp.int32),
        dma((3, 2)),
        dma((3, 2)),
        per_fault(6),
        per_fault(6),
        dma,
        dma,
        pltpu.VMEM((8, LANES), f32),
        pltpu.VMEM((counts[2], 8, LANES), f32),
        dma((counts[2],)),
        dma((counts[2],)),
        *[pltpu.VMEM(s, f32) for s in faces],
        *[pltpu.VMEM((2,) + s, f32) for s in faces],
        dma((3, 2)),
        dma((2, 3, 2)),
        per_fault(3),
        per_fault(3),
        dma,
        dma((len(CUTS) - 1,)),
        per_fault(2),
        per_fault(2),
        dma((2,)),
        dma((2, len(CUTS) - 1)),
        pltpu.VMEM((devices * PARAM_REGIONS // LANES, 2, LANES), f32),
        pltpu.VMEM((devices, 2, LANES), f32),
        dma,
        dma,
    ]
    results = (
        jax.ShapeDtypeStruct((2, 3, nx, ny, nz), f32),
        jax.ShapeDtypeStruct((2, PARAM_REGIONS), f32),
    )
    found = pl.pallas_call(
        functools.partial(kernel, counts),
        out_shape=results,
        in_specs=[hbm] * 7 + [vmem] * 11,
        out_specs=(hbm, vmem),
        scratch_shapes=scratch,
        compiler_params=pltpu.CompilerParams(
            collective_id=0, has_side_effects=True, vmem_limit_bytes=60 * 2**20
        ),
    )(*arrays)

    def finish(lam_ref, region_ref, lam_out, region_out, sem):
        copy = pltpu.make_async_copy(lam_ref, lam_out, sem)
        copy.start()
        region_out[...] = region_ref[...]
        copy.wait()

    return pl.pallas_call(
        finish,
        out_shape=results,
        in_specs=[vmem, vmem],
        out_specs=(hbm, vmem),
        scratch_shapes=[dma],
    )(*found)


def solution(mesh):
    cells = P("gx", "gy", "gz")
    column = P("gx", "gy", None)
    every = ("gx", "gy", "gz")
    placed = (
        P(None, "gx", "gy", "gz"),
        P(None, None, "gx", "gy", "gz"),
        cells,
        cells,
        cells,
        P(None, None, None, "gx", "gy", "gz"),
        cells,
        column,
        column,
        column,
        column,
        P(None, "gx", "gy", None),
        P(None, "gx", "gy", None),
        P(every, None, None),
        P(every, None),
        P(every, None, None),
        P(every, None, None),
        cells,
    )
    return jax.shard_map(
        local,
        mesh=mesh,
        in_specs=placed,
        out_specs=(P(None, None, "gx", "gy", "gz"), P(None, every)),
        check_vma=False,
    )
```

```python
import functools

import jax
import jax.numpy as jnp
from jax import lax
from jax.experimental import pallas as pl
from jax.experimental.pallas import tpu as pltpu
from jax.sharding import PartitionSpec as P

ITERS = 6
BOX = 4
PARAM_REGIONS = 32
LANES = 128
CUTS = (1, 8, 12, 16)
MESH = pl.DeviceIdType.MESH

fluid_viscosity = (0.4, 0.5, 1.0)
sigma_sq = 64.0
SIDES = tuple((dim, side) for dim in range(3) for side in range(2))


def phase_mobility(water_sat, oil_sat):
    gas_sat = 1.0 - water_sat - oil_sat
    return [
        water_sat * water_sat / fluid_viscosity[0],
        oil_sat * oil_sat / fluid_viscosity[1],
        gas_sat * gas_sat / fluid_viscosity[2],
    ]


def mobility_slopes(water_sat, oil_sat):
    gas_sat = 1.0 - water_sat - oil_sat
    return (
        2.0 * water_sat / fluid_viscosity[0] - 2.0 * gas_sat / fluid_viscosity[2],
        2.0 * oil_sat / fluid_viscosity[1] - 2.0 * gas_sat / fluid_viscosity[2],
    )


def split(value, parts):
    pieces = []
    for _ in range(parts):
        piece = value.astype(jnp.bfloat16)
        pieces.append(piece)
        value = value - piece.astype(jnp.float32)
    return pieces


def kernel(
    counts,
    pressure_hbm,
    saturation_hbm,
    perm_hbm,
    porosity_hbm,
    flags_hbm,
    inverse_hbm,
    seismic_hbm,
    well_x_ref,
    well_y_ref,
    well_top_ref,
    well_len_ref,
    bhp_ref,
    obs_ref,
    fault_cell_ref,
    fault_count_ref,
    fault_trans_ref,
    fault_up_ref,
    map_ref,
    lam_hbm,
    region_ref,
    pressure_ref,
    sat_ref,
    perm_ref,
    porosity_ref,
    flags_ref,
    inverse_ref,
    seismic_ref,
    in_sem,
    out_sem,
    mob,
    wp,
    wm,
    src,
    explicit,
    lam,
    const,
    turn_c,
    turn_d,
    push,
    push_turn_c,
    push_turn_d,
    flux_base,
    flux_lead,
    por,
    total_r,
    delta,
    row_hot,
    z_hot,
    found_hot,
    f_cell,
    f_scale,
    f_up,
    f_tmp,
    f_coef,
    f_send,
    bx_s,
    by_s,
    bz_s,
    bx_r,
    by_r,
    bz_r,
    b_ss,
    b_rs,
    map_r,
    map_ss,
    map_rs,
    m_s,
    m_r,
    m_ss,
    m_rs,
    w_s,
    w_r,
    w_ss,
    w_rs,
    x_s,
    y_s,
    z_s,
    x_r,
    y_r,
    z_r,
    h_ss,
    h_rs,
    v_s,
    v_r,
    v_ss,
    v_rs,
    c_s,
    c_r,
    c_ss,
    c_rs,
    r_s,
    r_r,
    r_ss,
    r_rs,
):
    n_gx, n_gy, n_gz = counts
    here = (lax.axis_index("gx"), lax.axis_index("gy"), lax.axis_index("gz"))
    peers = n_gy * n_gz
    devices = n_gx * peers
    me = here[1] * n_gz + here[2]
    index = here[0] * peers + me
    shape = perm_ref.shape
    nx, ny, nz = shape
    rows = nx * ny
    slots = c_r.shape[2]
    f32 = jnp.float32

    def flip(number, bits):
        bit = 1
        while bit <= bits:
            if bits & bit:
                number = number + bit - 2 * bit * lax.rem(number // bit, 2)
            bit *= 2
        return number

    def peer(order):
        return (here[0], flip(here[1], order // n_gz), flip(here[2], order % n_gz))

    def peer_place(order):
        other = peer(order)
        return other[1] * n_gz + other[2]

    def toward(dim, step):
        moved = list(here)
        moved[dim] = lax.rem(here[dim] + step + counts[dim], counts[dim])
        return tuple(moved)

    def device(number):
        return (number // peers, lax.rem(number, peers) // n_gz, lax.rem(number, n_gz))

    def remote(source, target, send, recv, to):
        return pltpu.make_async_remote_copy(
            src_ref=source,
            dst_ref=target,
            send_sem=send,
            recv_sem=recv,
            device_id=to,
            device_id_type=MESH,
        )

    has_next = [here[dim] < counts[dim] - 1 for dim in range(3)]
    has_last = [here[dim] > 0 for dim in range(3)]

    def sends(dim, side):
        return has_next[dim] if side == 0 else has_last[dim]

    def receives(dim, side):
        return has_last[dim] if side == 0 else has_next[dim]

    loads = [
        pltpu.make_async_copy(source, target, in_sem.at[n])
        for n, (source, target) in enumerate(
            (
                (saturation_hbm, sat_ref),
                (perm_hbm, perm_ref),
                (pressure_hbm, pressure_ref),
                (flags_hbm, flags_ref),
                (seismic_hbm, seismic_ref),
                (inverse_hbm, inverse_ref),
                (porosity_hbm, porosity_ref),
            )
        )
    ]
    for load in loads:
        load.start()
    for ref in (bx_r, by_r, bz_r, x_r, y_r, z_r, m_r, v_r, c_r, map_r):
        ref[...] = jnp.zeros_like(ref)

    barrier = pltpu.get_barrier_semaphore()
    for offset in range(1, devices):
        pl.semaphore_signal(
            barrier,
            inc=1,
            device_id=device(lax.rem(index + offset, devices)),
            device_id_type=MESH,
        )

    yi = lax.broadcasted_iota(jnp.int32, shape, 1)
    zi = lax.broadcasted_iota(jnp.int32, shape, 2)
    iotas = (None, yi, zi)
    diagonal = lax.broadcasted_iota(jnp.int32, shape, 0) == zi

    def pack(field, lane):
        return jnp.sum(jnp.where(diagonal, field[:, :, lane : lane + 1], 0.0), axis=0)

    def unpack(tile):
        return jnp.concatenate(
            [jnp.broadcast_to(tile[:, x : x + 1], (ny, nz))[None] for x in range(nx)], axis=0
        )

    def at_next(field, dim, edge):
        if dim == 0:
            return jnp.concatenate([field[1:], edge], axis=0)
        last = shape[dim] - 1
        return jnp.where(iotas[dim] == last, edge, pltpu.roll(field, last, dim))

    def at_last(field, dim, edge):
        if dim == 0:
            return jnp.concatenate([edge, field[:-1]], axis=0)
        return jnp.where(iotas[dim] == 0, edge, pltpu.roll(field, 1, dim))

    def edge_of(dim, halo):
        if dim == 0:
            return halo[None]
        return halo if dim == 1 else unpack(halo)

    def no_edge(dim):
        return jnp.zeros((1, ny, nz), f32) if dim == 0 else 0.0

    def faults_in_order(array, target):
        for order in range(peers):
            target[order : order + 1, :] = array[pl.ds(peer_place(order), 1), :]

    faults_in_order(fault_cell_ref.at[0], f_cell)
    faults_in_order(fault_up_ref.at[0], f_up)
    slot_index = lax.broadcasted_iota(jnp.int32, (1, slots), 1)
    for p in range(peers):
        f_tmp[p : p + 1, :] = jnp.where(
            slot_index < fault_count_ref[:, p : p + 1], fault_trans_ref[0, p : p + 1, :], 0.0
        )
    faults_in_order(f_tmp, f_scale)
    f_row = f_cell[...] // nz
    f_z = f_cell[...] - f_row * nz

    def gather_half(ref, low, high):
        row, at = f_row[low:high], f_z[low:high]

        def body(x, chosen):
            for y in range(ny):
                taken = jnp.take_along_axis(
                    jnp.broadcast_to(ref[x, y : y + 1, :], (high - low, nz)),
                    at,
                    axis=1,
                    mode="promise_in_bounds",
                )
                chosen = jnp.where(row == x * ny + y, taken, chosen)
            return chosen

        return lax.fori_loop(0, nx, body, jnp.zeros((high - low, slots), f32), unroll=True)

    def gather(refs):
        def body(x, chosen):
            for y in range(ny):
                here_row = f_row == x * ny + y
                chosen = [
                    jnp.where(
                        here_row,
                        jnp.take_along_axis(
                            jnp.broadcast_to(ref[x, y : y + 1, :], (peers, nz)),
                            f_z,
                            axis=1,
                            mode="promise_in_bounds",
                        ),
                        value,
                    )
                    for ref, value in zip(refs, chosen)
                ]
            return chosen

        start = [jnp.zeros((peers, slots), f32) for _ in refs]
        return lax.fori_loop(0, nx, body, start, unroll=True)

    loads[0].wait()
    mobility = [phase_mobility(sat_ref[t + 1, 0], sat_ref[t + 1, 1]) for t in range(2)]
    for t in range(2):
        for k in range(3):
            mob[t, k] = mobility[t][k]
    for load in loads[1:4]:
        load.wait()
    perm = perm_ref[...]

    def bundle(part, fields):
        for q, field in enumerate(fields):
            bx_s[part, 0, q] = field[nx - 1]
            bx_s[part, 1, q] = field[0]
            by_s[part, 0, q] = field[:, ny - 1 :, :]
            by_s[part, 1, q] = field[:, :1, :]
            bz_s[part, 0, q] = pack(field, nz - 1)
            bz_s[part, 1, q] = pack(field, 0)

    def bundle_copy(part, dim, side):
        sent, got = ((bx_s, bx_r), (by_s, by_r), (bz_s, bz_r))[dim]
        return remote(
            sent.at[part, side],
            got.at[part, side],
            b_ss.at[part, dim, side],
            b_rs.at[part, dim, side],
            toward(dim, 1 - 2 * side),
        )

    def map_copy(dim, side):
        return remote(
            map_ref,
            map_r.at[2 * dim + side],
            map_ss.at[dim, side],
            map_rs.at[dim, side],
            toward(dim, 1 - 2 * side),
        )

    def start_faces(copies):
        for dim, side in SIDES:

            @pl.when(sends(dim, side))
            def _():
                for copy in copies:
                    copy(dim, side).start()

    def wait_faces(copies):
        for dim, side in SIDES:

            @pl.when(sends(dim, side))
            def _():
                for copy in copies:
                    copy(dim, side).wait_send()

            @pl.when(receives(dim, side))
            def _():
                for copy in copies:
                    copy(dim, side).wait_recv()

    bundle(0, [perm] + mobility[1] + [flags_ref[...].astype(f32)])

    n_wells = well_top_ref.shape[2]
    eye = lax.broadcasted_iota(jnp.int32, (n_wells, n_wells), 0) == lax.broadcasted_iota(
        jnp.int32, (n_wells, n_wells), 1
    )

    def as_column(row):
        return jnp.sum(jnp.where(eye, row.astype(f32), 0.0), axis=1, keepdims=True)

    def as_row(column):
        return jnp.sum(jnp.where(eye, column, 0.0), axis=0, keepdims=True)

    well_row = well_x_ref[0] * ny + well_y_ref[0]
    well_hot = (
        (
            lax.broadcasted_iota(jnp.int32, (n_wells, rows), 1).astype(f32) == as_column(well_row)
        )
        .astype(f32)
        .astype(jnp.bfloat16)
    )
    well_hot_t = (lax.broadcasted_iota(jnp.int32, (rows, n_wells), 0) == well_row).astype(f32)
    depth = (here[2] * nz + lax.broadcasted_iota(jnp.int32, (n_wells, nz), 1)).astype(f32)
    top = as_column(well_top_ref[0])
    bottom = as_column(well_top_ref[0] + well_len_ref[0])
    perforated = jnp.where((depth >= top) & (depth < bottom), 1.0, 0.0)

    def total(t):
        return perm_ref[...] * (mob[t, 0] + mob[t, 1] + mob[t, 2])

    fields = []
    for t in range(2):
        whole = total(t)
        fields += [
            (whole * pressure_ref[t]).reshape(rows, nz),
            whole.reshape(rows, nz),
        ]
    pieces = jnp.concatenate(split(jnp.concatenate(fields, axis=1), 3), axis=0)
    of_wells = jnp.dot(
        jnp.concatenate([well_hot] * 3, axis=1), pieces, preferred_element_type=f32
    )
    w_s[...] = jnp.zeros_like(w_s)
    for t in range(2):
        bhp = as_column(bhp_ref[t, 0])
        rate = jnp.sum(
            perforated
            * (
                of_wells[:, 2 * t * nz : (2 * t + 1) * nz]
                - bhp * of_wells[:, (2 * t + 1) * nz : (2 * t + 2) * nz]
            ),
            axis=1,
            keepdims=True,
        )
        w_s[t : t + 1, :n_wells] = as_row(rate)

    pl.semaphore_wait(barrier, devices - 1)
    w_copies = []
    for offset in range(1, n_gz):
        copy = remote(
            w_s,
            w_r.at[offset],
            w_ss.at[offset],
            w_rs.at[offset],
            (here[0], here[1], lax.rem(here[2] + offset, n_gz)),
        )
        copy.start()
        w_copies.append(copy)
    start_faces([functools.partial(bundle_copy, 0)])

    def order_far_first():
        return range(peers - 1, 0, -1)

    groups = list(zip(CUTS[:-1], CUTS[1:]))

    def group(order):
        return [low <= order < high for low, high in groups].index(True)

    def mobility_copy(t, low, high, to):
        return remote(
            m_s.at[t, :, low:high], m_r.at[t, :, low:high], m_ss.at[t], m_rs.at[t], to
        )

    def send_mobility(t):
        own = gather([mob.at[t, k] for k in range(3)])
        for k in range(3):
            m_s[t, k] = own[k]
        for order in order_far_first():
            mobility_copy(t, order, order + 1, peer(order)).start()

    def fault_coefficients(t):
        mobility_copy(t, 1, peers, peer(1)).wait()
        own_up = jnp.bitwise_and(jnp.right_shift(f_up[...], t), 1) == 1
        for k in range(3):
            f_coef[t, k] = f_scale[...] * jnp.where(own_up, m_s[t, k], m_r[t, k])

    send_mobility(1)

    for order in range(peers):
        lanes = slice(order * slots, (order + 1) * slots)
        row_hot[:, lanes] = (
            (lax.broadcasted_iota(jnp.int32, (rows, slots), 0) == f_row[order : order + 1])
            .astype(f32)
            .astype(jnp.bfloat16)
        )
        z_hot[lanes, :] = (
            (lax.broadcasted_iota(jnp.int32, (nz, slots), 0) == f_z[order : order + 1])
            .astype(f32)
            .T.astype(jnp.bfloat16)
        )

    def scatter(read, start, stop):
        base = start // 4 * 4
        parts = split(read(base, stop), 2)
        marked = [[], []]
        for order in range(start, stop):
            hot = row_hot[:, order * slots : (order + 1) * slots]
            at = order - base
            for pieces, part in zip(marked, parts):
                pieces.append(hot * jnp.broadcast_to(part[at : at + 1], hot.shape))
        added = lax.dot_general(
            jnp.concatenate([jnp.concatenate(pieces, axis=1) for pieces in marked], axis=0),
            z_hot[start * slots : stop * slots, :],
            (((1,), (0,)), ((), ())),
            preferred_element_type=f32,
        )
        return (added[:rows] + added[rows:]).reshape(shape)

    for load in loads[4:]:
        load.wait()
    for copy in w_copies:
        copy.wait()
    rates = w_s[...]
    for offset in range(1, n_gz):
        rates = rates + w_r[offset]

    def sources(t):
        misfit = (rates[t : t + 1, :n_wells] - obs_ref[t, 0]) / sigma_sq
        weighted = well_hot_t * misfit
        both = jnp.concatenate([weighted, weighted * bhp_ref[t, 0]], axis=0)
        spread = jnp.dot(
            jnp.concatenate(split(both, 3), axis=0),
            perforated.astype(jnp.bfloat16),
            preferred_element_type=f32,
        )
        spread = spread[: 2 * rows] + spread[2 * rows : 4 * rows] + spread[4 * rows :]
        drawn = pressure_ref[t] * spread[:rows].reshape(shape) - spread[rows:].reshape(shape)
        water_slope, oil_slope = mobility_slopes(sat_ref[t + 1, 0], sat_ref[t + 1, 1])
        whole = total(t)
        src[t, 0] = whole * spread[:rows].reshape(shape)
        water_source = perm_ref[...] * drawn * water_slope
        if t == 1:
            water_source = water_source + (sat_ref[2, 0] - seismic_ref[...])
        src[t, 1] = water_source
        src[t, 2] = perm_ref[...] * drawn * oil_slope
        return whole * drawn

    def face_coefficients(t, flags, mob_from):
        own_flags = flags.astype(jnp.int32)
        for dim in range(3):
            got = (bx_r, by_r, bz_r)[dim]

            def halo(part, side, q):
                return edge_of(dim, got[part, side, q])

            up_face = jnp.sqrt(
                perm_ref[...] * at_next(perm_ref[...], dim, halo(0, 1, 0))
            )
            low_face = jnp.sqrt(
                perm_ref[...] * at_last(perm_ref[...], dim, halo(0, 0, 0))
            )
            up_ok = has_next[dim].astype(f32)
            low_ok = has_last[dim].astype(f32)
            if dim == 0:
                up_face = jnp.concatenate([up_face[:-1], up_face[-1:] * up_ok], axis=0)
                low_face = jnp.concatenate([low_face[:1] * low_ok, low_face[1:]], axis=0)
            else:
                up_face = up_face * jnp.where(iotas[dim] == shape[dim] - 1, up_ok, 1.0)
                low_face = low_face * jnp.where(iotas[dim] == 0, low_ok, 1.0)
            bit = 3 * t + dim
            low_flags = at_last(flags, dim, halo(0, 0, 4)).astype(jnp.int32)
            own_up = jnp.bitwise_and(jnp.right_shift(own_flags, bit), 1) == 1
            low_up = jnp.bitwise_and(jnp.right_shift(low_flags, bit), 1) == 1
            for k in range(3):
                part, q = mob_from(k)
                m = mob[t, k]
                wp[t, dim, k] = up_face * jnp.where(
                    own_up, m, at_next(m, dim, halo(part, 1, q))
                )
                wm[t, dim, k] = low_face * jnp.where(
                    low_up, at_last(m, dim, halo(part, 0, q)), m
                )

    def face_copy(parity, dim, side):
        sent, got = ((x_s, x_r), (y_s, y_r), (z_s, z_r))[dim]
        return remote(
            sent.at[side],
            got.at[parity, side],
            h_ss.at[dim, side],
            h_rs.at[parity, dim, side],
            toward(dim, 1 - 2 * side),
        )

    def send_faces(parity, up, down):
        x_s[0] = up[0][nx - 1]
        x_s[1] = down[0][0]
        y_s[0] = up[1][:, ny - 1 :, :]
        y_s[1] = down[1][:, :1, :]
        z_s[0] = pack(up[2], nz - 1)
        z_s[1] = pack(down[2], 0)
        start_faces([functools.partial(face_copy, parity)])
        inner = at_last(up[0], 0, no_edge(0)) + at_next(down[0], 0, no_edge(0))
        for dim in (1, 2):
            inner = inner + at_last(up[dim], dim, 0.0) + at_next(down[dim], dim, 0.0)
        return inner

    def add_faces(parity, inner):
        wait_faces([functools.partial(face_copy, parity)])
        inner = jnp.concatenate(
            [
                inner[:1] + x_r[parity, 0][None],
                inner[1 : nx - 1],
                inner[nx - 1 :] + x_r[parity, 1][None],
            ],
            axis=0,
        )
        inner = inner + jnp.where(
            yi == 0, y_r[parity, 0], jnp.where(yi == ny - 1, y_r[parity, 1], 0.0)
        )
        return inner + jnp.where(
            zi == 0,
            unpack(z_r[parity, 0]),
            jnp.where(zi == nz - 1, unpack(z_r[parity, 1]), 0.0),
        )

    def fault_copy(parity, low, high, order, to):
        return remote(
            c_s.at[parity, low:high],
            c_r.at[parity, low:high],
            c_ss.at[parity],
            c_rs.at[parity, group(low)],
            to,
        )

    def send_faults(parity, ref, lead, fixed):
        for low in range(peers - 8, -8, -8):
            part = slice(low, low + 8)
            values = f_send[lead, part] * gather_half(ref, low, low + 8)
            if fixed is not None:
                values = values + f_send[fixed, part]
            c_s[parity, part] = values
            for order in range(low + 7, max(low, 1) - 1, -1):
                fault_copy(parity, order, order + 1, order, peer(order)).start()

    def add_faults(parity, inner):
        def read(low, high):
            return c_r[parity, low:high]

        for low, high in groups:
            fault_copy(parity, low, high, low, peer(low)).wait_recv()
            inner = inner + scatter(read, low, high)
        fault_copy(parity, 1, peers, 1, peer(1)).wait_send()
        return inner

    def scalar_round(parity, t, aside):
        send_faults(parity, delta, t, None)
        now = delta[...]
        inner = send_faces(
            parity,
            [push[t, 0, dim] * now for dim in range(3)],
            [push[t, 1, dim] * now for dim in range(3)],
        )
        if aside is not None:
            aside()
        inner = add_faces(parity, inner)
        inner = add_faults(parity, inner)
        delta[...] = inner
        total_r[...] += inner

    def dot3(coefficients, values):
        return sum(coefficients(k) * values(k) for k in range(3))

    def scalar_push(t):
        for dim in range(3):
            push[t, 0, dim] = dot3(lambda k: wp[t, dim, k], lambda k: inverse_ref[t, 0, k])
            push[t, 1, dim] = dot3(lambda k: wm[t, dim, k], lambda k: inverse_ref[t, 0, k])

    def scalar_faults(t):
        values = gather([inverse_ref.at[t, 0, k] for k in range(3)])
        f_send[t] = dot3(lambda k: f_coef[t, k], lambda k: values[k])

    explicit[...] = sources(1)
    total_r[...] = src[1, 0]
    for k in range(3):
        const[k] = inverse_ref[1, 1, k] * src[1, 1] + inverse_ref[1, 2, k] * src[1, 2]
        lam[1, k] = const[k] + inverse_ref[1, 0, k] * src[1, 0]
    values = gather([lam.at[1, k] for k in range(3)])
    for k in range(3):
        v_s[k] = values[k]

    def vector_copy(low, high, to):
        return remote(
            v_s.at[:, low:high],
            v_r.at[:, low:high],
            v_ss,
            v_rs.at[group(low)],
            to,
        )

    for order in order_far_first():
        vector_copy(order, order + 1, peer(order)).start()
    wait_faces([functools.partial(bundle_copy, 0)])
    flags = flags_ref[...].astype(f32)
    face_coefficients(1, flags, lambda k: (0, 1 + k))
    inner = send_faces(
        0,
        [dot3(lambda k: wp[1, dim, k], lambda k: lam[1, k]) for dim in range(3)],
        [dot3(lambda k: wm[1, dim, k], lambda k: lam[1, k]) for dim in range(3)],
    )
    bundle(1, [mob[0, k] for k in range(3)] + [pressure_ref[t] for t in range(2)])
    start_faces([functools.partial(bundle_copy, 1), map_copy])
    scalar_push(1)
    send_mobility(0)
    fault_coefficients(1)
    scalar_faults(1)
    inner = add_faces(0, inner)

    def arrived(low, high):
        return dot3(lambda k: f_coef[1, k, low:high], lambda k: v_r[k, low:high])

    for low, high in groups:
        vector_copy(low, high, peer(low)).wait_recv()
        inner = inner + scatter(arrived, low, high)
    vector_copy(1, peers, peer(1)).wait_send()
    delta[...] = inner
    total_r[...] += inner

    def prepare_turn():
        explicit[...] += sources(0)
        wait_faces([functools.partial(bundle_copy, 1), map_copy])
        face_coefficients(0, flags_ref[...].astype(f32), lambda k: (1, k))
        porosity = porosity_ref[...]
        first = src[0, 1] + porosity * (const[0] - const[2])
        second = src[0, 2] + porosity * (const[1] - const[2])
        d_first = porosity * (inverse_ref[1, 0, 0] - inverse_ref[1, 0, 2])
        d_second = porosity * (inverse_ref[1, 0, 1] - inverse_ref[1, 0, 2])
        for k in range(3):
            turn_c[k] = (
                inverse_ref[0, 0, k] * src[0, 0]
                + inverse_ref[0, 1, k] * first
                + inverse_ref[0, 2, k] * second
            )
            turn_d[k] = inverse_ref[0, 1, k] * d_first + inverse_ref[0, 2, k] * d_second

    def prepare_sends():
        fault_coefficients(0)
        for side, w in enumerate((wp, wm)):
            for dim in range(3):
                push_turn_c[side, dim] = dot3(lambda k: w[0, dim, k], lambda k: turn_c[k])
                push_turn_d[side, dim] = dot3(lambda k: w[0, dim, k], lambda k: turn_d[k])
        values = gather([ref.at[k] for ref in (turn_c, turn_d) for k in range(3)])
        f_send[2] = dot3(lambda k: f_coef[0, k], lambda k: values[k])
        f_send[3] = dot3(lambda k: f_coef[0, k], lambda k: values[3 + k])

    n_rounds = ITERS - 1
    scalar_round(1, 1, prepare_turn)
    scalar_round(0, 1, prepare_sends)

    def more(t):
        def body(step, carry):
            scalar_round(lax.rem(step, 2), t, None)
            return carry

        return body

    lax.fori_loop(3, n_rounds, more(1), 0)

    out_late = pltpu.make_async_copy(lam.at[1], lam_hbm.at[1], out_sem.at[1])
    out_early = pltpu.make_async_copy(lam.at[0], lam_hbm.at[0], out_sem.at[0])
    parity = n_rounds % 2
    send_faults(parity, total_r, 3, 2)
    now = total_r[...]
    inner = send_faces(
        parity,
        [push_turn_c[0, dim] + push_turn_d[0, dim] * now for dim in range(3)],
        [push_turn_c[1, dim] + push_turn_d[1, dim] * now for dim in range(3)],
    )
    for k in range(3):
        lam[1, k] = const[k] + inverse_ref[1, 0, k] * total_r[...]
    out_late.start()
    porosity = porosity_ref[...]
    first = src[0, 1] + porosity * (lam[1, 0] - lam[1, 2])
    second = src[0, 2] + porosity * (lam[1, 1] - lam[1, 2])
    for k in range(3):
        const[k] = inverse_ref[0, 1, k] * first + inverse_ref[0, 2, k] * second
    scalar_push(0)
    scalar_faults(0)
    inner = add_faces(parity, inner)
    inner = add_faults(parity, inner)
    delta[...] = inner
    total_r[...] = src[0, 0] + inner

    n_bx, n_by, n_bz = nx // BOX, ny // BOX, nz // BOX
    n_boxes = n_bx * n_by
    wide = n_boxes * n_bz

    def prepare_gradient():
        for dim in range(3):
            got = (bx_r, by_r, bz_r)[dim]
            flux_base[0, dim] = jnp.zeros(shape, f32)
            flux_base[1, dim] = jnp.zeros(shape, f32)
            for t in range(2):
                p_here = pressure_ref[t]
                up_p = 0.5 * (
                    p_here - at_next(p_here, dim, edge_of(dim, got[1, 1, 3 + t]))
                )
                down_p = -0.5 * (
                    at_last(p_here, dim, edge_of(dim, got[1, 0, 3 + t])) - p_here
                )
                source = (lambda k: const[k]) if t == 0 else (lambda k: lam[1, k])
                flux_base[0, dim] += up_p * dot3(lambda k: wp[t, dim, k], source)
                flux_base[1, dim] += down_p * dot3(lambda k: wm[t, dim, k], source)
                if t == 0:
                    flux_lead[0, dim] = up_p * push[0, 0, dim]
                    flux_lead[1, dim] = down_p * push[0, 1, dim]
        steps = []
        for t in range(2):
            water = sat_ref[t + 1, 0] - sat_ref[t, 0]
            oil = sat_ref[t + 1, 1] - sat_ref[t, 1]
            steps.append((water, oil, water + oil))
        por[0] = -(
            lam[1, 0] * steps[1][0]
            + lam[1, 1] * steps[1][1]
            - lam[1, 2] * steps[1][2]
            + const[0] * steps[0][0]
            + const[1] * steps[0][1]
            - const[2] * steps[0][2]
        )
        por[1] = -(
            inverse_ref[0, 0, 0] * steps[0][0]
            + inverse_ref[0, 0, 1] * steps[0][1]
            - inverse_ref[0, 0, 2] * steps[0][2]
        )
        z_lane = lax.broadcasted_iota(jnp.int32, (1, n_bz), 1)

        def own_map(bx, by):
            return map_ref[bx, by : by + 1, :]

        def other_map(dim, side, bx, by):
            return map_r[2 * dim + side, bx, by : by + 1, :]

        labels = [[], [], []]
        for bx in range(n_bx):
            for by in range(n_by):
                labels[0].append(own_map(bx, by))
                labels[1].append(
                    other_map(1, 0, bx, n_by - 1) if by == 0 else other_map(1, 1, bx, 0)
                )
                if bx == 0:
                    label = other_map(0, 0, n_bx - 1, by)
                elif bx == n_bx - 1:
                    label = other_map(0, 1, 0, by)
                else:
                    even, odd = 2 * (bx - 1), 2 * (bx - 1) + 1
                    label = jnp.zeros((1, n_bz), jnp.int32)
                    for lane, side, box in (
                        (0, 0, even),
                        (1, 0, odd),
                        (n_bz - 2, 1, odd),
                        (n_bz - 1, 1, even),
                    ):
                        edge = n_bz - 1 if side == 0 else 0
                        label = jnp.where(
                            z_lane == lane,
                            other_map(2, side, box, by)[:, edge : edge + 1],
                            label,
                        )
                labels[2].append(label)
        n_regions = devices * PARAM_REGIONS
        region = lax.broadcasted_iota(jnp.int32, (LANES, n_regions), 1).astype(f32)
        for part in range(3):
            label = jnp.concatenate(labels[part], axis=1).astype(f32)
            for first in range(0, wide, LANES):
                column = jnp.broadcast_to(label[:, first : first + LANES], (LANES, LANES)).T
                found_hot[part * wide + first : part * wide + first + LANES, :] = (
                    (region == jnp.concatenate([column] * (n_regions // LANES), axis=1))
                    .astype(f32)
                    .astype(jnp.bfloat16)
                )

    parity = (n_rounds + 1) % 2
    scalar_round(parity, 0, prepare_gradient)
    lax.fori_loop(n_rounds + 2, 2 * n_rounds, more(0), 0)

    now = total_r[...]
    flux = [
        [flux_base[side, dim] + flux_lead[side, dim] * now for dim in range(3)]
        for side in range(2)
    ]
    gradient = explicit[...]
    for dim in range(3):
        gradient = gradient - (
            flux[0][dim]
            + flux[1][dim]
            + at_last(flux[0][dim], dim, no_edge(dim))
            + at_next(flux[1][dim], dim, no_edge(dim))
        )

    def x_sums(field):
        return jnp.sum(field.reshape(n_bx, BOX, ny, nz), axis=1)

    y_pushed = x_sums(jnp.where(yi == 0, flux[1][1], 0.0) + jnp.where(yi == ny - 1, flux[0][1], 0.0))
    z_pushed = x_sums(jnp.where(zi == 0, flux[1][2], 0.0) + jnp.where(zi == nz - 1, flux[0][2], 0.0))
    lane = lax.broadcasted_iota(jnp.int32, (ny, nz), 1)

    def moved(tile):
        return jnp.where(
            lane == BOX,
            pltpu.roll(tile, BOX, 1),
            jnp.where(lane == nz - 1 - BOX, pltpu.roll(tile, nz - BOX, 1), 0.0),
        )

    mixed = jnp.concatenate(
        [flux[1][0][0][None]]
        + [(z_pushed[2 * n] + moved(z_pushed[2 * n + 1]))[None] for n in range(n_bx // 2)]
        + [flux[0][0][nx - 1][None]],
        axis=0,
    )
    stacked = jnp.concatenate(
        [x_sums(gradient), x_sums(por[0] + por[1] * now), -y_pushed, -mixed], axis=0
    ).reshape(4 * n_bx * ny, nz)
    z_boxes = (
        (
            lax.broadcasted_iota(jnp.int32, (nz, wide), 0) // BOX
            == lax.rem(lax.broadcasted_iota(jnp.int32, (nz, wide), 1), n_bz)
        )
        .astype(f32)
        .astype(jnp.bfloat16)
    )
    boxed = jnp.dot(
        jnp.concatenate(split(stacked, 2), axis=1),
        jnp.concatenate([z_boxes] * 2, axis=0),
        preferred_element_type=f32,
    )
    in_box = (
        lax.broadcasted_iota(jnp.int32, (n_bx * ny, wide), 1) // n_bz
        == lax.broadcasted_iota(jnp.int32, (n_bx * ny, wide), 0) // BOX
    )
    sums = [
        jnp.sum(
            jnp.where(in_box, boxed[n * n_bx * ny : (n + 1) * n_bx * ny], 0.0),
            axis=0,
            keepdims=True,
        )
        for n in range(4)
    ]
    none = jnp.zeros((1, wide), f32)
    perm_row = jnp.concatenate([sums[0], sums[2], sums[3]], axis=1)
    por_row = jnp.concatenate([sums[1], none, none], axis=1)
    parts = [
        part.astype(f32) for row in (perm_row, por_row) for part in split(row, 2)
    ]
    which = lax.broadcasted_iota(jnp.int32, (8, 3 * wide), 0)
    lines = jnp.zeros((8, 3 * wide), f32)
    for n, part in enumerate(parts):
        lines = jnp.where(which == n, part, lines)
    found = jnp.dot(
        lines.astype(jnp.bfloat16), found_hot[...], preferred_element_type=f32
    )
    together = LANES // PARAM_REGIONS
    for n in range(devices // together):
        lanes = slice(n * LANES, (n + 1) * LANES)
        r_s[n, 0:1] = found[0:1, lanes] + found[1:2, lanes]
        r_s[n, 1:2] = found[2:3, lanes] + found[3:4, lanes]
    for order in sorted(range(1, devices), key=lambda n: (-(n % peers // n_gz), -n)):
        to = (flip(here[0], order // peers),) + peer(order % peers)[1:]
        other = to[0] * peers + to[1] * n_gz + to[2]
        remote(
            r_s.at[other // together],
            r_r.at[order],
            r_ss,
            r_rs,
            to,
        ).start()
    for k in range(3):
        lam[0, k] = const[k] + inverse_ref[0, 0, k] * total_r[...]
    out_early.start()
    part = r_s[index // together]
    r_all = remote(r_r.at[1:], r_r.at[1:], r_ss, r_rs, peer(1))
    r_all.wait_recv()
    for order in range(1, devices):
        part = part + r_r[order]
    mine = jnp.full((2, PARAM_REGIONS), lax.rem(index, together), jnp.int32)
    result = jnp.zeros((2, PARAM_REGIONS), f32)
    for n in range(together):
        result = jnp.where(
            mine == n, part[:, n * PARAM_REGIONS : (n + 1) * PARAM_REGIONS], result
        )
    region_ref[...] = result
    r_all.wait_send()
    out_late.wait()
    out_early.wait()


def local(*arrays):
    (
        pressure,
        saturation,
        permeability,
        porosity,
        upwind_flags,
        diag_inverse,
        seismic_obs,
        well_x,
        well_y,
        well_top,
        well_len,
        well_bhp,
        well_obs,
        fault_cell,
        fault_count,
        fault_trans,
        fault_up,
        region_map,
    ) = arrays
    counts = tuple(lax.axis_size(axis) for axis in ("gx", "gy", "gz"))
    nx, ny, nz = permeability.shape
    peers, slots = fault_cell.shape[1:]
    devices = counts[0] * peers
    hbm = pl.BlockSpec(memory_space=pltpu.HBM)
    vmem = pl.BlockSpec(memory_space=pltpu.VMEM)
    f32 = jnp.float32
    bf16 = jnp.bfloat16
    dma = pltpu.SemaphoreType.DMA

    def field(*lead, dtype=f32):
        return pltpu.VMEM(lead + (nx, ny, nz), dtype)

    def per_fault(*lead, dtype=f32):
        return pltpu.VMEM(lead + (peers, slots), dtype)

    bundles = [(2, 2, 5, ny, nz), (2, 2, 5, nx, 1, nz), (2, 2, 5, ny, nz)]
    faces = [(2, ny, nz), (2, nx, 1, nz), (2, ny, nz)]
    large = arrays[:7]
    scratch = [
        *[pltpu.VMEM(array.shape, array.dtype) for array in large],
        dma((len(large),)),
        dma((2,)),
        field(2, 3),
        field(2, 3, 3),
        field(2, 3, 3),
        field(2, 3),
        field(),
        field(2, 3),
        field(3),
        field(3),
        field(3),
        field(2, 2, 3),
        field(2, 3),
        field(2, 3),
        field(2, 3),
        field(2, 3),
        field(2),
        field(),
        field(),
        pltpu.VMEM((nx * ny, peers * slots), bf16),
        pltpu.VMEM((peers * slots, nz), bf16),
        pltpu.VMEM((3 * region_map.size, devices * PARAM_REGIONS), bf16),
        per_fault(dtype=jnp.int32),
        per_fault(),
        per_fault(dtype=jnp.int32),
        per_fault(),
        per_fault(2, 3),
        per_fault(4),
        *[pltpu.VMEM(s, f32) for s in bundles],
        *[pltpu.VMEM(s, f32) for s in bundles],
        dma((2, 3, 2)),
        dma((2, 3, 2)),
        pltpu.VMEM((6,) + region_map.shape, jnp.int32),
        dma((3, 2)),
        dma((3, 2)),
        per_fault(2, 3),
        per_fault(2, 3),
        dma((2,)),
        dma((2,)),
        pltpu.VMEM((8, LANES), f32),
        pltpu.VMEM((counts[2], 8, LANES), f32),
        dma((counts[2],)),
        dma((counts[2],)),
        *[pltpu.VMEM(s, f32) for s in faces],
        *[pltpu.VMEM((2,) + s, f32) for s in faces],
        dma((3, 2)),
        dma((2, 3, 2)),
        per_fault(3),
        per_fault(3),
        dma,
        dma((len(CUTS) - 1,)),
        per_fault(2),
        per_fault(2),
        dma((2,)),
        dma((2, len(CUTS) - 1)),
        pltpu.VMEM((devices * PARAM_REGIONS // LANES, 2, LANES), f32),
        pltpu.VMEM((devices, 2, LANES), f32),
        dma,
        dma,
    ]
    results = (
        jax.ShapeDtypeStruct((2, 3, nx, ny, nz), f32),
        jax.ShapeDtypeStruct((2, PARAM_REGIONS), f32),
    )
    found = pl.pallas_call(
        functools.partial(kernel, counts),
        out_shape=results,
        in_specs=[hbm] * 7 + [vmem] * 11,
        out_specs=(hbm, vmem),
        scratch_shapes=scratch,
        compiler_params=pltpu.CompilerParams(
            collective_id=0, has_side_effects=True, vmem_limit_bytes=60 * 2**20
        ),
    )(*arrays)

    def finish(lam_ref, region_ref, lam_out, region_out, sem):
        copy = pltpu.make_async_copy(lam_ref, lam_out, sem)
        copy.start()
        region_out[...] = region_ref[...]
        copy.wait()

    return pl.pallas_call(
        finish,
        out_shape=results,
        in_specs=[vmem, vmem],
        out_specs=(hbm, vmem),
        scratch_shapes=[dma],
    )(*found)


def solution(mesh):
    cells = P("gx", "gy", "gz")
    column = P("gx", "gy", None)
    every = ("gx", "gy", "gz")
    placed = (
        P(None, "gx", "gy", "gz"),
        P(None, None, "gx", "gy", "gz"),
        cells,
        cells,
        cells,
        P(None, None, None, "gx", "gy", "gz"),
        cells,
        column,
        column,
        column,
        column,
        P(None, "gx", "gy", None),
        P(None, "gx", "gy", None),
        P(every, None, None),
        P(every, None),
        P(every, None, None),
        P(every, None, None),
        cells,
    )
    return jax.shard_map(
        local,
        mesh=mesh,
        in_specs=placed,
        out_specs=(P(None, None, "gx", "gy", "gz"), P(None, every)),
        check_vma=False,
    )
```

```python
import functools

import jax
import jax.numpy as jnp
from jax import lax
from jax.experimental import pallas as pl
from jax.experimental.pallas import tpu as pltpu
from jax.sharding import PartitionSpec as P

ITERS = 6
BOX = 4
PARAM_REGIONS = 32
LANES = 128
CUTS = (1, 12, 16)
MESH = pl.DeviceIdType.MESH

fluid_viscosity = (0.4, 0.5, 1.0)
sigma_sq = 64.0
SIDES = tuple((dim, side) for dim in range(3) for side in range(2))


def phase_mobility(water_sat, oil_sat):
    gas_sat = 1.0 - water_sat - oil_sat
    return [
        water_sat * water_sat / fluid_viscosity[0],
        oil_sat * oil_sat / fluid_viscosity[1],
        gas_sat * gas_sat / fluid_viscosity[2],
    ]


def mobility_slopes(water_sat, oil_sat):
    gas_sat = 1.0 - water_sat - oil_sat
    return (
        2.0 * water_sat / fluid_viscosity[0] - 2.0 * gas_sat / fluid_viscosity[2],
        2.0 * oil_sat / fluid_viscosity[1] - 2.0 * gas_sat / fluid_viscosity[2],
    )


def split(value, parts):
    pieces = []
    for _ in range(parts):
        piece = value.astype(jnp.bfloat16)
        pieces.append(piece)
        value = value - piece.astype(jnp.float32)
    return pieces


def kernel(
    counts,
    pressure_hbm,
    saturation_hbm,
    perm_hbm,
    porosity_hbm,
    flags_hbm,
    inverse_hbm,
    seismic_hbm,
    well_x_hbm,
    well_y_hbm,
    well_top_hbm,
    well_len_hbm,
    bhp_hbm,
    obs_hbm,
    fault_cell_hbm,
    fault_count_hbm,
    fault_trans_hbm,
    fault_up_hbm,
    map_hbm,
    lam_hbm,
    region_ref,
    pressure_ref,
    sat_ref,
    perm_ref,
    porosity_ref,
    flags_ref,
    inverse_ref,
    seismic_ref,
    well_x_ref,
    well_y_ref,
    well_top_ref,
    well_len_ref,
    bhp_ref,
    obs_ref,
    fault_cell_ref,
    fault_count_ref,
    fault_trans_ref,
    fault_up_ref,
    map_ref,
    in_sem,
    out_sem,
    mob,
    wp,
    wm,
    src,
    explicit,
    lam,
    const,
    turn_c,
    turn_d,
    push,
    push_turn_c,
    push_turn_d,
    flux_base,
    flux_lead,
    por,
    total_r,
    delta,
    row_hot,
    z_hot,
    found_hot,
    f_cell,
    f_scale,
    f_up,
    f_tmp,
    f_coef,
    f_send,
    bx_s,
    by_s,
    bz_s,
    bx_r,
    by_r,
    bz_r,
    b_ss,
    b_rs,
    map_r,
    map_ss,
    map_rs,
    m_s,
    m_r,
    m_ss,
    m_rs,
    w_s,
    w_r,
    w_ss,
    w_rs,
    x_s,
    y_s,
    z_s,
    x_r,
    y_r,
    z_r,
    h_ss,
    h_rs,
    v_s,
    v_r,
    v_ss,
    v_rs,
    c_s,
    c_r,
    c_ss,
    c_rs,
    r_s,
    r_r,
    r_ss,
    r_rs,
):
    n_gx, n_gy, n_gz = counts
    here = (lax.axis_index("gx"), lax.axis_index("gy"), lax.axis_index("gz"))
    peers = n_gy * n_gz
    devices = n_gx * peers
    me = here[1] * n_gz + here[2]
    index = here[0] * peers + me
    shape = perm_ref.shape
    nx, ny, nz = shape
    rows = nx * ny
    slots = c_r.shape[2]
    f32 = jnp.float32

    def flip(number, bits):
        bit = 1
        while bit <= bits:
            if bits & bit:
                number = number + bit - 2 * bit * lax.rem(number // bit, 2)
            bit *= 2
        return number

    flipped_y = [flip(here[1], bits) for bits in range(n_gy)]
    flipped_z = [flip(here[2], bits) for bits in range(n_gz)]

    def peer(order):
        return (here[0], flipped_y[order // n_gz], flipped_z[order % n_gz])

    def peer_place(order):
        other = peer(order)
        return other[1] * n_gz + other[2]

    def toward(dim, step):
        moved = list(here)
        moved[dim] = lax.rem(here[dim] + step + counts[dim], counts[dim])
        return tuple(moved)

    def device(number):
        return (number // peers, lax.rem(number, peers) // n_gz, lax.rem(number, n_gz))

    def remote(source, target, send, recv, to):
        return pltpu.make_async_remote_copy(
            src_ref=source,
            dst_ref=target,
            send_sem=send,
            recv_sem=recv,
            device_id=to,
            device_id_type=MESH,
        )

    has_next = [here[dim] < counts[dim] - 1 for dim in range(3)]
    has_last = [here[dim] > 0 for dim in range(3)]

    def sends(dim, side):
        return has_next[dim] if side == 0 else has_last[dim]

    def receives(dim, side):
        return has_last[dim] if side == 0 else has_next[dim]

    loads = [
        pltpu.make_async_copy(source, target, in_sem.at[n])
        for n, (source, target) in enumerate(
            (
                (saturation_hbm, sat_ref),
                (perm_hbm, perm_ref),
                (pressure_hbm, pressure_ref),
                (well_x_hbm, well_x_ref),
                (well_y_hbm, well_y_ref),
                (well_top_hbm, well_top_ref),
                (well_len_hbm, well_len_ref),
                (bhp_hbm, bhp_ref),
                (obs_hbm, obs_ref),
                (fault_cell_hbm, fault_cell_ref),
                (fault_count_hbm, fault_count_ref),
                (fault_trans_hbm, fault_trans_ref),
                (fault_up_hbm, fault_up_ref),
                (map_hbm, map_ref),
                (flags_hbm, flags_ref),
                (seismic_hbm, seismic_ref),
                (inverse_hbm, inverse_ref),
                (porosity_hbm, porosity_ref),
            )
        )
    ]
    for load in loads:
        load.start()
    for ref in (bx_r, by_r, bz_r, x_r, y_r, z_r, m_r, v_r, c_r, map_r):
        ref[...] = jnp.zeros_like(ref)

    barrier = pltpu.get_barrier_semaphore()
    for offset in range(1, devices):
        pl.semaphore_signal(
            barrier,
            inc=1,
            device_id=device(lax.rem(index + offset, devices)),
            device_id_type=MESH,
        )

    yi = lax.broadcasted_iota(jnp.int32, shape, 1)
    zi = lax.broadcasted_iota(jnp.int32, shape, 2)
    iotas = (None, yi, zi)
    diagonal = lax.broadcasted_iota(jnp.int32, shape, 0) == zi

    def pack(field, lane):
        return jnp.sum(jnp.where(diagonal, field[:, :, lane : lane + 1], 0.0), axis=0)

    def unpack(tile):
        return jnp.concatenate(
            [jnp.broadcast_to(tile[:, x : x + 1], (ny, nz))[None] for x in range(nx)], axis=0
        )

    def at_next(field, dim, edge):
        if dim == 0:
            return jnp.concatenate([field[1:], edge], axis=0)
        last = shape[dim] - 1
        return jnp.where(iotas[dim] == last, edge, pltpu.roll(field, last, dim))

    def at_last(field, dim, edge):
        if dim == 0:
            return jnp.concatenate([edge, field[:-1]], axis=0)
        return jnp.where(iotas[dim] == 0, edge, pltpu.roll(field, 1, dim))

    def edge_of(dim, halo):
        if dim == 0:
            return halo[None]
        return halo if dim == 1 else unpack(halo)

    def no_edge(dim):
        return jnp.zeros((1, ny, nz), f32) if dim == 0 else 0.0

    def faults_in_order(array, target):
        for order in range(peers):
            target[order : order + 1, :] = array[pl.ds(peer_place(order), 1), :]

    for load in loads[:14]:
        load.wait()
    faults_in_order(fault_cell_ref.at[0], f_cell)
    faults_in_order(fault_up_ref.at[0], f_up)
    slot_index = lax.broadcasted_iota(jnp.int32, (1, slots), 1)
    for p in range(peers):
        f_tmp[p : p + 1, :] = jnp.where(
            slot_index < fault_count_ref[:, p : p + 1], fault_trans_ref[0, p : p + 1, :], 0.0
        )
    faults_in_order(f_tmp, f_scale)
    f_row = f_cell[...] // nz
    f_z = f_cell[...] - f_row * nz

    def gather(refs, low=0, high=None):
        high = peers if high is None else high
        row, at = f_row[low:high], f_z[low:high]

        def body(x, chosen):
            for y in range(ny):
                here_row = row == x * ny + y
                chosen = [
                    jnp.where(
                        here_row,
                        jnp.take_along_axis(
                            jnp.broadcast_to(ref[x, y : y + 1, :], (high - low, nz)),
                            at,
                            axis=1,
                            mode="promise_in_bounds",
                        ),
                        value,
                    )
                    for ref, value in zip(refs, chosen)
                ]
            return chosen

        start = [jnp.zeros((high - low, slots), f32) for _ in refs]
        return lax.fori_loop(0, nx, body, start, unroll=True)

    mobility = [phase_mobility(sat_ref[t + 1, 0], sat_ref[t + 1, 1]) for t in range(2)]
    for t in range(2):
        for k in range(3):
            mob[t, k] = mobility[t][k]
    perm = perm_ref[...]

    def bundle(part, fields):
        for q, field in enumerate(fields):
            bx_s[part, 0, q] = field[nx - 1]
            bx_s[part, 1, q] = field[0]
            by_s[part, 0, q] = field[:, ny - 1 :, :]
            by_s[part, 1, q] = field[:, :1, :]
            bz_s[part, 0, q] = pack(field, nz - 1)
            bz_s[part, 1, q] = pack(field, 0)

    def bundle_copy(part, dim, side):
        sent, got = ((bx_s, bx_r), (by_s, by_r), (bz_s, bz_r))[dim]
        return remote(
            sent.at[part, side],
            got.at[part, side],
            b_ss.at[part, dim, side],
            b_rs.at[part, dim, side],
            toward(dim, 1 - 2 * side),
        )

    def map_copy(dim, side):
        return remote(
            map_ref,
            map_r.at[2 * dim + side],
            map_ss.at[dim, side],
            map_rs.at[dim, side],
            toward(dim, 1 - 2 * side),
        )

    def start_faces(copies):
        for dim, side in SIDES:

            @pl.when(sends(dim, side))
            def _():
                for copy in copies:
                    copy(dim, side).start()

    def wait_faces(copies):
        for dim, side in SIDES:

            @pl.when(sends(dim, side))
            def _():
                for copy in copies:
                    copy(dim, side).wait_send()

            @pl.when(receives(dim, side))
            def _():
                for copy in copies:
                    copy(dim, side).wait_recv()


    n_wells = well_top_ref.shape[2]
    eye = lax.broadcasted_iota(jnp.int32, (n_wells, n_wells), 0) == lax.broadcasted_iota(
        jnp.int32, (n_wells, n_wells), 1
    )

    def as_column(row):
        return jnp.sum(jnp.where(eye, row.astype(f32), 0.0), axis=1, keepdims=True)

    def as_row(column):
        return jnp.sum(jnp.where(eye, column, 0.0), axis=0, keepdims=True)

    well_row = well_x_ref[0] * ny + well_y_ref[0]
    well_hot = (
        (
            lax.broadcasted_iota(jnp.int32, (n_wells, rows), 1).astype(f32) == as_column(well_row)
        )
        .astype(f32)
        .astype(jnp.bfloat16)
    )
    well_hot_t = (lax.broadcasted_iota(jnp.int32, (rows, n_wells), 0) == well_row).astype(f32)
    depth = (here[2] * nz + lax.broadcasted_iota(jnp.int32, (n_wells, nz), 1)).astype(f32)
    top = as_column(well_top_ref[0])
    bottom = as_column(well_top_ref[0] + well_len_ref[0])
    perforated = jnp.where((depth >= top) & (depth < bottom), 1.0, 0.0)

    def total(t):
        return perm_ref[...] * (mob[t, 0] + mob[t, 1] + mob[t, 2])

    fields = []
    for t in range(2):
        whole = total(t)
        fields += [
            (whole * pressure_ref[t]).reshape(rows, nz),
            whole.reshape(rows, nz),
        ]
    pieces = jnp.concatenate(split(jnp.concatenate(fields, axis=1), 3), axis=0)
    of_wells = jnp.dot(
        jnp.concatenate([well_hot] * 3, axis=1), pieces, preferred_element_type=f32
    )
    w_s[...] = jnp.zeros_like(w_s)
    for t in range(2):
        bhp = as_column(bhp_ref[t, 0])
        rate = jnp.sum(
            perforated
            * (
                of_wells[:, 2 * t * nz : (2 * t + 1) * nz]
                - bhp * of_wells[:, (2 * t + 1) * nz : (2 * t + 2) * nz]
            ),
            axis=1,
            keepdims=True,
        )
        w_s[t : t + 1, :n_wells] = as_row(rate)

    pl.semaphore_wait(barrier, devices - 1)
    w_copies = []
    for offset in range(1, n_gz):
        copy = remote(
            w_s,
            w_r.at[offset],
            w_ss.at[offset],
            w_rs.at[offset],
            (here[0], here[1], lax.rem(here[2] + offset, n_gz)),
        )
        copy.start()
        w_copies.append(copy)
    loads[14].wait()
    bundle(0, [perm_ref[...]] + [mob[1, k] for k in range(3)] + [flags_ref[...].astype(f32)])
    start_faces([functools.partial(bundle_copy, 0)])

    def order_far_first():
        return range(peers - 1, 0, -1)

    groups = list(zip(CUTS[:-1], CUTS[1:]))

    def group(order):
        return [low <= order < high for low, high in groups].index(True)

    def mobility_copy(t, low, high, to):
        return remote(
            m_s.at[t, :, low:high], m_r.at[t, :, low:high], m_ss.at[t], m_rs.at[t], to
        )

    def send_mobility(t):
        own = gather([mob.at[t, k] for k in range(3)])
        for k in range(3):
            m_s[t, k] = own[k]
        for order in order_far_first():
            mobility_copy(t, order, order + 1, peer(order)).start()

    def fault_coefficients(t):
        mobility_copy(t, 1, peers, peer(1)).wait()
        own_up = jnp.bitwise_and(jnp.right_shift(f_up[...], t), 1) == 1
        for k in range(3):
            f_coef[t, k] = f_scale[...] * jnp.where(own_up, m_s[t, k], m_r[t, k])

    send_mobility(1)

    for order in range(peers):
        lanes = slice(order * slots, (order + 1) * slots)
        row_hot[:, lanes] = (
            (lax.broadcasted_iota(jnp.int32, (rows, slots), 0) == f_row[order : order + 1])
            .astype(f32)
            .astype(jnp.bfloat16)
        )
        z_hot[lanes, :] = (
            (lax.broadcasted_iota(jnp.int32, (nz, slots), 0) == f_z[order : order + 1])
            .astype(f32)
            .T.astype(jnp.bfloat16)
        )

    def scatter(read, start, stop):
        base = start // 4 * 4
        parts = split(read(base, stop), 2)
        marked = [[], []]
        for order in range(start, stop):
            hot = row_hot[:, order * slots : (order + 1) * slots]
            at = order - base
            for pieces, part in zip(marked, parts):
                pieces.append(hot * jnp.broadcast_to(part[at : at + 1], hot.shape))
        added = lax.dot_general(
            jnp.concatenate([jnp.concatenate(pieces, axis=1) for pieces in marked], axis=0),
            z_hot[start * slots : stop * slots, :],
            (((1,), (0,)), ((), ())),
            preferred_element_type=f32,
        )
        return (added[:rows] + added[rows:]).reshape(shape)

    for load in loads[15:]:
        load.wait()
    for copy in w_copies:
        copy.wait()
    rates = w_s[...]
    for offset in range(1, n_gz):
        rates = rates + w_r[offset]

    def sources(t):
        misfit = (rates[t : t + 1, :n_wells] - obs_ref[t, 0]) / sigma_sq
        weighted = well_hot_t * misfit
        both = jnp.concatenate([weighted, weighted * bhp_ref[t, 0]], axis=0)
        spread = jnp.dot(
            jnp.concatenate(split(both, 3), axis=0),
            perforated.astype(jnp.bfloat16),
            preferred_element_type=f32,
        )
        spread = spread[: 2 * rows] + spread[2 * rows : 4 * rows] + spread[4 * rows :]
        drawn = pressure_ref[t] * spread[:rows].reshape(shape) - spread[rows:].reshape(shape)
        water_slope, oil_slope = mobility_slopes(sat_ref[t + 1, 0], sat_ref[t + 1, 1])
        whole = total(t)
        src[t, 0] = whole * spread[:rows].reshape(shape)
        water_source = perm_ref[...] * drawn * water_slope
        if t == 1:
            water_source = water_source + (sat_ref[2, 0] - seismic_ref[...])
        src[t, 1] = water_source
        src[t, 2] = perm_ref[...] * drawn * oil_slope
        return whole * drawn

    def face_coefficients(t, flags, mob_from):
        own_flags = flags.astype(jnp.int32)
        for dim in range(3):
            got = (bx_r, by_r, bz_r)[dim]

            def halo(part, side, q):
                return edge_of(dim, got[part, side, q])

            up_face = jnp.sqrt(
                perm_ref[...] * at_next(perm_ref[...], dim, halo(0, 1, 0))
            )
            low_face = jnp.sqrt(
                perm_ref[...] * at_last(perm_ref[...], dim, halo(0, 0, 0))
            )
            up_ok = has_next[dim].astype(f32)
            low_ok = has_last[dim].astype(f32)
            if dim == 0:
                up_face = jnp.concatenate([up_face[:-1], up_face[-1:] * up_ok], axis=0)
                low_face = jnp.concatenate([low_face[:1] * low_ok, low_face[1:]], axis=0)
            else:
                up_face = up_face * jnp.where(iotas[dim] == shape[dim] - 1, up_ok, 1.0)
                low_face = low_face * jnp.where(iotas[dim] == 0, low_ok, 1.0)
            bit = 3 * t + dim
            low_flags = at_last(flags, dim, halo(0, 0, 4)).astype(jnp.int32)
            own_up = jnp.bitwise_and(jnp.right_shift(own_flags, bit), 1) == 1
            low_up = jnp.bitwise_and(jnp.right_shift(low_flags, bit), 1) == 1
            for k in range(3):
                part, q = mob_from(k)
                m = mob[t, k]
                wp[t, dim, k] = up_face * jnp.where(
                    own_up, m, at_next(m, dim, halo(part, 1, q))
                )
                wm[t, dim, k] = low_face * jnp.where(
                    low_up, at_last(m, dim, halo(part, 0, q)), m
                )

    def face_copy(parity, dim, side):
        sent, got = ((x_s, x_r), (y_s, y_r), (z_s, z_r))[dim]
        return remote(
            sent.at[side],
            got.at[parity, side],
            h_ss.at[dim, side],
            h_rs.at[parity, dim, side],
            toward(dim, 1 - 2 * side),
        )

    def send_faces(parity, up, down):
        x_s[0] = up[0][nx - 1]
        x_s[1] = down[0][0]
        y_s[0] = up[1][:, ny - 1 :, :]
        y_s[1] = down[1][:, :1, :]
        z_s[0] = pack(up[2], nz - 1)
        z_s[1] = pack(down[2], 0)
        start_faces([functools.partial(face_copy, parity)])
        inner = at_last(up[0], 0, no_edge(0)) + at_next(down[0], 0, no_edge(0))
        for dim in (1, 2):
            inner = inner + at_last(up[dim], dim, 0.0) + at_next(down[dim], dim, 0.0)
        return inner

    def add_faces(parity, inner):
        wait_faces([functools.partial(face_copy, parity)])
        inner = jnp.concatenate(
            [
                inner[:1] + x_r[parity, 0][None],
                inner[1 : nx - 1],
                inner[nx - 1 :] + x_r[parity, 1][None],
            ],
            axis=0,
        )
        inner = inner + jnp.where(
            yi == 0, y_r[parity, 0], jnp.where(yi == ny - 1, y_r[parity, 1], 0.0)
        )
        return inner + jnp.where(
            zi == 0,
            unpack(z_r[parity, 0]),
            jnp.where(zi == nz - 1, unpack(z_r[parity, 1]), 0.0),
        )

    def fault_copy(parity, low, high, order, to):
        return remote(
            c_s.at[parity, low:high],
            c_r.at[parity, low:high],
            c_ss.at[parity],
            c_rs.at[parity, group(low)],
            to,
        )

    def send_faults(parity, ref, lead, fixed):
        for low in range(peers - 8, -8, -8):
            part = slice(low, low + 8)
            values = f_send[lead, part] * gather([ref], low, low + 8)[0]
            if fixed is not None:
                values = values + f_send[fixed, part]
            c_s[parity, part] = values
            for order in range(low + 7, max(low, 1) - 1, -1):
                fault_copy(parity, order, order + 1, order, peer(order)).start()

    def add_faults(parity, inner):
        def read(low, high):
            return c_r[parity, low:high]

        for low, high in groups:
            fault_copy(parity, low, high, low, peer(low)).wait_recv()
            inner = inner + scatter(read, low, high)
        fault_copy(parity, 1, peers, 1, peer(1)).wait_send()
        return inner

    def scalar_round(parity, t, aside):
        send_faults(parity, delta, t, None)
        now = delta[...]
        total_r[...] += now
        inner = send_faces(
            parity,
            [push[t, 0, dim] * now for dim in range(3)],
            [push[t, 1, dim] * now for dim in range(3)],
        )
        if aside is not None:
            aside()
        inner = add_faces(parity, inner)
        inner = add_faults(parity, inner)
        delta[...] = inner

    def dot3(coefficients, values):
        return sum(coefficients(k) * values(k) for k in range(3))

    def scalar_push(t):
        for dim in range(3):
            push[t, 0, dim] = dot3(lambda k: wp[t, dim, k], lambda k: inverse_ref[t, 0, k])
            push[t, 1, dim] = dot3(lambda k: wm[t, dim, k], lambda k: inverse_ref[t, 0, k])

    def scalar_faults(t):
        values = gather([inverse_ref.at[t, 0, k] for k in range(3)])
        f_send[t] = dot3(lambda k: f_coef[t, k], lambda k: values[k])

    explicit[...] = sources(1)
    total_r[...] = src[1, 0]
    for k in range(3):
        const[k] = inverse_ref[1, 1, k] * src[1, 1] + inverse_ref[1, 2, k] * src[1, 2]
        lam[1, k] = const[k] + inverse_ref[1, 0, k] * src[1, 0]
    def vector_copy(low, high, to):
        return remote(
            v_s.at[:, low:high],
            v_r.at[:, low:high],
            v_ss,
            v_rs.at[group(low)],
            to,
        )

    for low in range(peers - 8, -8, -8):
        values = gather([lam.at[1, k] for k in range(3)], low, low + 8)
        for k in range(3):
            v_s[k, low : low + 8] = values[k]
        for order in range(low + 7, max(low, 1) - 1, -1):
            vector_copy(order, order + 1, peer(order)).start()
    wait_faces([functools.partial(bundle_copy, 0)])
    flags = flags_ref[...].astype(f32)
    face_coefficients(1, flags, lambda k: (0, 1 + k))
    inner = send_faces(
        0,
        [dot3(lambda k: wp[1, dim, k], lambda k: lam[1, k]) for dim in range(3)],
        [dot3(lambda k: wm[1, dim, k], lambda k: lam[1, k]) for dim in range(3)],
    )
    bundle(1, [mob[0, k] for k in range(3)] + [pressure_ref[t] for t in range(2)])
    start_faces([functools.partial(bundle_copy, 1), map_copy])
    scalar_push(1)
    send_mobility(0)
    fault_coefficients(1)
    scalar_faults(1)
    inner = add_faces(0, inner)

    def arrived(low, high):
        return dot3(lambda k: f_coef[1, k, low:high], lambda k: v_r[k, low:high])

    for low, high in groups:
        vector_copy(low, high, peer(low)).wait_recv()
        inner = inner + scatter(arrived, low, high)
    vector_copy(1, peers, peer(1)).wait_send()
    delta[...] = inner

    def prepare_turn():
        explicit[...] += sources(0)
        wait_faces([functools.partial(bundle_copy, 1), map_copy])
        face_coefficients(0, flags_ref[...].astype(f32), lambda k: (1, k))
        porosity = porosity_ref[...]
        first = src[0, 1] + porosity * (const[0] - const[2])
        second = src[0, 2] + porosity * (const[1] - const[2])
        d_first = porosity * (inverse_ref[1, 0, 0] - inverse_ref[1, 0, 2])
        d_second = porosity * (inverse_ref[1, 0, 1] - inverse_ref[1, 0, 2])
        for k in range(3):
            turn_c[k] = (
                inverse_ref[0, 0, k] * src[0, 0]
                + inverse_ref[0, 1, k] * first
                + inverse_ref[0, 2, k] * second
            )
            turn_d[k] = inverse_ref[0, 1, k] * d_first + inverse_ref[0, 2, k] * d_second

    def prepare_sends():
        fault_coefficients(0)
        for side, w in enumerate((wp, wm)):
            for dim in range(3):
                push_turn_c[side, dim] = dot3(lambda k: w[0, dim, k], lambda k: turn_c[k])
                push_turn_d[side, dim] = dot3(lambda k: w[0, dim, k], lambda k: turn_d[k])
        values = gather([ref.at[k] for ref in (turn_c, turn_d) for k in range(3)])
        f_send[2] = dot3(lambda k: f_coef[0, k], lambda k: values[k])
        f_send[3] = dot3(lambda k: f_coef[0, k], lambda k: values[3 + k])

    n_rounds = ITERS - 1
    scalar_round(1, 1, prepare_turn)
    scalar_round(0, 1, prepare_sends)

    def more(t):
        def body(step, carry):
            scalar_round(lax.rem(step, 2), t, None)
            return carry

        return body

    lax.fori_loop(3, n_rounds, more(1), 0)

    out_late = pltpu.make_async_copy(lam.at[1], lam_hbm.at[1], out_sem.at[1])
    out_early = pltpu.make_async_copy(lam.at[0], lam_hbm.at[0], out_sem.at[0])
    parity = n_rounds % 2
    total_r[...] += delta[...]
    send_faults(parity, total_r, 3, 2)
    now = total_r[...]
    inner = send_faces(
        parity,
        [push_turn_c[0, dim] + push_turn_d[0, dim] * now for dim in range(3)],
        [push_turn_c[1, dim] + push_turn_d[1, dim] * now for dim in range(3)],
    )
    for k in range(3):
        lam[1, k] = const[k] + inverse_ref[1, 0, k] * total_r[...]
    out_late.start()
    porosity = porosity_ref[...]
    first = src[0, 1] + porosity * (lam[1, 0] - lam[1, 2])
    second = src[0, 2] + porosity * (lam[1, 1] - lam[1, 2])
    for k in range(3):
        const[k] = inverse_ref[0, 1, k] * first + inverse_ref[0, 2, k] * second
    scalar_push(0)
    scalar_faults(0)
    inner = add_faces(parity, inner)
    inner = add_faults(parity, inner)
    delta[...] = inner
    total_r[...] = src[0, 0]

    n_bx, n_by, n_bz = nx // BOX, ny // BOX, nz // BOX
    n_boxes = n_bx * n_by
    wide = n_boxes * n_bz

    def prepare_gradient():
        for dim in range(3):
            got = (bx_r, by_r, bz_r)[dim]
            flux_base[0, dim] = jnp.zeros(shape, f32)
            flux_base[1, dim] = jnp.zeros(shape, f32)
            for t in range(2):
                p_here = pressure_ref[t]
                up_p = 0.5 * (
                    p_here - at_next(p_here, dim, edge_of(dim, got[1, 1, 3 + t]))
                )
                down_p = -0.5 * (
                    at_last(p_here, dim, edge_of(dim, got[1, 0, 3 + t])) - p_here
                )
                source = (lambda k: const[k]) if t == 0 else (lambda k: lam[1, k])
                flux_base[0, dim] += up_p * dot3(lambda k: wp[t, dim, k], source)
                flux_base[1, dim] += down_p * dot3(lambda k: wm[t, dim, k], source)
                if t == 0:
                    flux_lead[0, dim] = up_p * push[0, 0, dim]
                    flux_lead[1, dim] = down_p * push[0, 1, dim]
        steps = []
        for t in range(2):
            water = sat_ref[t + 1, 0] - sat_ref[t, 0]
            oil = sat_ref[t + 1, 1] - sat_ref[t, 1]
            steps.append((water, oil, water + oil))
        por[0] = -(
            lam[1, 0] * steps[1][0]
            + lam[1, 1] * steps[1][1]
            - lam[1, 2] * steps[1][2]
            + const[0] * steps[0][0]
            + const[1] * steps[0][1]
            - const[2] * steps[0][2]
        )
        por[1] = -(
            inverse_ref[0, 0, 0] * steps[0][0]
            + inverse_ref[0, 0, 1] * steps[0][1]
            - inverse_ref[0, 0, 2] * steps[0][2]
        )
        z_lane = lax.broadcasted_iota(jnp.int32, (1, n_bz), 1)

        def own_map(bx, by):
            return map_ref[bx, by : by + 1, :]

        def other_map(dim, side, bx, by):
            return map_r[2 * dim + side, bx, by : by + 1, :]

        labels = [[], [], []]
        for bx in range(n_bx):
            for by in range(n_by):
                labels[0].append(own_map(bx, by))
                labels[1].append(
                    other_map(1, 0, bx, n_by - 1) if by == 0 else other_map(1, 1, bx, 0)
                )
                if bx == 0:
                    label = other_map(0, 0, n_bx - 1, by)
                elif bx == n_bx - 1:
                    label = other_map(0, 1, 0, by)
                else:
                    even, odd = 2 * (bx - 1), 2 * (bx - 1) + 1
                    label = jnp.zeros((1, n_bz), jnp.int32)
                    for lane, side, box in (
                        (0, 0, even),
                        (1, 0, odd),
                        (n_bz - 2, 1, odd),
                        (n_bz - 1, 1, even),
                    ):
                        edge = n_bz - 1 if side == 0 else 0
                        label = jnp.where(
                            z_lane == lane,
                            other_map(2, side, box, by)[:, edge : edge + 1],
                            label,
                        )
                labels[2].append(label)
        n_regions = devices * PARAM_REGIONS
        region = lax.broadcasted_iota(jnp.int32, (LANES, n_regions), 1).astype(f32)
        for part in range(3):
            label = jnp.concatenate(labels[part], axis=1).astype(f32)
            for first in range(0, wide, LANES):
                column = jnp.broadcast_to(label[:, first : first + LANES], (LANES, LANES)).T
                found_hot[part * wide + first : part * wide + first + LANES, :] = (
                    (region == jnp.concatenate([column] * (n_regions // LANES), axis=1))
                    .astype(f32)
                    .astype(jnp.bfloat16)
                )

    parity = (n_rounds + 1) % 2
    scalar_round(parity, 0, prepare_gradient)
    lax.fori_loop(n_rounds + 2, 2 * n_rounds, more(0), 0)

    total_r[...] += delta[...]
    now = total_r[...]
    flux = [
        [flux_base[side, dim] + flux_lead[side, dim] * now for dim in range(3)]
        for side in range(2)
    ]
    gradient = explicit[...]
    for dim in range(3):
        gradient = gradient - (
            flux[0][dim]
            + flux[1][dim]
            + at_last(flux[0][dim], dim, no_edge(dim))
            + at_next(flux[1][dim], dim, no_edge(dim))
        )

    def x_sums(field):
        return jnp.sum(field.reshape(n_bx, BOX, ny, nz), axis=1)

    y_pushed = x_sums(jnp.where(yi == 0, flux[1][1], 0.0) + jnp.where(yi == ny - 1, flux[0][1], 0.0))
    z_pushed = x_sums(jnp.where(zi == 0, flux[1][2], 0.0) + jnp.where(zi == nz - 1, flux[0][2], 0.0))
    lane = lax.broadcasted_iota(jnp.int32, (ny, nz), 1)

    def moved(tile):
        return jnp.where(
            lane == BOX,
            pltpu.roll(tile, BOX, 1),
            jnp.where(lane == nz - 1 - BOX, pltpu.roll(tile, nz - BOX, 1), 0.0),
        )

    mixed = jnp.concatenate(
        [flux[1][0][0][None]]
        + [(z_pushed[2 * n] + moved(z_pushed[2 * n + 1]))[None] for n in range(n_bx // 2)]
        + [flux[0][0][nx - 1][None]],
        axis=0,
    )
    stacked = jnp.concatenate(
        [x_sums(gradient), x_sums(por[0] + por[1] * now), -y_pushed, -mixed], axis=0
    ).reshape(4 * n_bx * ny, nz)
    z_boxes = (
        (
            lax.broadcasted_iota(jnp.int32, (nz, wide), 0) // BOX
            == lax.rem(lax.broadcasted_iota(jnp.int32, (nz, wide), 1), n_bz)
        )
        .astype(f32)
        .astype(jnp.bfloat16)
    )
    boxed = jnp.dot(
        jnp.concatenate(split(stacked, 2), axis=1),
        jnp.concatenate([z_boxes] * 2, axis=0),
        preferred_element_type=f32,
    )
    in_box = (
        lax.broadcasted_iota(jnp.int32, (n_bx * ny, wide), 1) // n_bz
        == lax.broadcasted_iota(jnp.int32, (n_bx * ny, wide), 0) // BOX
    )
    sums = [
        jnp.sum(
            jnp.where(in_box, boxed[n * n_bx * ny : (n + 1) * n_bx * ny], 0.0),
            axis=0,
            keepdims=True,
        )
        for n in range(4)
    ]
    none = jnp.zeros((1, wide), f32)
    perm_row = jnp.concatenate([sums[0], sums[2], sums[3]], axis=1)
    por_row = jnp.concatenate([sums[1], none, none], axis=1)
    parts = [
        part.astype(f32) for row in (perm_row, por_row) for part in split(row, 2)
    ]
    which = lax.broadcasted_iota(jnp.int32, (8, 3 * wide), 0)
    lines = jnp.zeros((8, 3 * wide), f32)
    for n, part in enumerate(parts):
        lines = jnp.where(which == n, part, lines)
    found = jnp.dot(
        lines.astype(jnp.bfloat16), found_hot[...], preferred_element_type=f32
    )
    together = LANES // PARAM_REGIONS
    for n in range(devices // together):
        lanes = slice(n * LANES, (n + 1) * LANES)
        r_s[n, 0:1] = found[0:1, lanes] + found[1:2, lanes]
        r_s[n, 1:2] = found[2:3, lanes] + found[3:4, lanes]
    for order in sorted(range(1, devices), key=lambda n: (-(n % peers // n_gz), -n)):
        to = (flip(here[0], order // peers),) + peer(order % peers)[1:]
        other = to[0] * peers + to[1] * n_gz + to[2]
        remote(
            r_s.at[other // together],
            r_r.at[order],
            r_ss,
            r_rs,
            to,
        ).start()
    for k in range(3):
        lam[0, k] = const[k] + inverse_ref[0, 0, k] * total_r[...]
    out_early.start()
    part = r_s[index // together]
    r_all = remote(r_r.at[1:], r_r.at[1:], r_ss, r_rs, peer(1))
    r_all.wait_recv()
    for order in range(1, devices):
        part = part + r_r[order]
    mine = jnp.full((2, PARAM_REGIONS), lax.rem(index, together), jnp.int32)
    result = jnp.zeros((2, PARAM_REGIONS), f32)
    for n in range(together):
        result = jnp.where(
            mine == n, part[:, n * PARAM_REGIONS : (n + 1) * PARAM_REGIONS], result
        )
    region_ref[...] = result
    r_all.wait_send()
    out_late.wait()
    out_early.wait()


def local(*arrays):
    (
        pressure,
        saturation,
        permeability,
        porosity,
        upwind_flags,
        diag_inverse,
        seismic_obs,
        well_x,
        well_y,
        well_top,
        well_len,
        well_bhp,
        well_obs,
        fault_cell,
        fault_count,
        fault_trans,
        fault_up,
        region_map,
    ) = arrays
    counts = tuple(lax.axis_size(axis) for axis in ("gx", "gy", "gz"))
    nx, ny, nz = permeability.shape
    peers, slots = fault_cell.shape[1:]
    devices = counts[0] * peers
    hbm = pl.BlockSpec(memory_space=pltpu.HBM)
    vmem = pl.BlockSpec(memory_space=pltpu.VMEM)
    f32 = jnp.float32
    bf16 = jnp.bfloat16
    dma = pltpu.SemaphoreType.DMA

    def field(*lead, dtype=f32):
        return pltpu.VMEM(lead + (nx, ny, nz), dtype)

    def per_fault(*lead, dtype=f32):
        return pltpu.VMEM(lead + (peers, slots), dtype)

    bundles = [(2, 2, 5, ny, nz), (2, 2, 5, nx, 1, nz), (2, 2, 5, ny, nz)]
    faces = [(2, ny, nz), (2, nx, 1, nz), (2, ny, nz)]
    scratch = [
        *[pltpu.VMEM(array.shape, array.dtype) for array in arrays],
        dma((len(arrays),)),
        dma((2,)),
        field(2, 3),
        field(2, 3, 3),
        field(2, 3, 3),
        field(2, 3),
        field(),
        field(2, 3),
        field(3),
        field(3),
        field(3),
        field(2, 2, 3),
        field(2, 3),
        field(2, 3),
        field(2, 3),
        field(2, 3),
        field(2),
        field(),
        field(),
        pltpu.VMEM((nx * ny, peers * slots), bf16),
        pltpu.VMEM((peers * slots, nz), bf16),
        pltpu.VMEM((3 * region_map.size, devices * PARAM_REGIONS), bf16),
        per_fault(dtype=jnp.int32),
        per_fault(),
        per_fault(dtype=jnp.int32),
        per_fault(),
        per_fault(2, 3),
        per_fault(4),
        *[pltpu.VMEM(s, f32) for s in bundles],
        *[pltpu.VMEM(s, f32) for s in bundles],
        dma((2, 3, 2)),
        dma((2, 3, 2)),
        pltpu.VMEM((6,) + region_map.shape, jnp.int32),
        dma((3, 2)),
        dma((3, 2)),
        per_fault(2, 3),
        per_fault(2, 3),
        dma((2,)),
        dma((2,)),
        pltpu.VMEM((8, LANES), f32),
        pltpu.VMEM((counts[2], 8, LANES), f32),
        dma((counts[2],)),
        dma((counts[2],)),
        *[pltpu.VMEM(s, f32) for s in faces],
        *[pltpu.VMEM((2,) + s, f32) for s in faces],
        dma((3, 2)),
        dma((2, 3, 2)),
        per_fault(3),
        per_fault(3),
        dma,
        dma((len(CUTS) - 1,)),
        per_fault(2),
        per_fault(2),
        dma((2,)),
        dma((2, len(CUTS) - 1)),
        pltpu.VMEM((devices * PARAM_REGIONS // LANES, 2, LANES), f32),
        pltpu.VMEM((devices, 2, LANES), f32),
        dma,
        dma,
    ]
    results = (
        jax.ShapeDtypeStruct((2, 3, nx, ny, nz), f32),
        jax.ShapeDtypeStruct((2, PARAM_REGIONS), f32),
    )
    found = pl.pallas_call(
        functools.partial(kernel, counts),
        out_shape=results,
        in_specs=[hbm] * len(arrays),
        out_specs=(hbm, vmem),
        scratch_shapes=scratch,
        compiler_params=pltpu.CompilerParams(
            collective_id=0, has_side_effects=True, vmem_limit_bytes=60 * 2**20
        ),
    )(*arrays)

    def finish(lam_ref, region_ref, lam_out, region_out, sem):
        copy = pltpu.make_async_copy(lam_ref, lam_out, sem)
        copy.start()
        region_out[...] = region_ref[...]
        copy.wait()

    return pl.pallas_call(
        finish,
        out_shape=results,
        in_specs=[vmem, vmem],
        out_specs=(hbm, vmem),
        scratch_shapes=[dma],
    )(*found)


def solution(mesh):
    cells = P("gx", "gy", "gz")
    column = P("gx", "gy", None)
    every = ("gx", "gy", "gz")
    placed = (
        P(None, "gx", "gy", "gz"),
        P(None, None, "gx", "gy", "gz"),
        cells,
        cells,
        cells,
        P(None, None, None, "gx", "gy", "gz"),
        cells,
        column,
        column,
        column,
        column,
        P(None, "gx", "gy", None),
        P(None, "gx", "gy", None),
        P(every, None, None),
        P(every, None),
        P(every, None, None),
        P(every, None, None),
        cells,
    )
    return jax.shard_map(
        local,
        mesh=mesh,
        in_specs=placed,
        out_specs=(P(None, None, "gx", "gy", "gz"), P(None, every)),
        check_vma=False,
    )
```

```python
import functools

import jax
import jax.numpy as jnp
from jax import lax
from jax.experimental import pallas as pl
from jax.experimental.pallas import tpu as pltpu
from jax.sharding import PartitionSpec as P

ITERS = 6
BOX = 4
PARAM_REGIONS = 32
LANES = 128
CUTS = (1, 12, 16)
MESH = pl.DeviceIdType.MESH

fluid_viscosity = (0.4, 0.5, 1.0)
sigma_sq = 64.0
SIDES = tuple((dim, side) for dim in range(3) for side in range(2))


def phase_mobility(water_sat, oil_sat):
    gas_sat = 1.0 - water_sat - oil_sat
    return [
        water_sat * water_sat / fluid_viscosity[0],
        oil_sat * oil_sat / fluid_viscosity[1],
        gas_sat * gas_sat / fluid_viscosity[2],
    ]


def mobility_slopes(water_sat, oil_sat):
    gas_sat = 1.0 - water_sat - oil_sat
    return (
        2.0 * water_sat / fluid_viscosity[0] - 2.0 * gas_sat / fluid_viscosity[2],
        2.0 * oil_sat / fluid_viscosity[1] - 2.0 * gas_sat / fluid_viscosity[2],
    )


def split(value, parts):
    pieces = []
    for _ in range(parts):
        piece = value.astype(jnp.bfloat16)
        pieces.append(piece)
        value = value - piece.astype(jnp.float32)
    return pieces


def kernel(
    counts,
    pressure_hbm,
    saturation_hbm,
    perm_hbm,
    porosity_hbm,
    flags_hbm,
    inverse_hbm,
    seismic_hbm,
    well_x_hbm,
    well_y_hbm,
    well_top_hbm,
    well_len_hbm,
    bhp_hbm,
    obs_hbm,
    fault_cell_hbm,
    fault_count_hbm,
    fault_trans_hbm,
    fault_up_hbm,
    map_hbm,
    lam_hbm,
    region_ref,
    pressure_ref,
    sat_ref,
    perm_ref,
    porosity_ref,
    flags_ref,
    inverse_ref,
    seismic_ref,
    well_x_ref,
    well_y_ref,
    well_top_ref,
    well_len_ref,
    bhp_ref,
    obs_ref,
    fault_cell_ref,
    fault_count_ref,
    fault_trans_ref,
    fault_up_ref,
    map_ref,
    in_sem,
    out_sem,
    mob,
    wp,
    wm,
    src,
    explicit,
    lam,
    const,
    turn_c,
    turn_d,
    push,
    push_turn_c,
    push_turn_d,
    flux_base,
    flux_lead,
    por,
    total_r,
    delta,
    row_hot,
    z_hot,
    found_hot,
    f_cell,
    f_scale,
    f_up,
    f_tmp,
    f_coef,
    f_send,
    bx_s,
    by_s,
    bz_s,
    bx_r,
    by_r,
    bz_r,
    b_ss,
    b_rs,
    map_r,
    map_ss,
    map_rs,
    m_s,
    m_r,
    m_ss,
    m_rs,
    w_s,
    w_r,
    w_ss,
    w_rs,
    x_s,
    y_s,
    z_s,
    x_r,
    y_r,
    z_r,
    h_ss,
    h_rs,
    v_s,
    v_r,
    v_ss,
    v_rs,
    c_s,
    c_r,
    c_ss,
    c_rs,
    r_s,
    r_r,
    r_ss,
    r_rs,
):
    n_gx, n_gy, n_gz = counts
    here = (lax.axis_index("gx"), lax.axis_index("gy"), lax.axis_index("gz"))
    peers = n_gy * n_gz
    devices = n_gx * peers
    me = here[1] * n_gz + here[2]
    index = here[0] * peers + me
    shape = perm_ref.shape
    nx, ny, nz = shape
    rows = nx * ny
    slots = c_r.shape[2]
    f32 = jnp.float32

    def flip(number, bits):
        bit = 1
        while bit <= bits:
            if bits & bit:
                number = number + bit - 2 * bit * lax.rem(number // bit, 2)
            bit *= 2
        return number

    flipped_y = [flip(here[1], bits) for bits in range(n_gy)]
    flipped_z = [flip(here[2], bits) for bits in range(n_gz)]

    def peer(order):
        return (here[0], flipped_y[order // n_gz], flipped_z[order % n_gz])

    def peer_place(order):
        other = peer(order)
        return other[1] * n_gz + other[2]

    def toward(dim, step):
        moved = list(here)
        moved[dim] = lax.rem(here[dim] + step + counts[dim], counts[dim])
        return tuple(moved)

    def device(number):
        return (number // peers, lax.rem(number, peers) // n_gz, lax.rem(number, n_gz))

    def remote(source, target, send, recv, to):
        return pltpu.make_async_remote_copy(
            src_ref=source,
            dst_ref=target,
            send_sem=send,
            recv_sem=recv,
            device_id=to,
            device_id_type=MESH,
        )

    has_next = [here[dim] < counts[dim] - 1 for dim in range(3)]
    has_last = [here[dim] > 0 for dim in range(3)]

    def sends(dim, side):
        return has_next[dim] if side == 0 else has_last[dim]

    def receives(dim, side):
        return has_last[dim] if side == 0 else has_next[dim]

    loads = [
        pltpu.make_async_copy(source, target, in_sem.at[n])
        for n, (source, target) in enumerate(
            (
                (saturation_hbm, sat_ref),
                (perm_hbm, perm_ref),
                (pressure_hbm, pressure_ref),
                (well_x_hbm, well_x_ref),
                (well_y_hbm, well_y_ref),
                (well_top_hbm, well_top_ref),
                (well_len_hbm, well_len_ref),
                (bhp_hbm, bhp_ref),
                (obs_hbm, obs_ref),
                (fault_cell_hbm, fault_cell_ref),
                (fault_count_hbm, fault_count_ref),
                (fault_trans_hbm, fault_trans_ref),
                (fault_up_hbm, fault_up_ref),
                (map_hbm, map_ref),
                (flags_hbm, flags_ref),
                (seismic_hbm, seismic_ref),
                (inverse_hbm, inverse_ref),
                (porosity_hbm, porosity_ref),
            )
        )
    ]
    for load in loads:
        load.start()
    for ref in (bx_r, by_r, bz_r, x_r, y_r, z_r, m_r, v_r, c_r, map_r):
        ref[...] = jnp.zeros_like(ref)

    barrier = pltpu.get_barrier_semaphore()
    for offset in range(1, devices):
        pl.semaphore_signal(
            barrier,
            inc=1,
            device_id=device(lax.rem(index + offset, devices)),
            device_id_type=MESH,
        )

    yi = lax.broadcasted_iota(jnp.int32, shape, 1)
    zi = lax.broadcasted_iota(jnp.int32, shape, 2)
    iotas = (None, yi, zi)
    diagonal = lax.broadcasted_iota(jnp.int32, shape, 0) == zi

    def pack(field, lane):
        return jnp.sum(jnp.where(diagonal, field[:, :, lane : lane + 1], 0.0), axis=0)

    def unpack(tile):
        return jnp.concatenate(
            [jnp.broadcast_to(tile[:, x : x + 1], (ny, nz))[None] for x in range(nx)], axis=0
        )

    def at_next(field, dim, edge):
        if dim == 0:
            return jnp.concatenate([field[1:], edge], axis=0)
        last = shape[dim] - 1
        return jnp.where(iotas[dim] == last, edge, pltpu.roll(field, last, dim))

    def at_last(field, dim, edge):
        if dim == 0:
            return jnp.concatenate([edge, field[:-1]], axis=0)
        return jnp.where(iotas[dim] == 0, edge, pltpu.roll(field, 1, dim))

    def edge_of(dim, halo):
        if dim == 0:
            return halo[None]
        return halo if dim == 1 else unpack(halo)

    def no_edge(dim):
        return jnp.zeros((1, ny, nz), f32) if dim == 0 else 0.0

    def faults_in_order(array, target):
        for order in range(peers):
            target[order : order + 1, :] = array[pl.ds(peer_place(order), 1), :]

    for load in loads[:14]:
        load.wait()
    faults_in_order(fault_cell_ref.at[0], f_cell)
    faults_in_order(fault_up_ref.at[0], f_up)
    slot_index = lax.broadcasted_iota(jnp.int32, (1, slots), 1)
    for p in range(peers):
        f_tmp[p : p + 1, :] = jnp.where(
            slot_index < fault_count_ref[:, p : p + 1], fault_trans_ref[0, p : p + 1, :], 0.0
        )
    faults_in_order(f_tmp, f_scale)
    f_row = f_cell[...] // nz
    f_z = f_cell[...] - f_row * nz

    def gather(refs, low=0, high=None):
        high = peers if high is None else high
        row, at = f_row[low:high], f_z[low:high]

        def body(x, chosen):
            for y in range(ny):
                here_row = row == x * ny + y
                chosen = [
                    jnp.where(
                        here_row,
                        jnp.take_along_axis(
                            jnp.broadcast_to(ref[x, y : y + 1, :], (high - low, nz)),
                            at,
                            axis=1,
                            mode="promise_in_bounds",
                        ),
                        value,
                    )
                    for ref, value in zip(refs, chosen)
                ]
            return chosen

        start = [jnp.zeros((high - low, slots), f32) for _ in refs]
        return lax.fori_loop(0, nx, body, start, unroll=True)

    mobility = [phase_mobility(sat_ref[t + 1, 0], sat_ref[t + 1, 1]) for t in range(2)]
    for t in range(2):
        for k in range(3):
            mob[t, k] = mobility[t][k]
    perm = perm_ref[...]

    def bundle(part, fields):
        for q, field in enumerate(fields):
            bx_s[part, 0, q] = field[nx - 1]
            bx_s[part, 1, q] = field[0]
            by_s[part, 0, q] = field[:, ny - 1 :, :]
            by_s[part, 1, q] = field[:, :1, :]
            bz_s[part, 0, q] = pack(field, nz - 1)
            bz_s[part, 1, q] = pack(field, 0)

    def bundle_copy(part, dim, side):
        sent, got = ((bx_s, bx_r), (by_s, by_r), (bz_s, bz_r))[dim]
        return remote(
            sent.at[part, side],
            got.at[part, side],
            b_ss.at[part, dim, side],
            b_rs.at[part, dim, side],
            toward(dim, 1 - 2 * side),
        )

    def map_copy(dim, side):
        return remote(
            map_ref,
            map_r.at[2 * dim + side],
            map_ss.at[dim, side],
            map_rs.at[dim, side],
            toward(dim, 1 - 2 * side),
        )

    def start_faces(copies):
        for dim, side in SIDES:

            @pl.when(sends(dim, side))
            def _():
                for copy in copies:
                    copy(dim, side).start()

    def wait_faces(copies):
        for dim, side in SIDES:

            @pl.when(sends(dim, side))
            def _():
                for copy in copies:
                    copy(dim, side).wait_send()

            @pl.when(receives(dim, side))
            def _():
                for copy in copies:
                    copy(dim, side).wait_recv()


    n_wells = well_top_ref.shape[2]
    eye = lax.broadcasted_iota(jnp.int32, (n_wells, n_wells), 0) == lax.broadcasted_iota(
        jnp.int32, (n_wells, n_wells), 1
    )

    def as_column(row):
        return jnp.sum(jnp.where(eye, row.astype(f32), 0.0), axis=1, keepdims=True)

    def as_row(column):
        return jnp.sum(jnp.where(eye, column, 0.0), axis=0, keepdims=True)

    well_row = well_x_ref[0] * ny + well_y_ref[0]
    well_hot = (
        (
            lax.broadcasted_iota(jnp.int32, (n_wells, rows), 1).astype(f32) == as_column(well_row)
        )
        .astype(f32)
        .astype(jnp.bfloat16)
    )
    well_hot_t = (lax.broadcasted_iota(jnp.int32, (rows, n_wells), 0) == well_row).astype(f32)
    depth = (here[2] * nz + lax.broadcasted_iota(jnp.int32, (n_wells, nz), 1)).astype(f32)
    top = as_column(well_top_ref[0])
    bottom = as_column(well_top_ref[0] + well_len_ref[0])
    perforated = jnp.where((depth >= top) & (depth < bottom), 1.0, 0.0)

    def total(t):
        return perm_ref[...] * (mob[t, 0] + mob[t, 1] + mob[t, 2])

    fields = []
    for t in range(2):
        whole = total(t)
        fields += [
            (whole * pressure_ref[t]).reshape(rows, nz),
            whole.reshape(rows, nz),
        ]
    pieces = jnp.concatenate(split(jnp.concatenate(fields, axis=1), 3), axis=0)
    of_wells = jnp.dot(
        jnp.concatenate([well_hot] * 3, axis=1), pieces, preferred_element_type=f32
    )
    w_s[...] = jnp.zeros_like(w_s)
    for t in range(2):
        bhp = as_column(bhp_ref[t, 0])
        rate = jnp.sum(
            perforated
            * (
                of_wells[:, 2 * t * nz : (2 * t + 1) * nz]
                - bhp * of_wells[:, (2 * t + 1) * nz : (2 * t + 2) * nz]
            ),
            axis=1,
            keepdims=True,
        )
        w_s[t : t + 1, :n_wells] = as_row(rate)

    pl.semaphore_wait(barrier, devices - 1)
    w_copies = []
    for offset in range(1, n_gz):
        copy = remote(
            w_s,
            w_r.at[offset],
            w_ss.at[offset],
            w_rs.at[offset],
            (here[0], here[1], lax.rem(here[2] + offset, n_gz)),
        )
        copy.start()
        w_copies.append(copy)
    loads[14].wait()
    bundle(0, [perm_ref[...]] + [mob[1, k] for k in range(3)] + [flags_ref[...].astype(f32)])
    start_faces([functools.partial(bundle_copy, 0)])

    def order_far_first():
        return range(peers - 1, 0, -1)

    groups = list(zip(CUTS[:-1], CUTS[1:]))

    def group(order):
        return [low <= order < high for low, high in groups].index(True)

    def mobility_copy(t, low, high, to):
        return remote(
            m_s.at[t, :, low:high], m_r.at[t, :, low:high], m_ss.at[t], m_rs.at[t], to
        )

    def send_mobility(t):
        own = gather([mob.at[t, k] for k in range(3)])
        for k in range(3):
            m_s[t, k] = own[k]
        for order in order_far_first():
            mobility_copy(t, order, order + 1, peer(order)).start()

    def fault_coefficients(t):
        mobility_copy(t, 1, peers, peer(1)).wait()
        own_up = jnp.bitwise_and(jnp.right_shift(f_up[...], t), 1) == 1
        for k in range(3):
            f_coef[t, k] = f_scale[...] * jnp.where(own_up, m_s[t, k], m_r[t, k])

    send_mobility(1)

    for order in range(peers):
        lanes = slice(order * slots, (order + 1) * slots)
        row_hot[:, lanes] = (
            (lax.broadcasted_iota(jnp.int32, (rows, slots), 0) == f_row[order : order + 1])
            .astype(f32)
            .astype(jnp.bfloat16)
        )
        z_hot[lanes, :] = (
            (lax.broadcasted_iota(jnp.int32, (nz, slots), 0) == f_z[order : order + 1])
            .astype(f32)
            .T.astype(jnp.bfloat16)
        )

    def scatter(read, start, stop):
        base = start // 4 * 4
        parts = split(read(base, stop), 2)
        marked = [[], []]
        for order in range(start, stop):
            hot = row_hot[:, order * slots : (order + 1) * slots]
            at = order - base
            for pieces, part in zip(marked, parts):
                pieces.append(hot * jnp.broadcast_to(part[at : at + 1], hot.shape))
        added = lax.dot_general(
            jnp.concatenate([jnp.concatenate(pieces, axis=1) for pieces in marked], axis=0),
            z_hot[start * slots : stop * slots, :],
            (((1,), (0,)), ((), ())),
            preferred_element_type=f32,
        )
        return (added[:rows] + added[rows:]).reshape(shape)

    for load in loads[15:]:
        load.wait()
    for copy in w_copies:
        copy.wait()
    rates = w_s[...]
    for offset in range(1, n_gz):
        rates = rates + w_r[offset]

    def sources(t):
        misfit = (rates[t : t + 1, :n_wells] - obs_ref[t, 0]) / sigma_sq
        weighted = perforated * as_column(misfit)
        both = jnp.concatenate([weighted, weighted * as_column(bhp_ref[t, 0])], axis=1)
        spread = jnp.dot(
            jnp.concatenate([well_hot_t.astype(jnp.bfloat16)] * 3, axis=1),
            jnp.concatenate(split(both, 3), axis=0),
            preferred_element_type=f32,
        )
        spread = jnp.concatenate([spread[:, :nz], spread[:, nz:]], axis=0)
        drawn = pressure_ref[t] * spread[:rows].reshape(shape) - spread[rows:].reshape(shape)
        water_slope, oil_slope = mobility_slopes(sat_ref[t + 1, 0], sat_ref[t + 1, 1])
        whole = total(t)
        src[t, 0] = whole * spread[:rows].reshape(shape)
        water_source = perm_ref[...] * drawn * water_slope
        if t == 1:
            water_source = water_source + (sat_ref[2, 0] - seismic_ref[...])
        src[t, 1] = water_source
        src[t, 2] = perm_ref[...] * drawn * oil_slope
        return whole * drawn

    def face_coefficients(t, flags, mob_from):
        own_flags = flags.astype(jnp.int32)
        for dim in range(3):
            got = (bx_r, by_r, bz_r)[dim]

            def halo(part, side, q):
                return edge_of(dim, got[part, side, q])

            up_face = jnp.sqrt(
                perm_ref[...] * at_next(perm_ref[...], dim, halo(0, 1, 0))
            )
            low_face = jnp.sqrt(
                perm_ref[...] * at_last(perm_ref[...], dim, halo(0, 0, 0))
            )
            up_ok = has_next[dim].astype(f32)
            low_ok = has_last[dim].astype(f32)
            if dim == 0:
                up_face = jnp.concatenate([up_face[:-1], up_face[-1:] * up_ok], axis=0)
                low_face = jnp.concatenate([low_face[:1] * low_ok, low_face[1:]], axis=0)
            else:
                up_face = up_face * jnp.where(iotas[dim] == shape[dim] - 1, up_ok, 1.0)
                low_face = low_face * jnp.where(iotas[dim] == 0, low_ok, 1.0)
            bit = 3 * t + dim
            low_flags = at_last(flags, dim, halo(0, 0, 4)).astype(jnp.int32)
            own_up = jnp.bitwise_and(jnp.right_shift(own_flags, bit), 1) == 1
            low_up = jnp.bitwise_and(jnp.right_shift(low_flags, bit), 1) == 1
            for k in range(3):
                part, q = mob_from(k)
                m = mob[t, k]
                wp[t, dim, k] = up_face * jnp.where(
                    own_up, m, at_next(m, dim, halo(part, 1, q))
                )
                wm[t, dim, k] = low_face * jnp.where(
                    low_up, at_last(m, dim, halo(part, 0, q)), m
                )

    def face_copy(parity, dim, side):
        sent, got = ((x_s, x_r), (y_s, y_r), (z_s, z_r))[dim]
        return remote(
            sent.at[side],
            got.at[parity, side],
            h_ss.at[dim, side],
            h_rs.at[parity, dim, side],
            toward(dim, 1 - 2 * side),
        )

    def send_faces(parity, up, down):
        x_s[0] = up[0][nx - 1]
        x_s[1] = down[0][0]
        y_s[0] = up[1][:, ny - 1 :, :]
        y_s[1] = down[1][:, :1, :]
        z_s[0] = pack(up[2], nz - 1)
        z_s[1] = pack(down[2], 0)
        start_faces([functools.partial(face_copy, parity)])
        inner = at_last(up[0], 0, no_edge(0)) + at_next(down[0], 0, no_edge(0))
        for dim in (1, 2):
            inner = inner + at_last(up[dim], dim, 0.0) + at_next(down[dim], dim, 0.0)
        return inner

    def add_faces(parity, inner):
        wait_faces([functools.partial(face_copy, parity)])
        inner = jnp.concatenate(
            [
                inner[:1] + x_r[parity, 0][None],
                inner[1 : nx - 1],
                inner[nx - 1 :] + x_r[parity, 1][None],
            ],
            axis=0,
        )
        inner = inner + jnp.where(
            yi == 0, y_r[parity, 0], jnp.where(yi == ny - 1, y_r[parity, 1], 0.0)
        )
        return inner + jnp.where(
            zi == 0,
            unpack(z_r[parity, 0]),
            jnp.where(zi == nz - 1, unpack(z_r[parity, 1]), 0.0),
        )

    def fault_copy(parity, low, high, order, to):
        return remote(
            c_s.at[parity, low:high],
            c_r.at[parity, low:high],
            c_ss.at[parity],
            c_rs.at[parity, group(low)],
            to,
        )

    def send_faults(parity, ref, lead, fixed):
        for low in range(peers - 8, -8, -8):
            part = slice(low, low + 8)
            values = f_send[lead, part] * gather([ref], low, low + 8)[0]
            if fixed is not None:
                values = values + f_send[fixed, part]
            c_s[parity, part] = values
            for order in range(low + 7, max(low, 1) - 1, -1):
                fault_copy(parity, order, order + 1, order, peer(order)).start()

    def add_faults(parity, inner):
        def read(low, high):
            return c_r[parity, low:high]

        for low, high in groups:
            fault_copy(parity, low, high, low, peer(low)).wait_recv()
            inner = inner + scatter(read, low, high)
        fault_copy(parity, 1, peers, 1, peer(1)).wait_send()
        return inner

    def scalar_round(parity, t, aside):
        send_faults(parity, delta, t, None)
        now = delta[...]
        total_r[...] += now
        inner = send_faces(
            parity,
            [push[t, 0, dim] * now for dim in range(3)],
            [push[t, 1, dim] * now for dim in range(3)],
        )
        if aside is not None:
            aside()
        inner = add_faces(parity, inner)
        inner = add_faults(parity, inner)
        delta[...] = inner

    def dot3(coefficients, values):
        return sum(coefficients(k) * values(k) for k in range(3))

    def scalar_push(t):
        for dim in range(3):
            push[t, 0, dim] = dot3(lambda k: wp[t, dim, k], lambda k: inverse_ref[t, 0, k])
            push[t, 1, dim] = dot3(lambda k: wm[t, dim, k], lambda k: inverse_ref[t, 0, k])

    def scalar_faults(t):
        values = gather([inverse_ref.at[t, 0, k] for k in range(3)])
        f_send[t] = dot3(lambda k: f_coef[t, k], lambda k: values[k])

    explicit[...] = sources(1)
    total_r[...] = src[1, 0]
    for k in range(3):
        const[k] = inverse_ref[1, 1, k] * src[1, 1] + inverse_ref[1, 2, k] * src[1, 2]
        lam[1, k] = const[k] + inverse_ref[1, 0, k] * src[1, 0]
    def vector_copy(low, high, to):
        return remote(
            v_s.at[:, low:high],
            v_r.at[:, low:high],
            v_ss,
            v_rs.at[group(low)],
            to,
        )

    for low in range(peers - 8, -8, -8):
        values = gather([lam.at[1, k] for k in range(3)], low, low + 8)
        for k in range(3):
            v_s[k, low : low + 8] = values[k]
        for order in range(low + 7, max(low, 1) - 1, -1):
            vector_copy(order, order + 1, peer(order)).start()
    wait_faces([functools.partial(bundle_copy, 0)])
    flags = flags_ref[...].astype(f32)
    face_coefficients(1, flags, lambda k: (0, 1 + k))
    inner = send_faces(
        0,
        [dot3(lambda k: wp[1, dim, k], lambda k: lam[1, k]) for dim in range(3)],
        [dot3(lambda k: wm[1, dim, k], lambda k: lam[1, k]) for dim in range(3)],
    )
    bundle(1, [mob[0, k] for k in range(3)] + [pressure_ref[t] for t in range(2)])
    start_faces([functools.partial(bundle_copy, 1), map_copy])
    scalar_push(1)
    send_mobility(0)
    fault_coefficients(1)
    scalar_faults(1)
    inner = add_faces(0, inner)

    def arrived(low, high):
        return dot3(lambda k: f_coef[1, k, low:high], lambda k: v_r[k, low:high])

    for low, high in groups:
        vector_copy(low, high, peer(low)).wait_recv()
        inner = inner + scatter(arrived, low, high)
    vector_copy(1, peers, peer(1)).wait_send()
    delta[...] = inner

    def prepare_turn():
        explicit[...] += sources(0)
        wait_faces([functools.partial(bundle_copy, 1), map_copy])
        face_coefficients(0, flags_ref[...].astype(f32), lambda k: (1, k))
        porosity = porosity_ref[...]
        first = src[0, 1] + porosity * (const[0] - const[2])
        second = src[0, 2] + porosity * (const[1] - const[2])
        d_first = porosity * (inverse_ref[1, 0, 0] - inverse_ref[1, 0, 2])
        d_second = porosity * (inverse_ref[1, 0, 1] - inverse_ref[1, 0, 2])
        for k in range(3):
            turn_c[k] = (
                inverse_ref[0, 0, k] * src[0, 0]
                + inverse_ref[0, 1, k] * first
                + inverse_ref[0, 2, k] * second
            )
            turn_d[k] = inverse_ref[0, 1, k] * d_first + inverse_ref[0, 2, k] * d_second

    def prepare_sends():
        fault_coefficients(0)
        for side, w in enumerate((wp, wm)):
            for dim in range(3):
                push_turn_c[side, dim] = dot3(lambda k: w[0, dim, k], lambda k: turn_c[k])
                push_turn_d[side, dim] = dot3(lambda k: w[0, dim, k], lambda k: turn_d[k])
        values = gather([ref.at[k] for ref in (turn_c, turn_d) for k in range(3)])
        f_send[2] = dot3(lambda k: f_coef[0, k], lambda k: values[k])
        f_send[3] = dot3(lambda k: f_coef[0, k], lambda k: values[3 + k])

    n_rounds = ITERS - 1
    scalar_round(1, 1, prepare_turn)
    scalar_round(0, 1, prepare_sends)

    def more(t):
        def body(step, carry):
            scalar_round(lax.rem(step, 2), t, None)
            return carry

        return body

    lax.fori_loop(3, n_rounds, more(1), 0)

    out_late = pltpu.make_async_copy(lam.at[1], lam_hbm.at[1], out_sem.at[1])
    out_early = pltpu.make_async_copy(lam.at[0], lam_hbm.at[0], out_sem.at[0])
    parity = n_rounds % 2
    total_r[...] += delta[...]
    send_faults(parity, total_r, 3, 2)
    now = total_r[...]
    inner = send_faces(
        parity,
        [push_turn_c[0, dim] + push_turn_d[0, dim] * now for dim in range(3)],
        [push_turn_c[1, dim] + push_turn_d[1, dim] * now for dim in range(3)],
    )
    for k in range(3):
        lam[1, k] = const[k] + inverse_ref[1, 0, k] * total_r[...]
    out_late.start()
    porosity = porosity_ref[...]
    first = src[0, 1] + porosity * (lam[1, 0] - lam[1, 2])
    second = src[0, 2] + porosity * (lam[1, 1] - lam[1, 2])
    for k in range(3):
        const[k] = inverse_ref[0, 1, k] * first + inverse_ref[0, 2, k] * second
    scalar_push(0)
    scalar_faults(0)
    inner = add_faces(parity, inner)
    inner = add_faults(parity, inner)
    delta[...] = inner
    total_r[...] = src[0, 0]

    n_bx, n_by, n_bz = nx // BOX, ny // BOX, nz // BOX
    n_boxes = n_bx * n_by
    wide = n_boxes * n_bz

    def prepare_gradient():
        for dim in range(3):
            got = (bx_r, by_r, bz_r)[dim]
            flux_base[0, dim] = jnp.zeros(shape, f32)
            flux_base[1, dim] = jnp.zeros(shape, f32)
            for t in range(2):
                p_here = pressure_ref[t]
                up_p = 0.5 * (
                    p_here - at_next(p_here, dim, edge_of(dim, got[1, 1, 3 + t]))
                )
                down_p = -0.5 * (
                    at_last(p_here, dim, edge_of(dim, got[1, 0, 3 + t])) - p_here
                )
                source = (lambda k: const[k]) if t == 0 else (lambda k: lam[1, k])
                flux_base[0, dim] += up_p * dot3(lambda k: wp[t, dim, k], source)
                flux_base[1, dim] += down_p * dot3(lambda k: wm[t, dim, k], source)
                if t == 0:
                    flux_lead[0, dim] = up_p * push[0, 0, dim]
                    flux_lead[1, dim] = down_p * push[0, 1, dim]
        steps = []
        for t in range(2):
            water = sat_ref[t + 1, 0] - sat_ref[t, 0]
            oil = sat_ref[t + 1, 1] - sat_ref[t, 1]
            steps.append((water, oil, water + oil))
        por[0] = -(
            lam[1, 0] * steps[1][0]
            + lam[1, 1] * steps[1][1]
            - lam[1, 2] * steps[1][2]
            + const[0] * steps[0][0]
            + const[1] * steps[0][1]
            - const[2] * steps[0][2]
        )
        por[1] = -(
            inverse_ref[0, 0, 0] * steps[0][0]
            + inverse_ref[0, 0, 1] * steps[0][1]
            - inverse_ref[0, 0, 2] * steps[0][2]
        )
        z_lane = lax.broadcasted_iota(jnp.int32, (1, n_bz), 1)

        def own_map(bx, by):
            return map_ref[bx, by : by + 1, :]

        def other_map(dim, side, bx, by):
            return map_r[2 * dim + side, bx, by : by + 1, :]

        labels = [[], [], []]
        for bx in range(n_bx):
            for by in range(n_by):
                labels[0].append(own_map(bx, by))
                labels[1].append(
                    other_map(1, 0, bx, n_by - 1) if by == 0 else other_map(1, 1, bx, 0)
                )
                if bx == 0:
                    label = other_map(0, 0, n_bx - 1, by)
                elif bx == n_bx - 1:
                    label = other_map(0, 1, 0, by)
                else:
                    even, odd = 2 * (bx - 1), 2 * (bx - 1) + 1
                    label = jnp.zeros((1, n_bz), jnp.int32)
                    for lane, side, box in (
                        (0, 0, even),
                        (1, 0, odd),
                        (n_bz - 2, 1, odd),
                        (n_bz - 1, 1, even),
                    ):
                        edge = n_bz - 1 if side == 0 else 0
                        label = jnp.where(
                            z_lane == lane,
                            other_map(2, side, box, by)[:, edge : edge + 1],
                            label,
                        )
                labels[2].append(label)
        n_regions = devices * PARAM_REGIONS
        region = lax.broadcasted_iota(jnp.int32, (LANES, n_regions), 1).astype(f32)
        for part in range(3):
            label = jnp.concatenate(labels[part], axis=1).astype(f32)
            for first in range(0, wide, LANES):
                column = jnp.broadcast_to(label[:, first : first + LANES], (LANES, LANES)).T
                found_hot[part * wide + first : part * wide + first + LANES, :] = (
                    (region == jnp.concatenate([column] * (n_regions // LANES), axis=1))
                    .astype(f32)
                    .astype(jnp.bfloat16)
                )

    parity = (n_rounds + 1) % 2
    scalar_round(parity, 0, prepare_gradient)
    lax.fori_loop(n_rounds + 2, 2 * n_rounds, more(0), 0)

    total_r[...] += delta[...]
    now = total_r[...]
    flux = [
        [flux_base[side, dim] + flux_lead[side, dim] * now for dim in range(3)]
        for side in range(2)
    ]
    gradient = explicit[...]
    for dim in range(3):
        gradient = gradient - (
            flux[0][dim]
            + flux[1][dim]
            + at_last(flux[0][dim], dim, no_edge(dim))
            + at_next(flux[1][dim], dim, no_edge(dim))
        )

    def x_sums(field):
        return jnp.sum(field.reshape(n_bx, BOX, ny, nz), axis=1)

    y_pushed = x_sums(jnp.where(yi == 0, flux[1][1], 0.0) + jnp.where(yi == ny - 1, flux[0][1], 0.0))
    z_pushed = x_sums(jnp.where(zi == 0, flux[1][2], 0.0) + jnp.where(zi == nz - 1, flux[0][2], 0.0))
    lane = lax.broadcasted_iota(jnp.int32, (ny, nz), 1)

    def moved(tile):
        return jnp.where(
            lane == BOX,
            pltpu.roll(tile, BOX, 1),
            jnp.where(lane == nz - 1 - BOX, pltpu.roll(tile, nz - BOX, 1), 0.0),
        )

    mixed = jnp.concatenate(
        [flux[1][0][0][None]]
        + [(z_pushed[2 * n] + moved(z_pushed[2 * n + 1]))[None] for n in range(n_bx // 2)]
        + [flux[0][0][nx - 1][None]],
        axis=0,
    )
    stacked = jnp.concatenate(
        [x_sums(gradient), x_sums(por[0] + por[1] * now), -y_pushed, -mixed], axis=0
    ).reshape(4 * n_bx * ny, nz)
    z_boxes = (
        (
            lax.broadcasted_iota(jnp.int32, (nz, wide), 0) // BOX
            == lax.rem(lax.broadcasted_iota(jnp.int32, (nz, wide), 1), n_bz)
        )
        .astype(f32)
        .astype(jnp.bfloat16)
    )
    boxed = jnp.dot(
        jnp.concatenate(split(stacked, 2), axis=1),
        jnp.concatenate([z_boxes] * 2, axis=0),
        preferred_element_type=f32,
    )
    in_box = (
        lax.broadcasted_iota(jnp.int32, (n_bx * ny, wide), 1) // n_bz
        == lax.broadcasted_iota(jnp.int32, (n_bx * ny, wide), 0) // BOX
    )
    sums = [
        jnp.sum(
            jnp.where(in_box, boxed[n * n_bx * ny : (n + 1) * n_bx * ny], 0.0),
            axis=0,
            keepdims=True,
        )
        for n in range(4)
    ]
    none = jnp.zeros((1, wide), f32)
    perm_row = jnp.concatenate([sums[0], sums[2], sums[3]], axis=1)
    por_row = jnp.concatenate([sums[1], none, none], axis=1)
    parts = [
        part.astype(f32) for row in (perm_row, por_row) for part in split(row, 2)
    ]
    which = lax.broadcasted_iota(jnp.int32, (8, 3 * wide), 0)
    lines = jnp.zeros((8, 3 * wide), f32)
    for n, part in enumerate(parts):
        lines = jnp.where(which == n, part, lines)
    found = jnp.dot(
        lines.astype(jnp.bfloat16), found_hot[...], preferred_element_type=f32
    )
    together = LANES // PARAM_REGIONS
    for n in range(devices // together):
        lanes = slice(n * LANES, (n + 1) * LANES)
        r_s[n, 0:1] = found[0:1, lanes] + found[1:2, lanes]
        r_s[n, 1:2] = found[2:3, lanes] + found[3:4, lanes]
    for order in sorted(range(1, devices), key=lambda n: (-(n % peers // n_gz), -n)):
        to = (flip(here[0], order // peers),) + peer(order % peers)[1:]
        other = to[0] * peers + to[1] * n_gz + to[2]
        remote(
            r_s.at[other // together],
            r_r.at[order],
            r_ss,
            r_rs,
            to,
        ).start()
    for k in range(3):
        lam[0, k] = const[k] + inverse_ref[0, 0, k] * total_r[...]
    out_early.start()
    part = r_s[index // together]
    r_all = remote(r_r.at[1:], r_r.at[1:], r_ss, r_rs, peer(1))
    r_all.wait_recv()
    for order in range(1, devices):
        part = part + r_r[order]
    mine = jnp.full((2, PARAM_REGIONS), lax.rem(index, together), jnp.int32)
    result = jnp.zeros((2, PARAM_REGIONS), f32)
    for n in range(together):
        result = jnp.where(
            mine == n, part[:, n * PARAM_REGIONS : (n + 1) * PARAM_REGIONS], result
        )
    region_ref[...] = result
    r_all.wait_send()
    out_late.wait()
    out_early.wait()


def local(*arrays):
    (
        pressure,
        saturation,
        permeability,
        porosity,
        upwind_flags,
        diag_inverse,
        seismic_obs,
        well_x,
        well_y,
        well_top,
        well_len,
        well_bhp,
        well_obs,
        fault_cell,
        fault_count,
        fault_trans,
        fault_up,
        region_map,
    ) = arrays
    counts = tuple(lax.axis_size(axis) for axis in ("gx", "gy", "gz"))
    nx, ny, nz = permeability.shape
    peers, slots = fault_cell.shape[1:]
    devices = counts[0] * peers
    hbm = pl.BlockSpec(memory_space=pltpu.HBM)
    vmem = pl.BlockSpec(memory_space=pltpu.VMEM)
    f32 = jnp.float32
    bf16 = jnp.bfloat16
    dma = pltpu.SemaphoreType.DMA

    def field(*lead, dtype=f32):
        return pltpu.VMEM(lead + (nx, ny, nz), dtype)

    def per_fault(*lead, dtype=f32):
        return pltpu.VMEM(lead + (peers, slots), dtype)

    bundles = [(2, 2, 5, ny, nz), (2, 2, 5, nx, 1, nz), (2, 2, 5, ny, nz)]
    faces = [(2, ny, nz), (2, nx, 1, nz), (2, ny, nz)]
    scratch = [
        *[pltpu.VMEM(array.shape, array.dtype) for array in arrays],
        dma((len(arrays),)),
        dma((2,)),
        field(2, 3),
        field(2, 3, 3),
        field(2, 3, 3),
        field(2, 3),
        field(),
        field(2, 3),
        field(3),
        field(3),
        field(3),
        field(2, 2, 3),
        field(2, 3),
        field(2, 3),
        field(2, 3),
        field(2, 3),
        field(2),
        field(),
        field(),
        pltpu.VMEM((nx * ny, peers * slots), bf16),
        pltpu.VMEM((peers * slots, nz), bf16),
        pltpu.VMEM((3 * region_map.size, devices * PARAM_REGIONS), bf16),
        per_fault(dtype=jnp.int32),
        per_fault(),
        per_fault(dtype=jnp.int32),
        per_fault(),
        per_fault(2, 3),
        per_fault(4),
        *[pltpu.VMEM(s, f32) for s in bundles],
        *[pltpu.VMEM(s, f32) for s in bundles],
        dma((2, 3, 2)),
        dma((2, 3, 2)),
        pltpu.VMEM((6,) + region_map.shape, jnp.int32),
        dma((3, 2)),
        dma((3, 2)),
        per_fault(2, 3),
        per_fault(2, 3),
        dma((2,)),
        dma((2,)),
        pltpu.VMEM((8, LANES), f32),
        pltpu.VMEM((counts[2], 8, LANES), f32),
        dma((counts[2],)),
        dma((counts[2],)),
        *[pltpu.VMEM(s, f32) for s in faces],
        *[pltpu.VMEM((2,) + s, f32) for s in faces],
        dma((3, 2)),
        dma((2, 3, 2)),
        per_fault(3),
        per_fault(3),
        dma,
        dma((len(CUTS) - 1,)),
        per_fault(2),
        per_fault(2),
        dma((2,)),
        dma((2, len(CUTS) - 1)),
        pltpu.VMEM((devices * PARAM_REGIONS // LANES, 2, LANES), f32),
        pltpu.VMEM((devices, 2, LANES), f32),
        dma,
        dma,
    ]
    results = (
        jax.ShapeDtypeStruct((2, 3, nx, ny, nz), f32),
        jax.ShapeDtypeStruct((2, PARAM_REGIONS), f32),
    )
    found = pl.pallas_call(
        functools.partial(kernel, counts),
        out_shape=results,
        in_specs=[hbm] * len(arrays),
        out_specs=(hbm, vmem),
        scratch_shapes=scratch,
        compiler_params=pltpu.CompilerParams(
            collective_id=0, has_side_effects=True, vmem_limit_bytes=60 * 2**20
        ),
    )(*arrays)

    def finish(lam_ref, region_ref, lam_out, region_out, sem):
        copy = pltpu.make_async_copy(lam_ref, lam_out, sem)
        copy.start()
        region_out[...] = region_ref[...]
        copy.wait()

    return pl.pallas_call(
        finish,
        out_shape=results,
        in_specs=[vmem, vmem],
        out_specs=(hbm, vmem),
        scratch_shapes=[dma],
    )(*found)


def solution(mesh):
    cells = P("gx", "gy", "gz")
    column = P("gx", "gy", None)
    every = ("gx", "gy", "gz")
    placed = (
        P(None, "gx", "gy", "gz"),
        P(None, None, "gx", "gy", "gz"),
        cells,
        cells,
        cells,
        P(None, None, None, "gx", "gy", "gz"),
        cells,
        column,
        column,
        column,
        column,
        P(None, "gx", "gy", None),
        P(None, "gx", "gy", None),
        P(every, None, None),
        P(every, None),
        P(every, None, None),
        P(every, None, None),
        cells,
    )
    return jax.shard_map(
        local,
        mesh=mesh,
        in_specs=placed,
        out_specs=(P(None, None, "gx", "gy", "gz"), P(None, every)),
        check_vma=False,
    )
```
